32 devices in a mesh: img: 16 (over z, x, core), seq: 2 (over y).
Axes of the slice: x: 2, y: 2, z: 4, core: 2. Of those that a mesh axis runs over, the one named last changes fastest.
Arguments:
- tokens: bfloat16 [16, 640, 768], P('img', 'seq'), may hold values from -6 to 6
- masked: int32 [16, 640], P('img', 'seq'), may hold values from 0 to 1, as said below
- out_grad: bfloat16 [16, 640, 768], P('img', 'seq'), may hold values from -6 to 6
- norm1_gain: float32 [768], replicated, may hold values from 0.5 to 1.5
- norm1_bias: float32 [768], replicated, may hold values from -3 to 3
- qkv_weight: bfloat16 [768, 2304], replicated, may hold values from -0.21875 to 0.21875
- query_bias: float32 [768], replicated, may hold values from -3 to 3
- value_bias: float32 [768], replicated, may hold values from -3 to 3
- rel_table: float32 [2212, 12], replicated, may hold values from -4 to 4
- proj_weight: bfloat16 [768, 768], replicated, may hold values from -1 to 1
- proj_bias: float32 [768], replicated, may hold values from -3 to 3
- scale1: float32 [768], replicated, may hold values from 0.1 to 1.9
- norm2_gain: float32 [768], replicated, may hold values from 0.5 to 1.5
- norm2_bias: float32 [768], replicated, may hold values from -3 to 3
- fc1_weight: bfloat16 [768, 3072], replicated, may hold values from -0.21875 to 0.21875
- fc1_bias: float32 [3072], replicated, may hold values from -3 to 3
- fc2_weight: bfloat16 [3072, 768], replicated, may hold values from -0.109375 to 0.109375
- fc2_bias: float32 [768], replicated, may hold values from -3 to 3
- scale2: float32 [768], replicated, may hold values from 0.1 to 1.9
Outputs:
- result: bfloat16 [16, 640, 768], P('img', 'seq')
- tokens_grad: bfloat16 [16, 640, 768], P('img', 'seq')
- norm1_gain_grad: float32 [768], replicated
- norm1_bias_grad: float32 [768], replicated
- qkv_weight_grad: float32 [768, 2304], P('img', 'seq')
- query_bias_grad: float32 [768], replicated
- value_bias_grad: float32 [768], replicated
- rel_table_grad: float32 [2212, 12], replicated
- proj_weight_grad: float32 [768, 768], P('img', 'seq')
- proj_bias_grad: float32 [768], replicated
- scale1_grad: float32 [768], replicated
- norm2_gain_grad: float32 [768], replicated
- norm2_bias_grad: float32 [768], replicated
- fc1_weight_grad: float32 [768, 3072], P('img', 'seq')
- fc1_bias_grad: float32 [3072], replicated
- fc2_weight_grad: float32 [3072, 768], P('img', 'seq')
- fc2_bias_grad: float32 [768], replicated
- scale2_grad: float32 [768], replicated
The draws below stay inside these ranges and needn't reach their ends.
Inputs may be any that keep to these rules, and one draw needn't show every extreme that they name: masked is 0 at slot 0 and at slots past 24 * 24; each image has between 120 and 320 ones among its patches, and some image has exactly 320.
All inputs are finite; a program needn't handle non-finite values.
Results may differ from the reference program's by a relative error of at most 0.02.
Values may be sent and summed in bfloat16 or wider, within the bound.
No kernel may reach another device: no remote copies, remote signals or barrier semaphores. Data moves between devices by JAX's collectives and lax.ppermute only.
A program may use at most 320 MiB of HBM per device.

```python
import jax
import jax.numpy as jnp
from jax import lax

D = 768
H = 12
HD = 64
FF = 3072
GRID = 24
SLOTS = 640
MASK_LO = 120
MASK_HI = 320
IMAGES = 16
TABLE = 2212


def draw_masked(key, part):
    base_key = jax.random.fold_in(key, 7)
    first_key, second_key, third_key = jax.random.split(base_key, 3)
    draws = jax.random.randint(first_key, (IMAGES,), 0, 1000)
    cubed_draw = draws * draws // 1000 * draws // 1000
    counts = MASK_LO + (MASK_HI - MASK_LO) * cubed_draw // 1000
    chosen = jax.random.randint(third_key, (), 0, IMAGES)
    counts = jnp.where(jnp.arange(IMAGES) == chosen, MASK_HI, counts)
    patch_count = GRID * GRID
    scores = jax.random.randint(second_key, (IMAGES, patch_count), 0, 1 << 20) * 1024 + jnp.arange(patch_count)
    ordering = jnp.argsort(scores, axis=1)
    ranking = jnp.argsort(ordering, axis=1)
    picked = (ranking < counts[:, None]).astype(jnp.int32)
    mask_full = jnp.zeros((IMAGES, SLOTS), jnp.int32)
    return mask_full.at[:, 1:patch_count + 1].set(picked)


def with_spikes(entries, stream_key, source, target, parts, factor):
    def block_of(dim):
        return (jnp.arange(entries.shape[dim]) // (entries.shape[dim] // parts)).reshape((-1,) + (1,) * (entries.ndim - 1 - dim))

    near = jax.random.permutation(stream_key, parts)[block_of(target)]
    second = (block_of(target) + parts // 2) % parts
    return jnp.where((block_of(source) == near) | (block_of(source) == second), factor * entries, entries)


def level_of(key, dims, cuts, least, top_value):
    level = 1.0
    for position, parts in cuts:
        heights = jax.random.uniform(jax.random.fold_in(jax.random.fold_in(key, 6), position), (parts,), jnp.float32, least / len(cuts), top_value / len(cuts))
        level = level * jnp.repeat(jnp.exp(heights), dims[position] // parts).reshape((-1,) + (1,) * (len(dims) - 1 - position))
    return level


def normal_values(stream_key, dims, width, limit, cuts=(), kind=jnp.bfloat16):
    level = level_of(stream_key, dims, cuts, -0.22, 0.18) if cuts else 1.0
    entries = jax.random.normal(stream_key, dims, jnp.float32) * width * level
    return jnp.minimum(jnp.maximum(entries, -limit), limit).astype(kind)


def heavy_noise(stream_key, dims, width, most, shards, heavy, held_as=jnp.bfloat16):
    result = width * jax.random.normal(stream_key, dims, jnp.float32)
    if shards:
        result = result * level_of(stream_key, dims, shards, -0.22, 0.18)
    return jnp.clip(with_spikes(result, jax.random.fold_in(stream_key, 3), *heavy), -most, most).astype(held_as)


def setup_inputs(seed: int = 0) -> dict:
    key_of = jax.random.split(jax.random.key(seed), 20)
    tokens = heavy_noise(key_of[0], (IMAGES, SLOTS, D), 1.0, 6.0, ((0, 16), (1, 2)), (0, 2, 16, 2.0))
    masked = draw_masked(jax.random.fold_in(key_of[19], 71), 0)
    out_grad = normal_values(key_of[2], (IMAGES, SLOTS, D), 1.0, 6.0, ((0, 16), (1, 2)))
    norm1_gain = jnp.clip(1.0 + 0.1 * jax.random.normal(key_of[3], (D,), jnp.float32), 0.5, 1.5)
    norm1_bias = normal_values(key_of[4], (D,), 0.5, 3.0, (), jnp.float32)
    qkv_weight = normal_values(key_of[5], (D, 3 * D), D ** -0.5, 0.21875)
    query_bias = normal_values(key_of[6], (D,), 0.5, 3.0, (), jnp.float32)
    value_bias = normal_values(key_of[7], (D,), 0.5, 3.0, (), jnp.float32)
    rel_table = normal_values(key_of[8], (TABLE, H), 1.0, 4.0, (), jnp.float32)
    proj_weight = normal_values(key_of[9], (D, D), (D // GRID) ** -0.5, 1.0)
    proj_bias = normal_values(key_of[10], (D,), 0.5, 3.0, (), jnp.float32)
    scale1 = jnp.clip(1.0 + 0.18 * jax.random.normal(key_of[11], (D,), jnp.float32), 0.1, 1.9)
    norm2_gain = jnp.clip(1.0 + 0.1 * jax.random.normal(key_of[12], (D,), jnp.float32), 0.5, 1.5)
    norm2_bias = normal_values(key_of[13], (D,), 0.5, 3.0, (), jnp.float32)
    fc1_weight = normal_values(key_of[14], (D, FF), D ** -0.5, 0.21875)
    fc1_bias = normal_values(key_of[15], (FF,), 0.5, 3.0, (), jnp.float32)
    fc2_weight = normal_values(key_of[16], (FF, D), FF ** -0.5, 0.109375)
    fc2_bias = normal_values(key_of[17], (D,), 0.5, 3.0, (), jnp.float32)
    scale2 = jnp.clip(1.0 + 0.18 * jax.random.normal(key_of[18], (D,), jnp.float32), 0.1, 1.9)
    return dict(tokens=tokens, masked=masked, out_grad=out_grad, norm1_gain=norm1_gain, norm1_bias=norm1_bias, qkv_weight=qkv_weight, query_bias=query_bias, value_bias=value_bias, rel_table=rel_table, proj_weight=proj_weight, proj_bias=proj_bias, scale1=scale1, norm2_gain=norm2_gain, norm2_bias=norm2_bias, fc1_weight=fc1_weight, fc1_bias=fc1_bias, fc2_weight=fc2_weight, fc2_bias=fc2_bias, scale2=scale2)


EPSILON = 1e-06
NEGATIVE = -1e+30
ROOT_HALF = 0.7071067811865476

@jax.custom_vjp
def low(v):
    return lax.optimization_barrier(v.astype(jnp.bfloat16)).astype(jnp.float32)

@jax.custom_vjp
def low_back(v):
    return v

def low_keep(v):
    return (low(v), None)

def low_pass(kept, grad):
    return (grad,)

def back_keep(v):
    return (v, None)

def back_low(kept, grad):
    return (low(grad),)
low.defvjp(low_keep, low_pass)
low_back.defvjp(back_keep, back_low)

def rel_index(query_pos, key_pos):
    span_width = 2 * GRID - 1
    far_index = span_width * span_width
    last_cell = GRID * GRID - 1
    query_cell = jnp.clip(query_pos - 1, 0, last_cell)
    key_cell = jnp.clip(key_pos - 1, 0, last_cell)
    row_gap = query_cell // GRID - key_cell // GRID + GRID - 1
    col_gap = query_cell % GRID - key_cell % GRID + GRID - 1
    relative = row_gap * span_width + col_gap
    relative = jnp.where(query_pos == 0, far_index, relative)
    relative = jnp.where(key_pos == 0, far_index + 1, relative)
    relative = jnp.where((query_pos == 0) & (key_pos == 0), far_index + 2, relative)
    return relative.astype(jnp.int32)

def gelu_value(argument):
    return 0.5 * argument * (1.0 + lax.erf(argument * ROOT_HALF))

def normalize(values, gain, shift):
    center = values - lax.optimization_barrier(jnp.mean(values, axis=-1, keepdims=True))
    inverse = lax.rsqrt(lax.optimization_barrier(jnp.mean(center * center, axis=-1, keepdims=True)) + EPSILON)
    return center * inverse * gain + shift

def block_forward(inputs, params, index_table, key_valid):
    norm1_gain, norm1_bias, qkv_weight, query_bias, value_bias, rel_table, proj_weight, proj_bias, scale1, norm2_gain, norm2_bias, fc1_weight, fc1_bias, fc2_weight, fc2_bias, scale2 = params
    highest = lax.Precision.HIGHEST
    hidden1 = low(normalize(inputs, norm1_gain, norm1_bias))
    projected = jnp.dot(hidden1, qkv_weight, precision=highest)
    queries = low(low_back((projected[:, 0:D] + query_bias) * HD ** (-0.5)))
    keys_all = low(low_back(projected[:, D:2 * D]))
    values_all = low(low_back(projected[:, 2 * D:3 * D] + value_bias))
    query_heads = queries.reshape(SLOTS, H, HD)
    key_heads = keys_all.reshape(SLOTS, H, HD)
    value_heads = values_all.reshape(SLOTS, H, HD)
    bias = jnp.take(rel_table.T, index_table, axis=1)
    scores = jnp.einsum('qhd,khd->hqk', query_heads, key_heads, precision=highest) + bias
    scores = low_back(jnp.where(key_valid[None, None, :], scores, NEGATIVE))
    row_max = lax.optimization_barrier(jnp.max(scores, axis=-1, keepdims=True))
    expo = jnp.exp(scores - row_max)
    probs = low(expo / lax.optimization_barrier(jnp.sum(expo, axis=-1, keepdims=True)))
    attended = jnp.einsum('hqk,khd->qhd', probs, value_heads, precision=highest).reshape(SLOTS, D)
    attended = low(low_back(attended))
    mixed_out = low_back(jnp.dot(attended, proj_weight, precision=highest) + proj_bias)
    residual1 = inputs + scale1 * mixed_out
    hidden2 = low(normalize(residual1, norm2_gain, norm2_bias))
    pre_act = low_back(jnp.dot(hidden2, fc1_weight, precision=highest) + fc1_bias)
    activated = low(gelu_value(pre_act))
    ffn_out = low_back(jnp.dot(activated, fc2_weight, precision=highest) + fc2_bias)
    return residual1 + scale2 * ffn_out

def reference(tokens, masked, out_grad, norm1_gain, norm1_bias, qkv_weight, query_bias, value_bias, rel_table, proj_weight, proj_bias, scale1, norm2_gain, norm2_bias, fc1_weight, fc1_bias, fc2_weight, fc2_bias, scale2):
    floats = (norm1_gain.astype(jnp.float32), norm1_bias.astype(jnp.float32), qkv_weight.astype(jnp.float32), query_bias.astype(jnp.float32), value_bias.astype(jnp.float32), rel_table.astype(jnp.float32), proj_weight.astype(jnp.float32), proj_bias.astype(jnp.float32), scale1.astype(jnp.float32), norm2_gain.astype(jnp.float32), norm2_bias.astype(jnp.float32), fc1_weight.astype(jnp.float32), fc1_bias.astype(jnp.float32), fc2_weight.astype(jnp.float32), fc2_bias.astype(jnp.float32), scale2.astype(jnp.float32))
    slot_ids = jnp.arange(SLOTS, dtype=jnp.int32)
    index_table = rel_index(slot_ids[:, None], slot_ids[None, :])
    key_valid = slot_ids <= GRID * GRID

    def forward_one(inputs, params):
        return block_forward(inputs, params, index_table, key_valid)

    def one_image(grad_sums, slices):
        image_in, grad_in, mask_row = slices
        inputs = image_in.astype(jnp.float32)
        out_value, pullback = jax.vjp(forward_one, inputs, floats)
        cotangent = grad_in.astype(jnp.float32) * mask_row.astype(jnp.float32)[:, None]
        d_inputs, d_params = pullback(cotangent)
        grad_sums = jax.tree.map(jnp.add, grad_sums, d_params)
        return (grad_sums, (out_value.astype(jnp.bfloat16), d_inputs.astype(jnp.bfloat16)))
    zero_sums = jax.tree.map(jnp.zeros_like, floats)
    grad_sums, (outputs, d_tokens) = lax.scan(one_image, zero_sums, (tokens, out_grad, masked))
    return (outputs, d_tokens, grad_sums[0], grad_sums[1], grad_sums[2], grad_sums[3], grad_sums[4], grad_sums[5], grad_sums[6], grad_sums[7], grad_sums[8], grad_sums[9], grad_sums[10], grad_sums[11], grad_sums[12], grad_sums[13], grad_sums[14], grad_sums[15])
```

```python
import functools

import jax
import jax.numpy as jnp
import numpy as np
from jax import lax
from jax.experimental import pallas as pl
from jax.experimental.pallas import tpu as pltpu
from jax.sharding import PartitionSpec as P

GRID = 24


EPSILON = 1e-06
NEGATIVE = -1e30
ROOT_HALF = 0.7071067811865476
GAUSS_NORM = 0.3989422804014327


def passed_along(value, axis, steps):
    count = lax.axis_size(axis)
    pairs = [(source, (source + steps) % count) for source in range(count)]
    return lax.ppermute(value, axis, pairs)


def gap_onehot():
    span_width = 2 * GRID - 1
    grid_ids = jnp.arange(GRID, dtype=jnp.int32)
    gaps = grid_ids[:, None, None] - grid_ids[None, :, None] + GRID - 1
    return (gaps == jnp.arange(span_width, dtype=jnp.int32)[None, None, :]).astype(jnp.float32)


def bias_full(rel_table, all_slots):
    highest = lax.Precision.HIGHEST
    span_width = 2 * GRID - 1
    far_index = span_width * span_width
    cells = GRID * GRID
    head_count = rel_table.shape[1]
    spare = all_slots - 1 - cells
    selector = gap_onehot()
    patch_table = rel_table[0:far_index].reshape(span_width, span_width, head_count)
    row_pick = jnp.einsum("pqa,abh->pqbh", selector, patch_table, precision=highest)
    spread = jnp.einsum("pqbh,rsb->hprqs", row_pick, selector, precision=highest)
    patch_bias = spread.reshape(head_count, cells, cells)
    patch_bias = jnp.concatenate(
        [
            patch_bias,
            jnp.broadcast_to(patch_bias[:, cells - 1 : cells, :], (head_count, spare, cells)),
        ],
        axis=1,
    )
    patch_bias = jnp.concatenate(
        [
            patch_bias,
            jnp.broadcast_to(
                patch_bias[:, :, cells - 1 : cells], (head_count, cells + spare, spare)
            ),
        ],
        axis=2,
    )
    top_row = jnp.broadcast_to(rel_table[far_index][:, None, None], (head_count, 1, all_slots - 1))
    left_col = jnp.broadcast_to(
        rel_table[far_index + 1][:, None, None], (head_count, all_slots - 1, 1)
    )
    corner = rel_table[far_index + 2][:, None, None]
    upper = jnp.concatenate([corner, top_row], axis=2)
    lower = jnp.concatenate([left_col, patch_bias], axis=2)
    return jnp.concatenate([upper, lower], axis=1)


def table_back(grad_full):
    highest = lax.Precision.HIGHEST
    span_width = 2 * GRID - 1
    cells = GRID * GRID
    head_count = grad_full.shape[0]
    corner = grad_full[:, 0, 0]
    far_grad = jnp.sum(grad_full[:, 0, 1:], axis=1)
    near_grad = jnp.sum(grad_full[:, 1:, 0], axis=1)
    patch_grad = grad_full[:, 1:, 1:]
    patch_grad = jnp.concatenate(
        [
            patch_grad[:, 0 : cells - 1, :],
            jnp.sum(patch_grad[:, cells - 1 :, :], axis=1, keepdims=True),
        ],
        axis=1,
    )
    patch_grad = jnp.concatenate(
        [
            patch_grad[:, :, 0 : cells - 1],
            jnp.sum(patch_grad[:, :, cells - 1 :], axis=2, keepdims=True),
        ],
        axis=2,
    )
    selector = gap_onehot()
    spread = patch_grad.reshape(head_count, GRID, GRID, GRID, GRID)
    row_sums = jnp.einsum("hprqs,rsb->pqbh", spread, selector, precision=highest)
    patch_table = jnp.einsum("pqa,pqbh->abh", selector, row_sums, precision=highest)
    tail = jnp.stack([far_grad, near_grad, corner], axis=0)
    return jnp.concatenate([patch_table.reshape(span_width * span_width, head_count), tail], axis=0)


def gelu_value(argument):
    return 0.5 * argument * (1.0 + lax.erf(argument * ROOT_HALF))


def gelu_slope(argument):
    return (
        0.5 * (1.0 + lax.erf(argument * ROOT_HALF))
        + argument * jnp.exp(-0.5 * argument * argument) * GAUSS_NORM
    )


def normalize(values, gain, shift):
    center = values - jnp.mean(values, axis=-1, keepdims=True)
    inverse = lax.rsqrt(jnp.mean(center * center, axis=-1, keepdims=True) + EPSILON)
    normed = center * inverse
    return (normed * gain + shift, normed, inverse)


def normalize_back(grad_out, normed, inverse, gain):
    signal = grad_out * gain
    inner = (
        signal
        - jnp.mean(signal, axis=-1, keepdims=True)
        - normed * jnp.mean(signal * normed, axis=-1, keepdims=True)
    )
    return (inverse * inner, jnp.sum(grad_out * normed, axis=0), jnp.sum(grad_out, axis=0))


def general_body(
    tokens,
    masked,
    out_grad,
    norm1_gain,
    norm1_bias,
    qkv_weight,
    query_bias,
    value_bias,
    rel_table,
    proj_weight,
    proj_bias,
    scale1,
    norm2_gain,
    norm2_bias,
    fc1_weight,
    fc1_bias,
    fc2_weight,
    fc2_bias,
    scale2,
):
    images, local_rows, model_width = tokens.shape
    head_count = rel_table.shape[1]
    head_size = model_width // head_count
    head_scale = head_size ** (-0.5)
    cycle_size = lax.axis_size("seq")
    position = lax.axis_index("seq")
    all_slots = local_rows * cycle_size
    key_pos = jnp.arange(all_slots, dtype=jnp.int32)
    position_bias = lax.dynamic_slice_in_dim(
        bias_full(rel_table, all_slots), position * local_rows, local_rows, 1
    )
    key_valid = key_pos <= GRID * GRID
    flat_rows = images * local_rows
    head_shape = (images, local_rows, head_count, head_size)
    inputs = tokens.astype(jnp.float32).reshape(flat_rows, model_width)
    normed1, centred1, inverse1 = normalize(inputs, norm1_gain, norm1_bias)
    hidden1 = normed1.astype(jnp.bfloat16)
    projected = jnp.dot(hidden1, qkv_weight, preferred_element_type=jnp.float32)
    queries = ((projected[:, 0:model_width] + query_bias) * head_scale).astype(jnp.bfloat16)
    keys_local = (
        projected[:, model_width : 2 * model_width]
        .astype(jnp.bfloat16)
        .reshape(images, local_rows, model_width)
    )
    values_local = (
        (projected[:, 2 * model_width :] + value_bias)
        .astype(jnp.bfloat16)
        .reshape(images, local_rows, model_width)
    )
    query_heads = queries.reshape(head_shape)

    def block_scores(key_block, offset):
        key_count = key_block.shape[1]
        key_heads = key_block.reshape(images, key_count, head_count, head_size)
        logits = jnp.einsum(
            "gqhd,gkhd->ghqk", query_heads, key_heads, preferred_element_type=jnp.float32
        )
        logits = logits + lax.dynamic_slice_in_dim(position_bias, offset, key_count, 2)[None]
        usable = lax.dynamic_slice_in_dim(key_valid, offset, key_count, 0)
        return (jnp.where(usable, logits, NEGATIVE), usable)

    row_max = jnp.full((images, head_count, local_rows), NEGATIVE, jnp.float32)
    key_block = lax.all_gather(keys_local, "seq", axis=1, tiled=True)
    value_block = lax.all_gather(values_local, "seq", axis=1, tiled=True)
    key_count = key_block.shape[1]
    scores, usable = block_scores(key_block, jnp.int32(0))
    new_max = jnp.maximum(row_max, jnp.max(scores, axis=-1))
    weights = jnp.where(usable, jnp.exp(scores - new_max[..., None]), 0.0)
    totals = jnp.sum(weights, axis=-1)
    value_heads = value_block.reshape(images, key_count, head_count, head_size)
    update = jnp.einsum(
        "ghqk,gkhd->gqhd",
        weights.astype(jnp.bfloat16),
        value_heads,
        preferred_element_type=jnp.float32,
    )
    weighted = update
    row_max, totals, weighted = (new_max, totals, weighted)
    log_total = row_max + jnp.log(totals)
    attended = weighted / jnp.transpose(totals, (0, 2, 1))[..., None]
    attn_low = attended.reshape(flat_rows, model_width).astype(jnp.bfloat16)
    mixed_out = jnp.dot(attn_low, proj_weight, preferred_element_type=jnp.float32) + proj_bias
    residual1 = inputs + scale1 * mixed_out
    normed2, centred2, inverse2 = normalize(residual1, norm2_gain, norm2_bias)
    hidden2 = normed2.astype(jnp.bfloat16)
    pre_act = jnp.dot(hidden2, fc1_weight, preferred_element_type=jnp.float32) + fc1_bias
    activated = gelu_value(pre_act).astype(jnp.bfloat16)
    ffn_out = jnp.dot(activated, fc2_weight, preferred_element_type=jnp.float32) + fc2_bias
    result = (residual1 + scale2 * ffn_out).astype(jnp.bfloat16).reshape(tokens.shape)
    cotangent = (out_grad.astype(jnp.float32) * masked.astype(jnp.float32)[..., None]).reshape(
        flat_rows, model_width
    )
    d_ffn = (scale2 * cotangent).astype(jnp.bfloat16)
    scale2_grad = jnp.sum(cotangent * ffn_out, axis=0)
    fc2_bias_grad = jnp.sum(d_ffn.astype(jnp.float32), axis=0)
    fc2_weight_grad = jnp.einsum("nf,nd->fd", activated, d_ffn, preferred_element_type=jnp.float32)
    d_act = jnp.einsum("nd,fd->nf", d_ffn, fc2_weight, preferred_element_type=jnp.float32)
    d_pre = (d_act * gelu_slope(pre_act)).astype(jnp.bfloat16)
    fc1_bias_grad = jnp.sum(d_pre.astype(jnp.float32), axis=0)
    fc1_weight_grad = jnp.einsum("nd,nf->df", hidden2, d_pre, preferred_element_type=jnp.float32)
    d_hidden2 = jnp.einsum("nf,df->nd", d_pre, fc1_weight, preferred_element_type=jnp.float32)
    back_two, norm2_gain_grad, norm2_bias_grad = normalize_back(
        d_hidden2, centred2, inverse2, norm2_gain
    )
    d_resid1 = cotangent + back_two
    d_mixed = (scale1 * d_resid1).astype(jnp.bfloat16)
    scale1_grad = jnp.sum(d_resid1 * mixed_out, axis=0)
    proj_bias_grad = jnp.sum(d_mixed.astype(jnp.float32), axis=0)
    proj_weight_grad = jnp.einsum(
        "nc,nd->cd", attn_low, d_mixed, preferred_element_type=jnp.float32
    )
    d_attn = jnp.einsum(
        "nd,cd->nc", d_mixed, proj_weight, preferred_element_type=jnp.float32
    ).astype(jnp.bfloat16)
    d_attn_heads = d_attn.reshape(head_shape)
    row_delta = jnp.transpose(
        jnp.sum(d_attn_heads.astype(jnp.float32) * attended, axis=-1), (0, 2, 1)
    )

    def back_block(key_block, value_block, offset):
        key_count = key_block.shape[1]
        scores, usable = block_scores(key_block, offset)
        prob_full = jnp.where(usable, jnp.exp(scores - log_total[..., None]), 0.0)
        prob_low = prob_full.astype(jnp.bfloat16)
        key_heads = key_block.reshape(images, key_count, head_count, head_size)
        value_heads = value_block.reshape(images, key_count, head_count, head_size)
        d_value = jnp.einsum(
            "ghqk,gqhd->gkhd", prob_low, d_attn_heads, preferred_element_type=jnp.float32
        )
        d_probs = jnp.einsum(
            "gqhd,gkhd->ghqk", d_attn_heads, value_heads, preferred_element_type=jnp.float32
        )
        d_scores = (prob_full * (d_probs - row_delta[..., None])).astype(jnp.bfloat16)
        d_query = jnp.einsum(
            "ghqk,gkhd->gqhd", d_scores, key_heads, preferred_element_type=jnp.float32
        )
        d_key = jnp.einsum(
            "ghqk,gqhd->gkhd", d_scores, query_heads, preferred_element_type=jnp.float32
        )
        table_part = jnp.sum(d_scores.astype(jnp.float32), axis=0)
        return (
            d_query,
            d_key.reshape(images, key_count, model_width),
            d_value.reshape(images, key_count, model_width),
            table_part,
        )

    def turn_grads(grad_pair):
        return (
            passed_along(grad_pair[0].astype(jnp.bfloat16), "seq", 1).astype(jnp.float32),
            passed_along(grad_pair[1].astype(jnp.bfloat16), "seq", 1).astype(jnp.float32),
        )

    def cycle_step(turn_index, cycle_state):
        key_block, value_block, d_key_acc, d_value_acc, d_query_acc, table_acc = cycle_state
        owner_rank = (position - turn_index) % cycle_size
        offset = owner_rank * local_rows
        d_query, d_key, d_value, table_part = back_block(key_block, value_block, offset)
        table_acc = lax.dynamic_update_slice_in_dim(table_acc, table_part, offset, 2)
        d_key_acc, d_value_acc = turn_grads((d_key_acc + d_key, d_value_acc + d_value))
        key_block, value_block = passed_along((key_block, value_block), "seq", 1)
        return (key_block, value_block, d_key_acc, d_value_acc, d_query_acc + d_query, table_acc)

    kv_zeros = jnp.zeros((images, local_rows, model_width), jnp.float32)
    initial = (
        keys_local,
        values_local,
        kv_zeros,
        kv_zeros,
        jnp.zeros(head_shape, jnp.float32),
        jnp.zeros((head_count, local_rows, all_slots), jnp.float32),
    )
    cycle_state = lax.fori_loop(0, cycle_size - 1, cycle_step, initial)
    key_block, value_block, d_key_acc, d_value_acc, d_query_acc, table_acc = cycle_state
    offset = (position + 1) % cycle_size * local_rows
    d_query, d_key, d_value, table_part = back_block(key_block, value_block, offset)
    table_acc = lax.dynamic_update_slice_in_dim(table_acc, table_part, offset, 2)
    d_key_all, d_value_all = turn_grads((d_key_acc + d_key, d_value_acc + d_value))
    d_query_all = d_query_acc + d_query
    d_query_low = d_query_all.reshape(flat_rows, model_width).astype(jnp.bfloat16) * head_scale
    d_key_low = d_key_all.reshape(flat_rows, model_width).astype(jnp.bfloat16)
    d_value_low = d_value_all.reshape(flat_rows, model_width).astype(jnp.bfloat16)
    d_qkv = jnp.concatenate([d_query_low, d_key_low, d_value_low], axis=1)
    qkv_weight_grad = jnp.einsum("nd,ne->de", hidden1, d_qkv, preferred_element_type=jnp.float32)
    query_bias_grad = jnp.sum(d_query_low.astype(jnp.float32), axis=0)
    value_bias_grad = jnp.sum(d_value_low.astype(jnp.float32), axis=0)
    d_hidden1 = jnp.einsum("ne,de->nd", d_qkv, qkv_weight, preferred_element_type=jnp.float32)
    back_one, norm1_gain_grad, norm1_bias_grad = normalize_back(
        d_hidden1, centred1, inverse1, norm1_gain
    )
    tokens_grad = (d_resid1 + back_one).astype(jnp.bfloat16).reshape(tokens.shape)
    grad_square = lax.dynamic_update_slice_in_dim(
        jnp.zeros((head_count, all_slots, all_slots), jnp.float32),
        table_acc,
        position * local_rows,
        1,
    )
    table_grad = table_back(grad_square)
    half_summed = (
        lax.psum_scatter(
            qkv_weight_grad.astype(jnp.bfloat16), "img", scatter_dimension=0, tiled=True
        ).astype(jnp.float32),
        lax.psum_scatter(
            proj_weight_grad.astype(jnp.bfloat16), "img", scatter_dimension=0, tiled=True
        ).astype(jnp.float32),
        lax.psum_scatter(
            fc1_weight_grad.astype(jnp.bfloat16), "img", scatter_dimension=0, tiled=True
        ).astype(jnp.float32),
        lax.psum_scatter(
            fc2_weight_grad.astype(jnp.bfloat16), "img", scatter_dimension=0, tiled=True
        ).astype(jnp.float32),
    )
    summed = (
        lax.psum_scatter(
            half_summed[0].astype(jnp.bfloat16), "seq", scatter_dimension=1, tiled=True
        ).astype(jnp.float32),
        lax.psum_scatter(
            half_summed[1].astype(jnp.bfloat16), "seq", scatter_dimension=1, tiled=True
        ).astype(jnp.float32),
        lax.psum_scatter(
            half_summed[2].astype(jnp.bfloat16), "seq", scatter_dimension=1, tiled=True
        ).astype(jnp.float32),
        lax.psum_scatter(
            half_summed[3].astype(jnp.bfloat16), "seq", scatter_dimension=1, tiled=True
        ).astype(jnp.float32),
    )
    smalls = lax.psum(
        (
            table_grad,
            norm1_gain_grad,
            norm1_bias_grad,
            query_bias_grad,
            value_bias_grad,
            proj_bias_grad,
            scale1_grad,
            norm2_gain_grad,
            norm2_bias_grad,
            fc1_bias_grad,
            fc2_bias_grad,
            scale2_grad,
        ),
        ("img", "seq"),
    )
    return (
        result,
        tokens_grad,
        smalls[1],
        smalls[2],
        summed[0],
        smalls[3],
        smalls[4],
        smalls[0],
        summed[1],
        smalls[5],
        smalls[6],
        smalls[7],
        smalls[8],
        summed[2],
        smalls[9],
        summed[3],
        smalls[10],
        smalls[11],
    )


LANES = 128
STRIP = 24
STRIP_WIDTH = 1280
MEGA = 1 << 20
NT = (((1,), (1,)), ((), ()))
TN = (((0,), (0,)), ((), ()))
NN = (((1,), (0,)), ((), ()))
BF = jnp.bfloat16
F32 = jnp.float32


def mul(left, right, dims=NN):
    return lax.dot_general(left, right, dims, preferred_element_type=F32)


def bits_of(img, seq):
    ring = img >> 2
    gray = ring ^ (ring >> 1)
    return {"core": img & 1, "x": (img >> 1) & 1, "za": gray & 1, "zb": gray >> 1, "y": seq}


def label_of(img, seq, order):
    bits = bits_of(img, seq)
    total = 0
    for name in order:
        total = total * 2 + bits[name]
    return total


def swap_pairs(name):
    order = ("core", "x", "za", "zb", "y")
    where = {label_of(img, seq, order): img * 2 + seq for img in range(16) for seq in range(2)}
    flip = 1 << (len(order) - 1 - order.index(name))
    return [(device, where[label ^ flip]) for label, device in where.items()]


def swapped(value, name):
    return lax.ppermute(value, ("img", "seq"), swap_pairs(name))


def reduce_scatter(keep, send, order):
    terms = [keep, swapped(send, order[0])]
    half = keep.shape[0]
    for name in order[1:]:
        half //= 2
        out = sum(term[half : 2 * half].astype(F32) for term in terms).astype(BF)
        terms = [term[:half] for term in terms] + [swapped(out, name)]
    return sum(term[0].astype(F32) for term in terms)


def layer_norm(values):
    center = values - jnp.mean(values, axis=-1, keepdims=True)
    inverse = lax.rsqrt(jnp.mean(center * center, axis=-1, keepdims=True) + EPSILON)
    return center * inverse, inverse


def layer_norm_back(grad_out, normed, inverse, gain):
    signal = grad_out * gain
    return inverse * (
        signal
        - jnp.mean(signal, axis=-1, keepdims=True)
        - normed * jnp.mean(signal * normed, axis=-1, keepdims=True)
    )


def spec(block, index):
    return pl.BlockSpec(block, index)


def full(shape):
    zeros = (0,) * len(shape)
    return pl.BlockSpec(shape, lambda *_: zeros)


def run(kernel, place, grid, in_specs, out_specs, out_shapes, scratch, operands, flops, vmem=48):
    moved = sum(int(np.prod(o.shape)) * o.dtype.itemsize for o in (*operands, *out_shapes))
    return pl.pallas_call(
        kernel,
        grid_spec=pltpu.PrefetchScalarGridSpec(
            num_scalar_prefetch=1,
            grid=grid,
            in_specs=in_specs,
            out_specs=out_specs,
            scratch_shapes=scratch,
        ),
        out_shape=out_shapes,
        compiler_params=pltpu.CompilerParams(vmem_limit_bytes=vmem * MEGA),
        cost_estimate=pl.CostEstimate(flops=flops, bytes_accessed=moved, transcendentals=0),
    )(place, *operands)


def shape(dims, dtype):
    return jax.ShapeDtypeStruct(dims, dtype)


def qkv_kernel(place, own, other, vecs, weight, qb, vb, qkv_out, hidden_out):
    step = pl.program_id(0)
    rows = own.shape[0]

    @pl.when(step == 0)
    def _():
        for source, side in ((own, place[0]), (other, 1 - place[0])):
            normed, _ = layer_norm(source[...].astype(F32))
            low = (normed * vecs[0:1, :] + vecs[1:2, :]).astype(BF)
            hidden_out[pl.ds(pl.multiple_of(side * rows, 64), rows), :] = low

    wide = mul(hidden_out[...], weight[...])
    shift = jnp.where(step == 0, qb[...], jnp.where(step == 2, vb[...], 0.0))
    factor = jnp.where(step == 0, 0.125, 1.0)
    qkv_out[0] = ((wide + shift) * factor).astype(BF)


def window(strip, block):
    off = (STRIP - block) * STRIP
    base = off // LANES * LANES
    held = strip[:, base : base + 6 * LANES]
    if off - base:
        held = pltpu.roll(held, 6 * LANES - (off - base), axis=1)
    return held[:, : 5 * LANES]


CHUNKS = tuple((start * 144, 144) for start in range(4)) + ((576, 64),)


def attend_kernel(place, qkv, strips, even_mask, own_out, send_out, expo_out, inv_out, strip, attended):
    slots = qkv.shape[1]
    half = slots // 2
    side = place[0]
    lane = lax.broadcasted_iota(jnp.int32, (1, LANES), 1)
    first = lane < LANES // 2
    masks = (jnp.where(first, 1.0, 0.0).astype(BF), jnp.where(first, 0.0, 1.0).astype(BF))
    keys = [qkv[1] * m for m in masks]
    values = [qkv[2] * m for m in masks]
    picks = even_mask[...] > 0.5
    for head in range(2):
        rolled = [
            pltpu.roll(
                jnp.broadcast_to(strips[0, head, par : par + 1, :], (STRIP, STRIP_WIDTH)),
                1,
                axis=1,
                stride=1,
                stride_axis=0,
            )
            for par in range(2)
        ]
        strip[head] = jnp.where(picks, rolled[0], rolled[1])
    block_lane = lax.broadcasted_iota(jnp.int32, (STRIP, LANES), 1)
    block_row = lax.broadcasted_iota(jnp.int32, (STRIP, LANES), 0)
    for start, count in CHUNKS:
        query = qkv[0, start : start + count, :]
        total = None
        scale = None
        for head in range(2):
            far = strips[0, head, 0:1, 1152:1153]
            near = strips[0, head, 0:1, 1153:1154]
            corner = strips[0, head, 0:1, 1154:1155]
            biases = []
            for block in range(start // STRIP, -(-(start + count) // STRIP)):
                if start == 576:
                    row = window(strip.at[head, 0:8, :], STRIP)[0:1, :]
                    piece = jnp.broadcast_to(row, (count, 5 * LANES))
                    ids = lax.broadcasted_iota(jnp.int32, (count, LANES), 1)
                else:
                    piece = window(strip.at[head], block)
                    ids = block_lane
                left = jnp.where(ids == 0, near, piece[:, :LANES])
                if block == 0:
                    piece = jnp.concatenate(
                        [
                            jnp.where(
                                block_row == 0, jnp.where(ids == 0, corner, far), left
                            )
                        ]
                        + [
                            jnp.where(block_row == 0, far, piece[:, n * LANES : (n + 1) * LANES])
                            for n in range(1, 4)
                        ]
                        + [
                            jnp.where(
                                ids > 64, NEGATIVE, jnp.where(block_row == 0, far, piece[:, 4 * LANES :])
                            )
                        ],
                        axis=1,
                    )
                else:
                    piece = jnp.concatenate(
                        [
                            left,
                            piece[:, LANES : 4 * LANES],
                            jnp.where(ids > 64, NEGATIVE, piece[:, 4 * LANES :]),
                        ],
                        axis=1,
                    )
                biases.append(piece)
                if start == 576:
                    break
            scores = mul(query, keys[head], NT) + jnp.concatenate(biases, axis=0)
            top = jnp.max(scores, axis=1, keepdims=True)
            expo = jnp.exp(scores - top)
            inverse = 1.0 / jnp.sum(expo, axis=1, keepdims=True)
            low = expo.astype(BF)
            expo_out[head, start : start + count, :] = low
            part = mul(low, values[head]) * inverse
            total = part if head == 0 else total + part
            spread = jnp.broadcast_to(inverse, (count, LANES))
            scale = spread if head == 0 else jnp.where(first, scale, spread)
        attended[start : start + count, :] = total
        inv_out[start : start + count, :] = scale
    own_out[...] = attended[pl.ds(pl.multiple_of(side * half, 64), half), :].astype(BF)
    send_out[...] = attended[pl.ds(pl.multiple_of((1 - side) * half, 64), half), :].astype(BF)


def attend_back_kernel(
    place, qkv, expo, attn_own, attn_send, grad_own, grad_other, inv, even_mask,
    dqkv_out, strip_out, grad_all, attn_all, d_scores, strip, dq_all,
):
    slots = qkv.shape[1]
    half = slots // 2
    here = pl.ds(pl.multiple_of(place[0] * half, 64), half)
    there = pl.ds(pl.multiple_of((1 - place[0]) * half, 64), half)
    lane = lax.broadcasted_iota(jnp.int32, (1, LANES), 1)
    first = lane < LANES // 2
    masks = (jnp.where(first, 1.0, 0.0).astype(BF), jnp.where(first, 0.0, 1.0).astype(BF))
    scaled = grad_own[...].astype(F32) * inv[here, :]
    grad_all[here, :] = scaled
    attn_all[here, :] = scaled * attn_own[...].astype(F32)
    scaled = grad_other[...].astype(F32) * inv[there, :]
    grad_all[there, :] = scaled
    attn_all[there, :] = scaled * attn_send[...].astype(F32)
    keys = [qkv[1] * m for m in masks]
    values = [qkv[2] * m for m in masks]
    block_lane = lax.broadcasted_iota(jnp.int32, (STRIP, LANES), 1)
    block_row = lax.broadcasted_iota(jnp.int32, (STRIP, LANES), 0)
    strip[...] = jnp.zeros_like(strip)
    columns = [jnp.zeros((8, LANES), F32) for _ in range(2)]
    tops = [None, None]
    zeros = jnp.zeros((STRIP, LANES), F32)
    for start, count in CHUNKS:
        grads = grad_all[start : start + count, :].astype(BF)
        products = attn_all[start : start + count, :]
        total = None
        for head in range(2):
            chosen = first if head == 0 else jnp.logical_not(first)
            delta = jnp.sum(jnp.where(chosen, products, 0.0), axis=1, keepdims=True)
            d_probs = mul(grads, values[head], NT)
            d_score = expo[head, start : start + count, :].astype(F32) * (d_probs - delta)
            low = d_score.astype(BF)
            d_scores[head, start : start + count, :] = low
            part = mul(low, keys[head])
            total = part if head == 0 else total + part
            if start == 576:
                for tile in range(count // 8):
                    columns[head] = columns[head] + d_score[8 * tile : 8 * tile + 8, :LANES]
                line = jnp.sum(d_score, axis=0, keepdims=True)
                line = jnp.concatenate([jnp.where(lane == 0, 0.0, line[:, :LANES]), line[:, LANES:]], axis=1)
                strip[head, 0:1, : 5 * LANES] = strip[head, 0:1, : 5 * LANES] + line
            else:
                for block in range(start // STRIP, (start + count) // STRIP):
                    at = block * STRIP - start
                    piece = d_score[at : at + STRIP, :]
                    left = piece[:, :LANES]
                    rest = piece[:, LANES:]
                    if block == 0:
                        tops[head] = piece[0:1, :]
                        left = jnp.where(block_row == 0, 0.0, left)
                        rest = jnp.concatenate(
                            [
                                jnp.where(block_row == 0, 0.0, rest[:, n * LANES : (n + 1) * LANES])
                                for n in range(4)
                            ],
                            axis=1,
                        )
                    columns[head] = columns[head] + left[0:8] + left[8:16] + left[16:24]
                    piece = jnp.concatenate(
                        [jnp.where(block_lane == 0, 0.0, left), rest, zeros], axis=1
                    )
                    off = (STRIP - block) * STRIP
                    base = off // LANES * LANES
                    if off - base:
                        piece = pltpu.roll(piece, off - base, axis=1)
                    strip[head, :, base : base + 6 * LANES] = (
                        strip[head, :, base : base + 6 * LANES] + piece
                    )
        dq_all[start : start + count, :] = total
    dqkv_out[0] = dq_all[...].astype(BF) * BF(0.125)
    d_key = None
    d_value = None
    low_grads = grad_all[...].astype(BF)
    for head in range(2):
        part = mul(d_scores[head], qkv[0] * masks[head], TN)
        d_key = part if head == 0 else d_key + part
        part = mul(expo[head], low_grads * masks[head], TN)
        d_value = part if head == 0 else d_value + part
    dqkv_out[1] = d_key.astype(BF)
    dqkv_out[2] = d_value.astype(BF)
    picks = even_mask[...] > 0.5
    row_id = lax.broadcasted_iota(jnp.int32, (STRIP, STRIP_WIDTH), 0)
    wide_lane = lax.broadcasted_iota(jnp.int32, (1, STRIP_WIDTH), 1)
    for head in range(2):
        held = strip[head]
        lines = []
        for par in range(2):
            part = jnp.where(picks, held, 0.0) if par == 0 else jnp.where(picks, 0.0, held)
            part = pltpu.roll(part, STRIP_WIDTH - 1, axis=1)
            for bit in (1, 2, 4, 8, 16):
                part = jnp.where(
                    (row_id & bit) > 0, pltpu.roll(part, STRIP_WIDTH - bit, axis=1), part
                )
            lines.append(jnp.sum(part, axis=0, keepdims=True))
        near = jnp.sum(jnp.where(lane == 0, columns[head], 0.0)).reshape(1, 1)
        corner = tops[head][:, 0:1]
        far = jnp.sum(tops[head], axis=1, keepdims=True) - corner
        line = lines[0]
        line = jnp.where(wide_lane >= 1152, 0.0, line)
        line = jnp.where(wide_lane == 1152, far, line)
        line = jnp.where(wide_lane == 1153, near, line)
        line = jnp.where(wide_lane == 1154, corner, line)
        strip_out[0, head, 0:1, :] = line
        strip_out[0, head, 1:2, :] = lines[1]


def ffn_kernel(
    place, tokens, cot, attn_own, attn_other, vecs, proj, fc1, fc1_bias, fc2, proj_own, proj_other,
    act_out, d_pre_out, fc1_bias_out, hidden_out, resid_out, d_ffn_out, attn_out, d_mixed_out, d_resid_out,
    grad_own_out, grad_send_out, small_out, mixed_held, d_hidden,
):
    step = pl.program_id(0)
    width = attn_own.shape[1]

    @pl.when(step == 0)
    def _():
        attn_out[:, pl.ds(pl.multiple_of(place[0] * width, LANES), width)] = attn_own[...]
        attn_out[:, pl.ds(pl.multiple_of((1 - place[0]) * width, LANES), width)] = attn_other[...]
        mixed = mul(attn_out[...], proj[...]) + vecs[2:3, :]
        mixed_held[...] = mixed
        resid = tokens[...].astype(F32) + vecs[3:4, :] * mixed
        resid_out[...] = resid
        normed, _ = layer_norm(resid)
        hidden_out[...] = (normed * vecs[4:5, :] + vecs[5:6, :]).astype(BF)
        d_ffn = (vecs[7:8, :] * cot[...].astype(F32)).astype(BF)
        d_ffn_out[...] = d_ffn
        d_hidden[...] = jnp.zeros_like(d_hidden)

    pre = mul(hidden_out[...], fc1[...]) + fc1_bias[...]
    gate = 0.5 * (1.0 + lax.erf(pre * ROOT_HALF))
    act_out[...] = (pre * gate).astype(BF)
    slope = gate + pre * jnp.exp(-0.5 * pre * pre) * GAUSS_NORM
    d_pre = (mul(d_ffn_out[...], fc2[...], NT) * slope).astype(BF)
    d_pre_out[...] = d_pre
    fc1_bias_out[...] = jnp.sum(d_pre.astype(F32), axis=0, keepdims=True)
    d_hidden[...] += mul(d_pre, fc1[...], NT)

    @pl.when(step == pl.num_programs(0) - 1)
    def _():
        grad = d_hidden[...]
        mixed = mixed_held[...]
        normed, inverse = layer_norm(resid_out[...])
        d_resid = cot[...].astype(F32) + layer_norm_back(grad, normed, inverse, vecs[4:5, :])
        d_resid_out[...] = d_resid
        d_mixed = (vecs[3:4, :] * d_resid).astype(BF)
        d_mixed_out[...] = d_mixed
        small_out[0:1, :] = jnp.sum(grad * normed, axis=0, keepdims=True)
        small_out[1:2, :] = jnp.sum(grad, axis=0, keepdims=True)
        small_out[2:3, :] = jnp.sum(d_resid * mixed, axis=0, keepdims=True)
        small_out[3:4, :] = jnp.sum(d_mixed.astype(F32), axis=0, keepdims=True)
        small_out[4:5, :] = jnp.sum(d_ffn_out[...].astype(F32), axis=0, keepdims=True)
        small_out[5:8, :] = jnp.zeros((3, small_out.shape[1]), F32)
        grad_own_out[...] = mul(d_mixed, proj_own[...], NT).astype(BF)
        grad_send_out[...] = mul(d_mixed, proj_other[...], NT).astype(BF)


def fc2_grad_kernel(place, act, d_ffn, keep_out, send_out, held, *, y_shift, rest):
    step = pl.program_id(0)
    held[...] = mul(act[...], d_ffn[...], TN)
    core = place[1]
    for pair in range(2):
        for seq in range(2):
            at = rest(pair, step, seq) ^ place[2]
            columns = slice(384 * seq, 384 * seq + 384)
            low = pl.multiple_of(384 * pair + 192 * core, 64)
            high = pl.multiple_of(384 * pair + 192 * (1 - core), 64)
            keep_out[at] = held[pl.ds(low, 192), columns].astype(BF)
            send_out[at] = held[pl.ds(high, 192), columns].astype(BF)


def fc1_grad_kernel(place, hidden, d_pre, attn, d_mixed, keep_out, send_out, held, *, rest):
    step = pl.program_id(0)
    core = place[1]
    held[...] = mul(hidden[...], d_pre[...], TN)
    seq = step // 2
    lanes = pl.ds(pl.multiple_of((step % 2) * 768, LANES), 768)
    for pair in range(8):
        at = rest(pair % 2, pair // 2, seq) ^ place[3]
        low = pl.multiple_of(96 * pair + 48 * core, 16)
        high = pl.multiple_of(96 * pair + 48 * (1 - core), 16)
        keep_out[at, :, lanes] = held[pl.ds(low, 48), :].astype(BF)
        send_out[at, :, lanes] = held[pl.ds(high, 48), :].astype(BF)

    @pl.when(step == pl.num_programs(0) - 1)
    def _():
        held[...] = mul(attn[...], d_mixed[...], TN)
        for pair in range(8):
            low = pl.multiple_of(96 * pair + 48 * core, 16)
            high = pl.multiple_of(96 * pair + 48 * (1 - core), 16)
            for side in range(2):
                at = rest(pair % 2, pair // 2, side) ^ place[3]
                columns = slice(384 * side, 384 * side + 384)
                keep_out[at, :, 1536:1920] = held[pl.ds(low, 48), columns].astype(BF)
                send_out[at, :, 1536:1920] = held[pl.ds(high, 48), columns].astype(BF)


def result_kernel(place, act, fc2, resid, cot, vecs, result_out, small_out, total):
    step = pl.program_id(0)

    @pl.when(step == 0)
    def _():
        total[...] = jnp.zeros_like(total)

    total[...] += mul(act[...], fc2[...])

    @pl.when(step == pl.num_programs(0) - 1)
    def _():
        ffn = total[...] + vecs[6:7, :]
        result_out[...] = (resid[...] + vecs[7:8, :] * ffn).astype(BF)
        small_out[0:1, :] = jnp.sum(cot[...].astype(F32) * ffn, axis=0, keepdims=True)
        small_out[1:8, :] = jnp.zeros((7, small_out.shape[1]), F32)


def hidden1_grad_kernel(place, dqkv, weight, own, other, keep_out, send_out, small_out, total):
    step = pl.program_id(0)
    rows = own.shape[0]
    here = pl.ds(pl.multiple_of(place[0] * rows, 64), rows)
    there = pl.ds(pl.multiple_of((1 - place[0]) * rows, 64), rows)

    @pl.when(step == 0)
    def _():
        total[...] = jnp.zeros_like(total)
        small_out[...] = jnp.zeros_like(small_out)

    grads = dqkv[0]
    total[...] += mul(grads, weight[...], NT)
    line = jnp.sum(grads.astype(F32), axis=0, keepdims=True)

    @pl.when(step == 0)
    def _():
        small_out[2:3, :384] = line

    @pl.when(step == 2)
    def _():
        small_out[2:3, 384:] = line
        mine = total[here, :]
        theirs = total[there, :]
        keep_out[...] = mine
        send_out[...] = theirs.astype(BF)
        normed_mine, _ = layer_norm(own[...].astype(F32))
        normed_theirs, _ = layer_norm(other[...].astype(F32))
        small_out[0:1, :] = jnp.sum(mine * normed_mine, axis=0, keepdims=True) + jnp.sum(
            theirs * normed_theirs, axis=0, keepdims=True
        )
        small_out[1:2, :] = jnp.sum(mine, axis=0, keepdims=True) + jnp.sum(
            theirs, axis=0, keepdims=True
        )


def qkv_grad_kernel(place, hidden, dqkv, keep_out, send_out, held, *, rest):
    step = pl.program_id(0)
    core = place[1]
    held[...] = mul(hidden[...], dqkv[0], TN)
    lanes = pl.ds(pl.multiple_of(step * 384, LANES), 384)
    for pair in range(8):
        at = rest(pair % 2, pair // 2, 0) ^ place[4]
        low = pl.multiple_of(96 * pair + 48 * core, 16)
        high = pl.multiple_of(96 * pair + 48 * (1 - core), 16)
        keep_out[at, :, lanes] = held[pl.ds(low, 48), :].astype(BF)
        send_out[at, :, lanes] = held[pl.ds(high, 48), :].astype(BF)


def tokens_grad_kernel(place, keep, recv, own, d_resid, vecs, grad_out):
    grad = keep[...] + recv[...].astype(F32)
    normed, inverse = layer_norm(own[...].astype(F32))
    back = layer_norm_back(grad, normed, inverse, vecs[0:1, :])
    grad_out[...] = (d_resid[...] + back).astype(BF)


def rest_label(order):
    def rest(x_bit, ring, seq):
        gray = ring ^ (ring >> 1)
        bits = {"x": x_bit, "za": gray & 1, "zb": gray >> 1, "y": seq}
        total = 0
        for name in order[1:]:
            total = total * 2 + bits[name]
        return total

    return rest


ORDER_A = ("core", "x", "y", "za", "zb")
ORDER_B = ("core", "za", "zb", "x", "y")
ORDER_Q = ("core", "x", "za", "zb")


def strips_of(table, seq, heads):
    own = lax.dynamic_slice_in_dim(table, seq * heads, heads, 1).T
    span = 2 * GRID - 1
    cells = span * span
    patch = own[:, :cells][:, ::-1].reshape(heads, span, span)
    patch = jnp.pad(patch, ((0, 0), (0, 1), (0, 1))).reshape(heads, 24, 2, 48)
    even = jnp.concatenate(
        [patch[:, :, 0].reshape(heads, 1152), own[:, cells:], jnp.zeros((heads, 125), F32)], axis=1
    )
    odd = jnp.pad(patch[:, :, 1].reshape(heads, 1152), ((0, 0), (24, 104)))
    return jnp.stack([even, odd], axis=1).reshape(heads // 2, 2, 2, STRIP_WIDTH)


def table_of(strips):
    heads = strips.shape[0]
    span = 2 * GRID - 1
    even = strips[:, 0, :1152].reshape(heads, 24, 1, 48)
    odd = strips[:, 1, 24:1176].reshape(heads, 24, 1, 48)
    patch = jnp.concatenate([even, odd], axis=2).reshape(heads, 48, 48)[:, :span, :span]
    flat = patch.reshape(heads, span * span)[:, ::-1]
    return jnp.concatenate([flat, strips[:, 0, 1152:1155]], axis=1)


def even_places():
    lane = np.arange(STRIP_WIDTH)[None, :]
    row = np.arange(STRIP)[:, None]
    turn = (lane - 1) // STRIP
    return np.where(row == 0, turn % 2 == 0, turn % 2 == 1).astype(np.float32)


def split_body(
    tokens,
    masked,
    out_grad,
    norm1_gain,
    norm1_bias,
    qkv_weight,
    query_bias,
    value_bias,
    rel_table,
    proj_weight,
    proj_bias,
    scale1,
    norm2_gain,
    norm2_bias,
    fc1_weight,
    fc1_bias,
    fc2_weight,
    fc2_bias,
    scale2,
):
    _, rows, width = tokens.shape
    slots = 2 * rows
    heads = rel_table.shape[1] // 2
    pairs = heads // 2
    share = width // 2
    hidden = fc1_weight.shape[1]
    seq = lax.axis_index("seq")
    img = lax.axis_index("img")
    core = img & 1
    ring = img >> 2
    x_bit = (img >> 1) & 1
    place = jnp.stack(
        [
            seq,
            core,
            rest_label(ORDER_A)(x_bit, ring, seq),
            rest_label(ORDER_B)(x_bit, ring, seq),
            rest_label(ORDER_Q)(x_bit, ring, seq),
        ]
    ).astype(jnp.int32)
    own = tokens.reshape(rows, width)
    other = swapped(own, "y")
    cot = (out_grad.astype(F32) * masked.astype(F32)[..., None]).astype(BF).reshape(rows, width)
    vecs = jnp.stack(
        [norm1_gain, norm1_bias, proj_bias, scale1, norm2_gain, norm2_bias, fc2_bias, scale2]
    )
    strips = strips_of(rel_table, seq, heads)
    even_mask = jnp.asarray(even_places())

    qkv, hidden1 = run(
        qkv_kernel, place, (3,),
        [
            full((rows, width)), full((rows, width)), full((8, width)),
            spec((width, share), lambda t, p: (0, 2 * t + p[0])),
            spec((1, share), lambda t, p: (0, p[0])), spec((1, share), lambda t, p: (0, p[0])),
        ],
        [spec((1, slots, share), lambda t, p: (t, 0, 0)), full((slots, width))],
        [shape((3, slots, share), BF), shape((slots, width), BF)],
        [],
        (own, other, vecs, qkv_weight, query_bias.reshape(1, width), value_bias.reshape(1, width)),
        2 * slots * width * 3 * share,
    )
    pair_rows = spec((slots, LANES), lambda n, p: (0, n))
    pair_half = spec((rows, LANES), lambda n, p: (0, n))
    pair_qkv = spec((3, slots, LANES), lambda n, p: (0, 0, n))
    pair_expo = spec((2, slots, slots), lambda n, p: (n, 0, 0))
    pair_strip = spec((1, 2, 2, STRIP_WIDTH), lambda n, p: (n, 0, 0, 0))
    attn_own, attn_send, expo, inv = run(
        attend_kernel, place, (pairs,),
        [pair_qkv, pair_strip, full((STRIP, STRIP_WIDTH))],
        [pair_half, pair_half, pair_expo, pair_rows],
        [
            shape((rows, share), BF), shape((rows, share), BF),
            shape((heads, slots, slots), BF), shape((slots, share), F32),
        ],
        [pltpu.VMEM((2, STRIP, STRIP_WIDTH), F32), pltpu.VMEM((slots, LANES), F32)],
        (qkv, strips, even_mask),
        16 * slots * slots * 64 * heads,
    )
    attn_other = swapped(attn_send, "y")
    parts = 4
    part = hidden // parts
    whole = full((rows, width))
    sliced = spec((rows, part), lambda c, p: (0, c))
    (
        act, d_pre, fc1_bias_part, hidden2, resid, d_ffn, attn_low, d_mixed, d_resid,
        grad_own, grad_send, small_ffn,
    ) = run(
        ffn_kernel, place, (parts,),
        [
            whole, whole, full((rows, share)), full((rows, share)), full((8, width)),
            full((width, width)), spec((width, part), lambda c, p: (0, c)),
            spec((1, part), lambda c, p: (0, c)), spec((part, width), lambda c, p: (c, 0)),
            spec((share, width), lambda c, p: (p[0], 0)), spec((share, width), lambda c, p: (1 - p[0], 0)),
        ],
        [
            sliced, sliced, spec((1, part), lambda c, p: (0, c)), whole, whole, whole, whole, whole, whole,
            full((rows, share)), full((rows, share)), full((8, width)),
        ],
        [
            shape((rows, hidden), BF), shape((rows, hidden), BF), shape((1, hidden), F32),
            shape((rows, width), BF), shape((rows, width), F32), shape((rows, width), BF),
            shape((rows, width), BF), shape((rows, width), BF), shape((rows, width), F32),
            shape((rows, share), BF), shape((rows, share), BF), shape((8, width), F32),
        ],
        [pltpu.VMEM((rows, width), F32), pltpu.VMEM((rows, width), F32)],
        (
            own, cot, attn_own, attn_other, vecs, proj_weight, fc1_weight, fc1_bias.reshape(1, hidden),
            fc2_weight, proj_weight, proj_weight,
        ),
        2 * rows * width * (3 * hidden + 2 * width),
    )
    grad_other = swapped(grad_send, "y")
    block = (16, 192, share)
    keep_a, send_a = run(
        functools.partial(fc2_grad_kernel, y_shift=0, rest=rest_label(ORDER_A)), place, (parts,),
        [sliced, whole], [full(block), full(block)], [shape(block, BF), shape(block, BF)],
        [pltpu.VMEM((part, width), F32)], (act, d_ffn), 2 * rows * width * hidden,
    )
    block = (16, 48, 5 * share)
    keep_b, send_b = run(
        functools.partial(fc1_grad_kernel, rest=rest_label(ORDER_B)), place, (parts,),
        [whole, sliced, whole, whole], [full(block), full(block)],
        [shape(block, BF), shape(block, BF)],
        [pltpu.VMEM((width, part), F32)], (hidden2, d_pre, attn_low, d_mixed),
        2 * rows * width * (hidden + width),
    )
    result, small_result = run(
        result_kernel, place, (parts,),
        [sliced, spec((part, width), lambda c, p: (c, 0)), whole, whole, full((8, width))],
        [whole, full((8, width))],
        [shape((rows, width), BF), shape((8, width), F32)],
        [pltpu.VMEM((rows, width), F32)], (act, fc2_weight, resid, cot, vecs),
        2 * rows * width * hidden,
    )
    dqkv, strip_grad = run(
        attend_back_kernel, place, (pairs,),
        [
            pair_qkv, pair_expo, pair_half, pair_half, pair_half, pair_half, pair_rows,
            full((STRIP, STRIP_WIDTH)),
        ],
        [pair_qkv, pair_strip],
        [shape((3, slots, share), BF), shape((pairs, 2, 2, STRIP_WIDTH), F32)],
        [
            pltpu.VMEM((slots, LANES), F32), pltpu.VMEM((slots, LANES), F32),
            pltpu.VMEM((2, slots, slots), BF), pltpu.VMEM((2, STRIP, STRIP_WIDTH), F32),
            pltpu.VMEM((slots, LANES), F32),
        ],
        (qkv, expo, attn_own, attn_send, grad_own, grad_other, inv, even_mask),
        32 * slots * slots * 64 * heads,
    )
    third = spec((1, slots, share), lambda t, p: (t, 0, 0))
    dh_keep, dh_send, small_last = run(
        hidden1_grad_kernel, place, (3,),
        [third, spec((width, share), lambda t, p: (0, 2 * t + p[0])), whole, whole],
        [whole, whole, full((8, width))],
        [shape((rows, width), F32), shape((rows, width), BF), shape((8, width), F32)],
        [pltpu.VMEM((slots, width), F32)], (dqkv, qkv_weight, own, other),
        2 * slots * width * 3 * share,
    )
    dh_recv = swapped(dh_send, "y")
    block = (8, 48, 3 * share)
    keep_q, send_q = run(
        functools.partial(qkv_grad_kernel, rest=rest_label(ORDER_Q)), place, (3,),
        [full((slots, width)), third], [full(block), full(block)],
        [shape(block, BF), shape(block, BF)],
        [pltpu.VMEM((width, share), F32)], (hidden1, dqkv), 2 * slots * width * 3 * share,
    )
    tokens_grad = run(
        tokens_grad_kernel, place, (1,),
        [whole, whole, whole, whole, full((8, width))], [whole],
        [shape((rows, width), BF)], [], (dh_keep, dh_recv, own, d_resid, vecs), 0,
    )[0]

    fc2_grad = reduce_scatter(keep_a, send_a, ORDER_A)
    fc1_proj = reduce_scatter(keep_b, send_b, ORDER_B)
    qkv_part = reduce_scatter(keep_q, send_q, ORDER_Q)
    fc1_grad = fc1_proj[:, : 4 * share]
    proj_grad = fc1_proj[:, 4 * share :]
    on_left = seq == 0
    given = jnp.where(on_left, qkv_part[:, 2 * share :], qkv_part[:, :share]).astype(BF)
    taken = swapped(given, "y").astype(F32)
    qkv_grad = jnp.where(
        on_left,
        jnp.concatenate([qkv_part[:, :share], taken, qkv_part[:, share : 2 * share]], axis=1),
        jnp.concatenate([qkv_part[:, share : 2 * share], taken, qkv_part[:, 2 * share :]], axis=1),
    )

    both = jnp.concatenate(
        [small_ffn[:5], small_result[:1], fc1_bias_part.reshape(4, width), small_last[:2]], axis=0
    )
    single = jnp.concatenate([strip_grad.reshape(-1, LANES), small_last[2].reshape(-1, LANES)], axis=0)
    cut = both.size // LANES
    packed = jnp.concatenate([both.reshape(-1, LANES), single], axis=0)
    for name in ("core", "x", "za", "zb"):
        packed = packed + swapped(packed, name)
    mate = swapped(packed, "y")
    both = (packed[:cut] + mate[:cut]).reshape(-1, width)
    ends = [jnp.where(on_left, packed[cut:], mate[cut:]), jnp.where(on_left, mate[cut:], packed[cut:])]
    count = strip_grad.size // LANES
    table_grad = jnp.concatenate(
        [table_of(end[:count].reshape(heads, 2, STRIP_WIDTH)) for end in ends], axis=0
    ).T
    tail = [end[count:].reshape(2, share) for end in ends]
    query_bias_grad = jnp.concatenate([tail[0][0], tail[1][0]])
    value_bias_grad = jnp.concatenate([tail[0][1], tail[1][1]])
    return (
        result.reshape(tokens.shape),
        tokens_grad.reshape(tokens.shape),
        both[10],
        both[11],
        qkv_grad,
        query_bias_grad,
        value_bias_grad,
        table_grad,
        proj_grad,
        both[3],
        both[2],
        both[0],
        both[1],
        fc1_grad,
        both[6:10].reshape(hidden),
        fc2_grad,
        both[4],
        both[5],
    )


def solution(mesh):
    in_specs = (
        P("img", "seq", None),
        P("img", "seq"),
        P("img", "seq", None),
        P(),
        P(),
        P(),
        P(),
        P(),
        P(),
        P(),
        P(),
        P(),
        P(),
        P(),
        P(),
        P(),
        P(),
        P(),
        P(),
    )
    out_specs = (
        P("img", "seq", None),
        P("img", "seq", None),
        P(),
        P(),
        P("img", "seq"),
        P(),
        P(),
        P(),
        P("img", "seq"),
        P(),
        P(),
        P(),
        P(),
        P("img", "seq"),
        P(),
        P("img", "seq"),
        P(),
        P(),
    )
    sizes = dict(mesh.shape)
    body = split_body if (sizes["img"], sizes["seq"]) == (16, 2) else general_body
    return jax.shard_map(body, mesh=mesh, in_specs=in_specs, out_specs=out_specs, check_vma=False)
```

```python
import functools

import jax
import jax.numpy as jnp
import numpy as np
from jax import lax
from jax.experimental import pallas as pl
from jax.experimental.pallas import tpu as pltpu
from jax.sharding import PartitionSpec as P

GRID = 24


EPSILON = 1e-06
NEGATIVE = -1e30
ROOT_HALF = 0.7071067811865476
GAUSS_NORM = 0.3989422804014327


def passed_along(value, axis, steps):
    count = lax.axis_size(axis)
    pairs = [(source, (source + steps) % count) for source in range(count)]
    return lax.ppermute(value, axis, pairs)


def gap_onehot():
    span_width = 2 * GRID - 1
    grid_ids = jnp.arange(GRID, dtype=jnp.int32)
    gaps = grid_ids[:, None, None] - grid_ids[None, :, None] + GRID - 1
    return (gaps == jnp.arange(span_width, dtype=jnp.int32)[None, None, :]).astype(jnp.float32)


def bias_full(rel_table, all_slots):
    highest = lax.Precision.HIGHEST
    span_width = 2 * GRID - 1
    far_index = span_width * span_width
    cells = GRID * GRID
    head_count = rel_table.shape[1]
    spare = all_slots - 1 - cells
    selector = gap_onehot()
    patch_table = rel_table[0:far_index].reshape(span_width, span_width, head_count)
    row_pick = jnp.einsum("pqa,abh->pqbh", selector, patch_table, precision=highest)
    spread = jnp.einsum("pqbh,rsb->hprqs", row_pick, selector, precision=highest)
    patch_bias = spread.reshape(head_count, cells, cells)
    patch_bias = jnp.concatenate(
        [
            patch_bias,
            jnp.broadcast_to(patch_bias[:, cells - 1 : cells, :], (head_count, spare, cells)),
        ],
        axis=1,
    )
    patch_bias = jnp.concatenate(
        [
            patch_bias,
            jnp.broadcast_to(
                patch_bias[:, :, cells - 1 : cells], (head_count, cells + spare, spare)
            ),
        ],
        axis=2,
    )
    top_row = jnp.broadcast_to(rel_table[far_index][:, None, None], (head_count, 1, all_slots - 1))
    left_col = jnp.broadcast_to(
        rel_table[far_index + 1][:, None, None], (head_count, all_slots - 1, 1)
    )
    corner = rel_table[far_index + 2][:, None, None]
    upper = jnp.concatenate([corner, top_row], axis=2)
    lower = jnp.concatenate([left_col, patch_bias], axis=2)
    return jnp.concatenate([upper, lower], axis=1)


def table_back(grad_full):
    highest = lax.Precision.HIGHEST
    span_width = 2 * GRID - 1
    cells = GRID * GRID
    head_count = grad_full.shape[0]
    corner = grad_full[:, 0, 0]
    far_grad = jnp.sum(grad_full[:, 0, 1:], axis=1)
    near_grad = jnp.sum(grad_full[:, 1:, 0], axis=1)
    patch_grad = grad_full[:, 1:, 1:]
    patch_grad = jnp.concatenate(
        [
            patch_grad[:, 0 : cells - 1, :],
            jnp.sum(patch_grad[:, cells - 1 :, :], axis=1, keepdims=True),
        ],
        axis=1,
    )
    patch_grad = jnp.concatenate(
        [
            patch_grad[:, :, 0 : cells - 1],
            jnp.sum(patch_grad[:, :, cells - 1 :], axis=2, keepdims=True),
        ],
        axis=2,
    )
    selector = gap_onehot()
    spread = patch_grad.reshape(head_count, GRID, GRID, GRID, GRID)
    row_sums = jnp.einsum("hprqs,rsb->pqbh", spread, selector, precision=highest)
    patch_table = jnp.einsum("pqa,pqbh->abh", selector, row_sums, precision=highest)
    tail = jnp.stack([far_grad, near_grad, corner], axis=0)
    return jnp.concatenate([patch_table.reshape(span_width * span_width, head_count), tail], axis=0)


def gelu_value(argument):
    return 0.5 * argument * (1.0 + lax.erf(argument * ROOT_HALF))


def gelu_slope(argument):
    return (
        0.5 * (1.0 + lax.erf(argument * ROOT_HALF))
        + argument * jnp.exp(-0.5 * argument * argument) * GAUSS_NORM
    )


def normalize(values, gain, shift):
    center = values - jnp.mean(values, axis=-1, keepdims=True)
    inverse = lax.rsqrt(jnp.mean(center * center, axis=-1, keepdims=True) + EPSILON)
    normed = center * inverse
    return (normed * gain + shift, normed, inverse)


def normalize_back(grad_out, normed, inverse, gain):
    signal = grad_out * gain
    inner = (
        signal
        - jnp.mean(signal, axis=-1, keepdims=True)
        - normed * jnp.mean(signal * normed, axis=-1, keepdims=True)
    )
    return (inverse * inner, jnp.sum(grad_out * normed, axis=0), jnp.sum(grad_out, axis=0))


def general_body(
    tokens,
    masked,
    out_grad,
    norm1_gain,
    norm1_bias,
    qkv_weight,
    query_bias,
    value_bias,
    rel_table,
    proj_weight,
    proj_bias,
    scale1,
    norm2_gain,
    norm2_bias,
    fc1_weight,
    fc1_bias,
    fc2_weight,
    fc2_bias,
    scale2,
):
    images, local_rows, model_width = tokens.shape
    head_count = rel_table.shape[1]
    head_size = model_width // head_count
    head_scale = head_size ** (-0.5)
    cycle_size = lax.axis_size("seq")
    position = lax.axis_index("seq")
    all_slots = local_rows * cycle_size
    key_pos = jnp.arange(all_slots, dtype=jnp.int32)
    position_bias = lax.dynamic_slice_in_dim(
        bias_full(rel_table, all_slots), position * local_rows, local_rows, 1
    )
    key_valid = key_pos <= GRID * GRID
    flat_rows = images * local_rows
    head_shape = (images, local_rows, head_count, head_size)
    inputs = tokens.astype(jnp.float32).reshape(flat_rows, model_width)
    normed1, centred1, inverse1 = normalize(inputs, norm1_gain, norm1_bias)
    hidden1 = normed1.astype(jnp.bfloat16)
    projected = jnp.dot(hidden1, qkv_weight, preferred_element_type=jnp.float32)
    queries = ((projected[:, 0:model_width] + query_bias) * head_scale).astype(jnp.bfloat16)
    keys_local = (
        projected[:, model_width : 2 * model_width]
        .astype(jnp.bfloat16)
        .reshape(images, local_rows, model_width)
    )
    values_local = (
        (projected[:, 2 * model_width :] + value_bias)
        .astype(jnp.bfloat16)
        .reshape(images, local_rows, model_width)
    )
    query_heads = queries.reshape(head_shape)

    def block_scores(key_block, offset):
        key_count = key_block.shape[1]
        key_heads = key_block.reshape(images, key_count, head_count, head_size)
        logits = jnp.einsum(
            "gqhd,gkhd->ghqk", query_heads, key_heads, preferred_element_type=jnp.float32
        )
        logits = logits + lax.dynamic_slice_in_dim(position_bias, offset, key_count, 2)[None]
        usable = lax.dynamic_slice_in_dim(key_valid, offset, key_count, 0)
        return (jnp.where(usable, logits, NEGATIVE), usable)

    row_max = jnp.full((images, head_count, local_rows), NEGATIVE, jnp.float32)
    key_block = lax.all_gather(keys_local, "seq", axis=1, tiled=True)
    value_block = lax.all_gather(values_local, "seq", axis=1, tiled=True)
    key_count = key_block.shape[1]
    scores, usable = block_scores(key_block, jnp.int32(0))
    new_max = jnp.maximum(row_max, jnp.max(scores, axis=-1))
    weights = jnp.where(usable, jnp.exp(scores - new_max[..., None]), 0.0)
    totals = jnp.sum(weights, axis=-1)
    value_heads = value_block.reshape(images, key_count, head_count, head_size)
    update = jnp.einsum(
        "ghqk,gkhd->gqhd",
        weights.astype(jnp.bfloat16),
        value_heads,
        preferred_element_type=jnp.float32,
    )
    weighted = update
    row_max, totals, weighted = (new_max, totals, weighted)
    log_total = row_max + jnp.log(totals)
    attended = weighted / jnp.transpose(totals, (0, 2, 1))[..., None]
    attn_low = attended.reshape(flat_rows, model_width).astype(jnp.bfloat16)
    mixed_out = jnp.dot(attn_low, proj_weight, preferred_element_type=jnp.float32) + proj_bias
    residual1 = inputs + scale1 * mixed_out
    normed2, centred2, inverse2 = normalize(residual1, norm2_gain, norm2_bias)
    hidden2 = normed2.astype(jnp.bfloat16)
    pre_act = jnp.dot(hidden2, fc1_weight, preferred_element_type=jnp.float32) + fc1_bias
    activated = gelu_value(pre_act).astype(jnp.bfloat16)
    ffn_out = jnp.dot(activated, fc2_weight, preferred_element_type=jnp.float32) + fc2_bias
    result = (residual1 + scale2 * ffn_out).astype(jnp.bfloat16).reshape(tokens.shape)
    cotangent = (out_grad.astype(jnp.float32) * masked.astype(jnp.float32)[..., None]).reshape(
        flat_rows, model_width
    )
    d_ffn = (scale2 * cotangent).astype(jnp.bfloat16)
    scale2_grad = jnp.sum(cotangent * ffn_out, axis=0)
    fc2_bias_grad = jnp.sum(d_ffn.astype(jnp.float32), axis=0)
    fc2_weight_grad = jnp.einsum("nf,nd->fd", activated, d_ffn, preferred_element_type=jnp.float32)
    d_act = jnp.einsum("nd,fd->nf", d_ffn, fc2_weight, preferred_element_type=jnp.float32)
    d_pre = (d_act * gelu_slope(pre_act)).astype(jnp.bfloat16)
    fc1_bias_grad = jnp.sum(d_pre.astype(jnp.float32), axis=0)
    fc1_weight_grad = jnp.einsum("nd,nf->df", hidden2, d_pre, preferred_element_type=jnp.float32)
    d_hidden2 = jnp.einsum("nf,df->nd", d_pre, fc1_weight, preferred_element_type=jnp.float32)
    back_two, norm2_gain_grad, norm2_bias_grad = normalize_back(
        d_hidden2, centred2, inverse2, norm2_gain
    )
    d_resid1 = cotangent + back_two
    d_mixed = (scale1 * d_resid1).astype(jnp.bfloat16)
    scale1_grad = jnp.sum(d_resid1 * mixed_out, axis=0)
    proj_bias_grad = jnp.sum(d_mixed.astype(jnp.float32), axis=0)
    proj_weight_grad = jnp.einsum(
        "nc,nd->cd", attn_low, d_mixed, preferred_element_type=jnp.float32
    )
    d_attn = jnp.einsum(
        "nd,cd->nc", d_mixed, proj_weight, preferred_element_type=jnp.float32
    ).astype(jnp.bfloat16)
    d_attn_heads = d_attn.reshape(head_shape)
    row_delta = jnp.transpose(
        jnp.sum(d_attn_heads.astype(jnp.float32) * attended, axis=-1), (0, 2, 1)
    )

    def back_block(key_block, value_block, offset):
        key_count = key_block.shape[1]
        scores, usable = block_scores(key_block, offset)
        prob_full = jnp.where(usable, jnp.exp(scores - log_total[..., None]), 0.0)
        prob_low = prob_full.astype(jnp.bfloat16)
        key_heads = key_block.reshape(images, key_count, head_count, head_size)
        value_heads = value_block.reshape(images, key_count, head_count, head_size)
        d_value = jnp.einsum(
            "ghqk,gqhd->gkhd", prob_low, d_attn_heads, preferred_element_type=jnp.float32
        )
        d_probs = jnp.einsum(
            "gqhd,gkhd->ghqk", d_attn_heads, value_heads, preferred_element_type=jnp.float32
        )
        d_scores = (prob_full * (d_probs - row_delta[..., None])).astype(jnp.bfloat16)
        d_query = jnp.einsum(
            "ghqk,gkhd->gqhd", d_scores, key_heads, preferred_element_type=jnp.float32
        )
        d_key = jnp.einsum(
            "ghqk,gqhd->gkhd", d_scores, query_heads, preferred_element_type=jnp.float32
        )
        table_part = jnp.sum(d_scores.astype(jnp.float32), axis=0)
        return (
            d_query,
            d_key.reshape(images, key_count, model_width),
            d_value.reshape(images, key_count, model_width),
            table_part,
        )

    def turn_grads(grad_pair):
        return (
            passed_along(grad_pair[0].astype(jnp.bfloat16), "seq", 1).astype(jnp.float32),
            passed_along(grad_pair[1].astype(jnp.bfloat16), "seq", 1).astype(jnp.float32),
        )

    def cycle_step(turn_index, cycle_state):
        key_block, value_block, d_key_acc, d_value_acc, d_query_acc, table_acc = cycle_state
        owner_rank = (position - turn_index) % cycle_size
        offset = owner_rank * local_rows
        d_query, d_key, d_value, table_part = back_block(key_block, value_block, offset)
        table_acc = lax.dynamic_update_slice_in_dim(table_acc, table_part, offset, 2)
        d_key_acc, d_value_acc = turn_grads((d_key_acc + d_key, d_value_acc + d_value))
        key_block, value_block = passed_along((key_block, value_block), "seq", 1)
        return (key_block, value_block, d_key_acc, d_value_acc, d_query_acc + d_query, table_acc)

    kv_zeros = jnp.zeros((images, local_rows, model_width), jnp.float32)
    initial = (
        keys_local,
        values_local,
        kv_zeros,
        kv_zeros,
        jnp.zeros(head_shape, jnp.float32),
        jnp.zeros((head_count, local_rows, all_slots), jnp.float32),
    )
    cycle_state = lax.fori_loop(0, cycle_size - 1, cycle_step, initial)
    key_block, value_block, d_key_acc, d_value_acc, d_query_acc, table_acc = cycle_state
    offset = (position + 1) % cycle_size * local_rows
    d_query, d_key, d_value, table_part = back_block(key_block, value_block, offset)
    table_acc = lax.dynamic_update_slice_in_dim(table_acc, table_part, offset, 2)
    d_key_all, d_value_all = turn_grads((d_key_acc + d_key, d_value_acc + d_value))
    d_query_all = d_query_acc + d_query
    d_query_low = d_query_all.reshape(flat_rows, model_width).astype(jnp.bfloat16) * head_scale
    d_key_low = d_key_all.reshape(flat_rows, model_width).astype(jnp.bfloat16)
    d_value_low = d_value_all.reshape(flat_rows, model_width).astype(jnp.bfloat16)
    d_qkv = jnp.concatenate([d_query_low, d_key_low, d_value_low], axis=1)
    qkv_weight_grad = jnp.einsum("nd,ne->de", hidden1, d_qkv, preferred_element_type=jnp.float32)
    query_bias_grad = jnp.sum(d_query_low.astype(jnp.float32), axis=0)
    value_bias_grad = jnp.sum(d_value_low.astype(jnp.float32), axis=0)
    d_hidden1 = jnp.einsum("ne,de->nd", d_qkv, qkv_weight, preferred_element_type=jnp.float32)
    back_one, norm1_gain_grad, norm1_bias_grad = normalize_back(
        d_hidden1, centred1, inverse1, norm1_gain
    )
    tokens_grad = (d_resid1 + back_one).astype(jnp.bfloat16).reshape(tokens.shape)
    grad_square = lax.dynamic_update_slice_in_dim(
        jnp.zeros((head_count, all_slots, all_slots), jnp.float32),
        table_acc,
        position * local_rows,
        1,
    )
    table_grad = table_back(grad_square)
    half_summed = (
        lax.psum_scatter(
            qkv_weight_grad.astype(jnp.bfloat16), "img", scatter_dimension=0, tiled=True
        ).astype(jnp.float32),
        lax.psum_scatter(
            proj_weight_grad.astype(jnp.bfloat16), "img", scatter_dimension=0, tiled=True
        ).astype(jnp.float32),
        lax.psum_scatter(
            fc1_weight_grad.astype(jnp.bfloat16), "img", scatter_dimension=0, tiled=True
        ).astype(jnp.float32),
        lax.psum_scatter(
            fc2_weight_grad.astype(jnp.bfloat16), "img", scatter_dimension=0, tiled=True
        ).astype(jnp.float32),
    )
    summed = (
        lax.psum_scatter(
            half_summed[0].astype(jnp.bfloat16), "seq", scatter_dimension=1, tiled=True
        ).astype(jnp.float32),
        lax.psum_scatter(
            half_summed[1].astype(jnp.bfloat16), "seq", scatter_dimension=1, tiled=True
        ).astype(jnp.float32),
        lax.psum_scatter(
            half_summed[2].astype(jnp.bfloat16), "seq", scatter_dimension=1, tiled=True
        ).astype(jnp.float32),
        lax.psum_scatter(
            half_summed[3].astype(jnp.bfloat16), "seq", scatter_dimension=1, tiled=True
        ).astype(jnp.float32),
    )
    smalls = lax.psum(
        (
            table_grad,
            norm1_gain_grad,
            norm1_bias_grad,
            query_bias_grad,
            value_bias_grad,
            proj_bias_grad,
            scale1_grad,
            norm2_gain_grad,
            norm2_bias_grad,
            fc1_bias_grad,
            fc2_bias_grad,
            scale2_grad,
        ),
        ("img", "seq"),
    )
    return (
        result,
        tokens_grad,
        smalls[1],
        smalls[2],
        summed[0],
        smalls[3],
        smalls[4],
        smalls[0],
        summed[1],
        smalls[5],
        smalls[6],
        smalls[7],
        smalls[8],
        summed[2],
        smalls[9],
        summed[3],
        smalls[10],
        smalls[11],
    )


LANES = 128
STRIP = 24
STRIP_WIDTH = 1280
MEGA = 1 << 20
NT = (((1,), (1,)), ((), ()))
TN = (((0,), (0,)), ((), ()))
NN = (((1,), (0,)), ((), ()))
BF = jnp.bfloat16
F32 = jnp.float32


def mul(left, right, dims=NN):
    return lax.dot_general(left, right, dims, preferred_element_type=F32)


def bits_of(img, seq):
    line = img >> 2
    return {"core": img & 1, "x": (img >> 1) & 1, "z1": line & 1, "z2": line >> 1, "y": seq}


def label_of(img, seq, order):
    bits = bits_of(img, seq)
    total = 0
    for name in order:
        total = total * 2 + bits[name]
    return total


def swap_pairs(*names):
    order = ("core", "x", "z1", "z2", "y")
    where = {label_of(img, seq, order): img * 2 + seq for img in range(16) for seq in range(2)}
    flip = sum(1 << (len(order) - 1 - order.index(name)) for name in names)
    return [(device, where[label ^ flip]) for label, device in where.items()]


def swapped(value, *names):
    return lax.ppermute(value, ("img", "seq"), swap_pairs(*names))


def half_in(terms, out, name):
    size = terms[0].shape[0] // 2
    return [term[:size] for term in terms] + [swapped(out, name)]


def added(terms):
    return sum(term[0].astype(F32) for term in terms)


def layer_norm(values):
    center = values - jnp.mean(values, axis=-1, keepdims=True)
    inverse = lax.rsqrt(jnp.mean(center * center, axis=-1, keepdims=True) + EPSILON)
    return center * inverse, inverse


def layer_norm_back(grad_out, normed, inverse, gain):
    signal = grad_out * gain
    return inverse * (
        signal
        - jnp.mean(signal, axis=-1, keepdims=True)
        - normed * jnp.mean(signal * normed, axis=-1, keepdims=True)
    )


def spec(block, index):
    return pl.BlockSpec(block, index)


def full(shape):
    zeros = (0,) * len(shape)
    return pl.BlockSpec(shape, lambda *_: zeros)


def run(kernel, place, grid, in_specs, out_specs, out_shapes, scratch, operands, flops, vmem=32, after=()):
    held = len(operands)
    inner = kernel

    def kernel(place_ref, *refs):
        inner(place_ref, *refs[:held], *refs[held + len(after) :])

    in_specs = [*in_specs, *[pl.BlockSpec(memory_space=pl.ANY)] * len(after)]
    return pl.pallas_call(
        kernel,
        grid_spec=pltpu.PrefetchScalarGridSpec(
            num_scalar_prefetch=1,
            grid=grid,
            in_specs=in_specs,
            out_specs=out_specs,
            scratch_shapes=scratch,
        ),
        out_shape=out_shapes,
        compiler_params=pltpu.CompilerParams(vmem_limit_bytes=vmem * MEGA),
        cost_estimate=pl.CostEstimate(flops=1, bytes_accessed=1, transcendentals=0),
    )(place, *operands, *after)


def add_kernel(place, *refs):
    refs[-1][...] = sum(ref[...].astype(F32) for ref in refs[:-1]).astype(BF)


def half_out(place, terms, after=()):
    size = terms[0].shape[0] // 2
    block = (min(size, 4), *terms[0].shape[1:])
    count = size // block[0]
    return run(
        add_kernel, place, (count,), [spec(block, lambda n, p: (n + count, 0, 0))] * len(terms),
        [spec(block, lambda n, p: (n, 0, 0))], [shape((size, *block[1:]), BF)], [], tuple(terms), 0,
        after=after,
    )[0]


def sum_kernel(place, left, right, out):
    out[...] = left[...] + right[...]


def summed(place, left, right, after=()):
    return run(
        sum_kernel, place, (1,), [full(left.shape)] * 2, [full(left.shape)],
        [shape(left.shape, F32)], [], (left, right), 0, after=after,
    )[0]


def shape(dims, dtype):
    return jax.ShapeDtypeStruct(dims, dtype)


def qkv_kernel(place, own, other, vecs, weight, qb, vb, qkv_out, hidden_out):
    step = pl.program_id(0)
    rows = own.shape[0]

    @pl.when(step == 0)
    def _():
        for source, side in ((own, place[0]), (other, 1 - place[0])):
            normed, _ = layer_norm(source[...].astype(F32))
            low = (normed * vecs[0:1, :] + vecs[1:2, :]).astype(BF)
            hidden_out[pl.ds(pl.multiple_of(side * rows, 64), rows), :] = low

    wide = mul(hidden_out[...], weight[...])
    shift = jnp.where(step == 0, qb[...], jnp.where(step == 2, vb[...], 0.0))
    factor = jnp.where(step == 0, 0.125, 1.0)
    qkv_out[0] = ((wide + shift) * factor).astype(BF)


def window(strip, block):
    off = (STRIP - block) * STRIP
    base = off // LANES * LANES
    held = strip[:, base : base + 6 * LANES]
    if off - base:
        held = pltpu.roll(held, 6 * LANES - (off - base), axis=1)
    return held[:, : 5 * LANES]


CHUNKS = tuple((start * 144, 144) for start in range(4)) + ((576, 64),)


def attend_kernel(place, qkv, strips, even_mask, own_out, send_out, expo_out, inv_out, strip, attended):
    slots = qkv.shape[1]
    half = slots // 2
    side = place[0]
    lane = lax.broadcasted_iota(jnp.int32, (1, LANES), 1)
    first = lane < LANES // 2
    masks = (jnp.where(first, 1.0, 0.0).astype(BF), jnp.where(first, 0.0, 1.0).astype(BF))
    keys = [qkv[1] * m for m in masks]
    values = [qkv[2] * m for m in masks]
    picks = even_mask[...] > 0.5
    at = side * 6 + 2 * pl.program_id(0)
    for head in range(2):
        rolled = [
            pltpu.roll(
                jnp.broadcast_to(strips[at + head, par : par + 1, :], (STRIP, STRIP_WIDTH)),
                1,
                axis=1,
                stride=1,
                stride_axis=0,
            )
            for par in range(2)
        ]
        strip[head] = jnp.where(picks, rolled[0], rolled[1])
    block_lane = lax.broadcasted_iota(jnp.int32, (STRIP, LANES), 1)
    block_row = lax.broadcasted_iota(jnp.int32, (STRIP, LANES), 0)
    for start, count in CHUNKS:
        query = qkv[0, start : start + count, :]
        total = None
        scale = None
        for head in range(2):
            lone = strips[at + head, 0:1, 1152:1280]
            far = lone[:, 0:1]
            near = lone[:, 1:2]
            corner = lone[:, 2:3]
            biases = []
            for block in range(start // STRIP, -(-(start + count) // STRIP)):
                if start == 576:
                    row = window(strip.at[head, 0:8, :], STRIP)[0:1, :]
                    piece = jnp.broadcast_to(row, (count, 5 * LANES))
                    ids = lax.broadcasted_iota(jnp.int32, (count, LANES), 1)
                else:
                    piece = window(strip.at[head], block)
                    ids = block_lane
                left = jnp.where(ids == 0, near, piece[:, :LANES])
                if block == 0:
                    piece = jnp.concatenate(
                        [
                            jnp.where(
                                block_row == 0, jnp.where(ids == 0, corner, far), left
                            )
                        ]
                        + [
                            jnp.where(block_row == 0, far, piece[:, n * LANES : (n + 1) * LANES])
                            for n in range(1, 4)
                        ]
                        + [
                            jnp.where(
                                ids > 64, NEGATIVE, jnp.where(block_row == 0, far, piece[:, 4 * LANES :])
                            )
                        ],
                        axis=1,
                    )
                else:
                    piece = jnp.concatenate(
                        [
                            left,
                            piece[:, LANES : 4 * LANES],
                            jnp.where(ids > 64, NEGATIVE, piece[:, 4 * LANES :]),
                        ],
                        axis=1,
                    )
                biases.append(piece)
                if start == 576:
                    break
            scores = mul(query, keys[head], NT) + jnp.concatenate(biases, axis=0)
            top = jnp.max(scores, axis=1, keepdims=True)
            expo = jnp.exp(scores - top)
            inverse = 1.0 / jnp.sum(expo, axis=1, keepdims=True)
            low = expo.astype(BF)
            expo_out[head, start : start + count, :] = low
            part = mul(low, values[head]) * inverse
            total = part if head == 0 else total + part
            spread = jnp.broadcast_to(inverse, (count, LANES))
            scale = spread if head == 0 else jnp.where(first, scale, spread)
        attended[start : start + count, :] = total
        inv_out[start : start + count, :] = scale
    own_out[...] = attended[pl.ds(pl.multiple_of(side * half, 64), half), :].astype(BF)
    send_out[...] = attended[pl.ds(pl.multiple_of((1 - side) * half, 64), half), :].astype(BF)


def attend_back_kernel(
    place, qkv, expo, attn_own, attn_send, grad_own, grad_other, inv, even_mask,
    dqkv_out, strip_out, grad_all, attn_all, d_scores, strip, dq_all,
):
    slots = qkv.shape[1]
    half = slots // 2
    here = pl.ds(pl.multiple_of(place[0] * half, 64), half)
    there = pl.ds(pl.multiple_of((1 - place[0]) * half, 64), half)
    lane = lax.broadcasted_iota(jnp.int32, (1, LANES), 1)
    first = lane < LANES // 2
    masks = (jnp.where(first, 1.0, 0.0).astype(BF), jnp.where(first, 0.0, 1.0).astype(BF))
    scaled = grad_own[...].astype(F32) * inv[here, :]
    grad_all[here, :] = scaled
    attn_all[here, :] = scaled * attn_own[...].astype(F32)
    scaled = grad_other[...].astype(F32) * inv[there, :]
    grad_all[there, :] = scaled
    attn_all[there, :] = scaled * attn_send[...].astype(F32)
    keys = [qkv[1] * m for m in masks]
    values = [qkv[2] * m for m in masks]
    block_lane = lax.broadcasted_iota(jnp.int32, (STRIP, LANES), 1)
    block_row = lax.broadcasted_iota(jnp.int32, (STRIP, LANES), 0)
    strip[...] = jnp.zeros_like(strip)
    columns = [jnp.zeros((8, LANES), F32) for _ in range(2)]
    tops = [None, None]
    zeros = jnp.zeros((STRIP, LANES), F32)
    for start, count in CHUNKS:
        grads = grad_all[start : start + count, :].astype(BF)
        products = attn_all[start : start + count, :]
        total = None
        for head in range(2):
            chosen = first if head == 0 else jnp.logical_not(first)
            delta = jnp.sum(jnp.where(chosen, products, 0.0), axis=1, keepdims=True)
            d_probs = mul(grads, values[head], NT)
            d_score = expo[head, start : start + count, :].astype(F32) * (d_probs - delta)
            low = d_score.astype(BF)
            d_scores[head, start : start + count, :] = low
            part = mul(low, keys[head])
            total = part if head == 0 else total + part
            if start == 576:
                for tile in range(count // 8):
                    columns[head] = columns[head] + d_score[8 * tile : 8 * tile + 8, :LANES]
                line = jnp.sum(d_score, axis=0, keepdims=True)
                line = jnp.concatenate([jnp.where(lane == 0, 0.0, line[:, :LANES]), line[:, LANES:]], axis=1)
                strip[head, 0:1, : 5 * LANES] = strip[head, 0:1, : 5 * LANES] + line
            else:
                for block in range(start // STRIP, (start + count) // STRIP):
                    at = block * STRIP - start
                    piece = d_score[at : at + STRIP, :]
                    left = piece[:, :LANES]
                    rest = piece[:, LANES:]
                    if block == 0:
                        tops[head] = piece[0:1, :]
                        left = jnp.where(block_row == 0, 0.0, left)
                        rest = jnp.concatenate(
                            [
                                jnp.where(block_row == 0, 0.0, rest[:, n * LANES : (n + 1) * LANES])
                                for n in range(4)
                            ],
                            axis=1,
                        )
                    columns[head] = columns[head] + left[0:8] + left[8:16] + left[16:24]
                    piece = jnp.concatenate(
                        [jnp.where(block_lane == 0, 0.0, left), rest, zeros], axis=1
                    )
                    off = (STRIP - block) * STRIP
                    base = off // LANES * LANES
                    if off - base:
                        piece = pltpu.roll(piece, off - base, axis=1)
                    strip[head, :, base : base + 6 * LANES] = (
                        strip[head, :, base : base + 6 * LANES] + piece
                    )
        dq_all[start : start + count, :] = total
    dqkv_out[0] = dq_all[...].astype(BF) * BF(0.125)
    d_key = None
    d_value = None
    low_grads = grad_all[...].astype(BF)
    for head in range(2):
        part = mul(d_scores[head], qkv[0] * masks[head], TN)
        d_key = part if head == 0 else d_key + part
        part = mul(expo[head], low_grads * masks[head], TN)
        d_value = part if head == 0 else d_value + part
    dqkv_out[1] = d_key.astype(BF)
    dqkv_out[2] = d_value.astype(BF)
    picks = even_mask[...] > 0.5
    row_id = lax.broadcasted_iota(jnp.int32, (STRIP, STRIP_WIDTH), 0)
    wide_lane = lax.broadcasted_iota(jnp.int32, (1, STRIP_WIDTH), 1)
    for head in range(2):
        held = strip[head]
        lines = []
        for par in range(2):
            part = jnp.where(picks, held, 0.0) if par == 0 else jnp.where(picks, 0.0, held)
            part = pltpu.roll(part, STRIP_WIDTH - 1, axis=1)
            for bit in (1, 2, 4, 8, 16):
                part = jnp.where(
                    (row_id & bit) > 0, pltpu.roll(part, STRIP_WIDTH - bit, axis=1), part
                )
            lines.append(jnp.sum(part, axis=0, keepdims=True))
        near = jnp.sum(jnp.where(lane == 0, columns[head], 0.0)).reshape(1, 1)
        corner = tops[head][:, 0:1]
        far = jnp.sum(tops[head], axis=1, keepdims=True) - corner
        line = lines[0]
        line = jnp.where(wide_lane >= 1152, 0.0, line)
        line = jnp.where(wide_lane == 1152, far, line)
        line = jnp.where(wide_lane == 1153, near, line)
        line = jnp.where(wide_lane == 1154, corner, line)
        strip_out[0, head, 0:1, :] = line
        strip_out[0, head, 1:2, :] = lines[1]


def ffn_kernel(
    place, tokens, cot, attn_own, attn_other, vecs, proj, fc1, fc1_bias, fc2, proj_own, proj_other,
    act_out, d_pre_out, fc1_bias_out, hidden_out, resid_out, d_ffn_out, attn_out, d_mixed_out, d_resid_out,
    grad_own_out, grad_send_out, small_out, mixed_held, d_hidden,
):
    step = pl.program_id(0)
    width = attn_own.shape[1]

    @pl.when(step == 0)
    def _():
        attn_out[:, pl.ds(pl.multiple_of(place[0] * width, LANES), width)] = attn_own[...]
        attn_out[:, pl.ds(pl.multiple_of((1 - place[0]) * width, LANES), width)] = attn_other[...]
        mixed = mul(attn_out[...], proj[...]) + vecs[2:3, :]
        mixed_held[...] = mixed
        resid = tokens[...].astype(F32) + vecs[3:4, :] * mixed
        resid_out[...] = resid
        normed, _ = layer_norm(resid)
        hidden_out[...] = (normed * vecs[4:5, :] + vecs[5:6, :]).astype(BF)
        d_ffn = (vecs[7:8, :] * cot[...].astype(F32)).astype(BF)
        d_ffn_out[...] = d_ffn
        d_hidden[...] = jnp.zeros_like(d_hidden)

    pre = mul(hidden_out[...], fc1[...]) + fc1_bias[...]
    gate = 0.5 * (1.0 + lax.erf(pre * ROOT_HALF))
    act_out[...] = (pre * gate).astype(BF)
    slope = gate + pre * jnp.exp(-0.5 * pre * pre) * GAUSS_NORM
    d_pre = (mul(d_ffn_out[...], fc2[...], NT) * slope).astype(BF)
    d_pre_out[...] = d_pre
    fc1_bias_out[...] = jnp.sum(d_pre.astype(F32), axis=0, keepdims=True)
    d_hidden[...] += mul(d_pre, fc1[...], NT)

    @pl.when(step == pl.num_programs(0) - 1)
    def _():
        grad = d_hidden[...]
        mixed = mixed_held[...]
        normed, inverse = layer_norm(resid_out[...])
        d_resid = cot[...].astype(F32) + layer_norm_back(grad, normed, inverse, vecs[4:5, :])
        d_resid_out[...] = d_resid
        d_mixed = (vecs[3:4, :] * d_resid).astype(BF)
        d_mixed_out[...] = d_mixed
        small_out[0:1, :] = jnp.sum(grad * normed, axis=0, keepdims=True)
        small_out[1:2, :] = jnp.sum(grad, axis=0, keepdims=True)
        small_out[2:3, :] = jnp.sum(d_resid * mixed, axis=0, keepdims=True)
        small_out[3:4, :] = jnp.sum(d_mixed.astype(F32), axis=0, keepdims=True)
        small_out[4:5, :] = jnp.sum(d_ffn_out[...].astype(F32), axis=0, keepdims=True)
        small_out[5:8, :] = jnp.zeros((3, small_out.shape[1]), F32)
        grad_own_out[...] = mul(d_mixed, proj_own[...], NT).astype(BF)
        grad_send_out[...] = mul(d_mixed, proj_other[...], NT).astype(BF)


def fc2_grad_kernel(place, act, d_ffn, attn, d_mixed, keep_out, send_out, held, *, rest):
    step = pl.program_id(0)
    held[...] = mul(act[...], d_ffn[...], TN)
    core = place[1]
    for pair in range(2):
        for seq in range(2):
            at = rest(pair, step, seq) ^ place[2]
            columns = slice(384 * seq, 384 * seq + 384)
            low = pl.multiple_of(384 * pair + 192 * core, 64)
            high = pl.multiple_of(384 * pair + 192 * (1 - core), 64)
            keep_out[at, :192] = held[pl.ds(low, 192), columns].astype(BF)
            send_out[at, :192] = held[pl.ds(high, 192), columns].astype(BF)

    @pl.when(step == pl.num_programs(0) - 1)
    def _():
        held[...] = mul(attn[...], d_mixed[...], TN)
        for pair in range(8):
            low = pl.multiple_of(96 * pair + 48 * core, 16)
            high = pl.multiple_of(96 * pair + 48 * (1 - core), 16)
            for side in range(2):
                at = rest(pair % 2, pair // 2, side) ^ place[2]
                columns = slice(384 * side, 384 * side + 384)
                keep_out[at, 192:] = held[pl.ds(low, 48), columns].astype(BF)
                send_out[at, 192:] = held[pl.ds(high, 48), columns].astype(BF)


def fc1_grad_kernel(place, hidden, d_pre, keep_out, send_out, held, *, rest):
    step = pl.program_id(0)
    core = place[1]
    held[...] = mul(hidden[...], d_pre[...], TN)
    seq = step // 2
    lanes = pl.ds(pl.multiple_of((step % 2) * 768, LANES), 768)
    for pair in range(8):
        at = rest(pair % 2, pair // 2, seq) ^ place[3]
        low = pl.multiple_of(96 * pair + 48 * core, 16)
        high = pl.multiple_of(96 * pair + 48 * (1 - core), 16)
        keep_out[at, :, lanes] = held[pl.ds(low, 48), :].astype(BF)
        send_out[at, :, lanes] = held[pl.ds(high, 48), :].astype(BF)


def result_kernel(place, act, fc2, resid, cot, vecs, result_out, small_out, total):
    step = pl.program_id(0)

    @pl.when(step == 0)
    def _():
        total[...] = jnp.zeros_like(total)

    total[...] += mul(act[...], fc2[...])

    @pl.when(step == pl.num_programs(0) - 1)
    def _():
        ffn = total[...] + vecs[6:7, :]
        result_out[...] = (resid[...] + vecs[7:8, :] * ffn).astype(BF)
        small_out[0:1, :] = jnp.sum(cot[...].astype(F32) * ffn, axis=0, keepdims=True)
        small_out[1:8, :] = jnp.zeros((7, small_out.shape[1]), F32)


def hidden1_grad_kernel(
    place, dqkv0, dqkv1, dqkv2, weight, own, other, keep_out, send_out, small_out, total, joined
):
    step = pl.program_id(0)
    rows = own.shape[0]
    here = pl.ds(pl.multiple_of(place[0] * rows, 64), rows)
    there = pl.ds(pl.multiple_of((1 - place[0]) * rows, 64), rows)

    @pl.when(step == 0)
    def _():
        total[...] = jnp.zeros_like(total)
        small_out[...] = jnp.zeros_like(small_out)

    for n, part in enumerate((dqkv0, dqkv1, dqkv2)):
        joined[:, LANES * n : LANES * (n + 1)] = part[0]
    grads = joined[...]
    total[...] += mul(grads, weight[...], NT)
    line = jnp.sum(grads.astype(F32), axis=0, keepdims=True)

    @pl.when(step == 0)
    def _():
        small_out[2:3, :384] = line

    @pl.when(step == 2)
    def _():
        small_out[2:3, 384:] = line
        mine = total[here, :]
        theirs = total[there, :]
        keep_out[...] = mine
        send_out[...] = theirs.astype(BF)
        normed_mine, _ = layer_norm(own[...].astype(F32))
        normed_theirs, _ = layer_norm(other[...].astype(F32))
        small_out[0:1, :] = jnp.sum(mine * normed_mine, axis=0, keepdims=True) + jnp.sum(
            theirs * normed_theirs, axis=0, keepdims=True
        )
        small_out[1:2, :] = jnp.sum(mine, axis=0, keepdims=True) + jnp.sum(
            theirs, axis=0, keepdims=True
        )


def qkv_grad_kernel(
    place, hidden, dqkv0, dqkv1, dqkv2, keep_out, send_out, held, joined, *, rest
):
    step = pl.program_id(0)
    core = place[1]
    for n, part in enumerate((dqkv0, dqkv1, dqkv2)):
        joined[:, LANES * n : LANES * (n + 1)] = part[0]
    held[...] = mul(hidden[...], joined[...], TN)
    lanes = pl.ds(pl.multiple_of(step * 384, LANES), 384)
    for pair in range(8):
        at = rest(pair % 2, pair // 2, 0) ^ place[4]
        low = pl.multiple_of(96 * pair + 48 * core, 16)
        high = pl.multiple_of(96 * pair + 48 * (1 - core), 16)
        keep_out[at, :, lanes] = held[pl.ds(low, 48), :].astype(BF)
        send_out[at, :, lanes] = held[pl.ds(high, 48), :].astype(BF)


def tokens_grad_kernel(place, keep, recv, own, d_resid, vecs, grad_out):
    grad = keep[...] + recv[...].astype(F32)
    normed, inverse = layer_norm(own[...].astype(F32))
    back = layer_norm_back(grad, normed, inverse, vecs[0:1, :])
    grad_out[...] = (d_resid[...] + back).astype(BF)


def rest_label(order):
    def rest(x_bit, line, seq):
        bits = {"x": x_bit, "z1": line & 1, "z2": line >> 1, "y": seq}
        total = 0
        for name in order[1:]:
            total = total * 2 + bits[name]
        return total

    return rest


ORDER_A = ("core", "x", "z1", "z2", "y")
ORDER_B = ("core", "y", "x", "z1", "z2")
ORDER_Q = ("core", "x", "z1", "z2")


SPAN = 2 * GRID - 1
CELLS = SPAN * SPAN


def flips():
    row = lax.broadcasted_iota(jnp.int32, (LANES, LANES), 0)
    lane = lax.broadcasted_iota(jnp.int32, (LANES, LANES), 1)
    return jnp.where(row + lane == LANES - 1, 1.0, 0.0)


def exact(left, right, dims):
    return lax.dot_general(
        left, right, dims, precision=lax.Precision.HIGHEST, preferred_element_type=F32
    )


def moved_window(source, start, target):
    base = start // LANES * LANES
    place = target % LANES
    held = source[:, base : base + 2 * LANES]
    turn = (place - (start - base)) % (2 * LANES)
    if turn:
        held = pltpu.roll(held, turn, axis=1)
    lane = lax.broadcasted_iota(jnp.int32, (1, 2 * LANES), 1)
    return jnp.where((lane >= place) & (lane < place + SPAN), held, 0.0)


def strips_kernel(place, table, strips_out, flat, sides):
    heads = table.shape[0]
    flat[...] = jnp.zeros_like(flat)
    flat[:heads, : CELLS + 3] = table[...]
    turned = pltpu.roll(flat[:, : 18 * LANES], 18 * LANES - CELLS, axis=1)
    tail = turned[:, :LANES]
    for n in range(18):
        block = 17 - n
        flat[:, LANES * n : LANES * (n + 1)] = exact(
            turned[:, LANES * block : LANES * (block + 1)], flips(), NN
        )
    sides[...] = jnp.zeros_like(sides)
    for b in range(SPAN):
        base = 24 * b // LANES * LANES
        part = moved_window(flat, SPAN * b, 24 * b)
        sides[b % 2, :, base : base + 2 * LANES] += part
    lane = lax.broadcasted_iota(jnp.int32, (16, LANES), 1)
    sides[0, :, 1152:1280] = jnp.where(lane < 3, tail, 0.0)
    for head in range(heads):
        for par in range(2):
            strips_out[head, par : par + 1, :] = sides[par, head : head + 1, :]


def pack_kernel(place, strip0, strip1, strip2, ffn, fc1_bias, last, result, packed):
    packed[...] = jnp.zeros_like(packed)
    for n in range(5):
        lanes = slice(256 * n, 256 * n + 256)
        for pair, strip in enumerate((strip0, strip1, strip2)):
            for head in range(2):
                for par in range(2):
                    row = 16 * n + 6 * par + 2 * pair + head
                    packed[row : row + 1, :] = strip[0, head, par : par + 1, lanes]
    for n in range(3):
        lanes = slice(256 * n, 256 * n + 256)
        row = 80 + 16 * n
        packed[row : row + 5, :] = ffn[0:5, lanes]
        packed[row + 5 : row + 6, :] = result[0:1, lanes]
        packed[row + 6 : row + 9, :] = last[0:3, lanes]
        for part in range(4):
            packed[row + 9 + part : row + 10 + part, :] = fc1_bias[
                :, 768 * part + 256 * n : 768 * part + 256 * n + 256
            ]


def unpack_kernel(
    place, packed, mate, table_out, norm2_gain, norm2_bias, scale1, proj_bias, fc2_bias, scale2,
    norm1_gain, norm1_bias, query_bias, value_bias, fc1_bias, flat, sides,
):
    heads = table_out.shape[0]
    half = heads // 2
    left = place[0] == 0
    flat[...] = jnp.zeros_like(flat)
    for n in range(5):
        lanes = slice(256 * n, 256 * n + 256)
        for par in range(2):
            rows = slice(16 * n + half * par, 16 * n + half * par + half)
            mine = packed[rows, :]
            theirs = mate[rows, :]
            sides[par, 0:half, lanes] = jnp.where(left, mine, theirs)
            sides[par, half:heads, lanes] = jnp.where(left, theirs, mine)
    for b in range(SPAN):
        target = SPAN * b
        base = target // LANES * LANES
        part = moved_window(sides.at[b % 2], 24 * b, target)
        flat[:, base : base + 2 * LANES] += part
    lane = lax.broadcasted_iota(jnp.int32, (16, LANES), 1)
    blocks = [
        exact(flat[:, LANES * (17 - n) : LANES * (18 - n)], flips(), NN) for n in range(18)
    ]
    blocks[0] = jnp.where(lane < 3, sides[0, :, 1152:1280], blocks[0])
    turned = pltpu.roll(jnp.concatenate(blocks, axis=1), CELLS, axis=1)
    table_out[...] = turned[:heads, : CELLS + 3]
    outs = (norm2_gain, norm2_bias, scale1, proj_bias, fc2_bias, scale2, norm1_gain, norm1_bias)
    for n in range(3):
        lanes = slice(256 * n, 256 * n + 256)
        for at, out in enumerate(outs):
            row = 80 + 16 * n + at
            out[0:1, lanes] = packed[row : row + 1, :] + mate[row : row + 1, :]
        for part in range(4):
            row = 89 + 16 * n + part
            fc1_bias[0:1, 768 * part + 256 * n : 768 * part + 256 * n + 256] = (
                packed[row : row + 1, :] + mate[row : row + 1, :]
            )
    for source, side in ((packed, place[0]), (mate, 1 - place[0])):
        line = jnp.concatenate([source[88 + 16 * n : 89 + 16 * n, :] for n in range(3)], axis=1)
        lanes = pl.ds(pl.multiple_of(side * 384, LANES), 384)
        query_bias[0:1, lanes] = line[:, :384]
        value_bias[0:1, lanes] = line[:, 384:]


def even_places():
    lane = np.arange(STRIP_WIDTH)[None, :]
    row = np.arange(STRIP)[:, None]
    turn = (lane - 1) // STRIP
    return np.where(row == 0, turn % 2 == 0, turn % 2 == 1).astype(np.float32)


def split_body(
    tokens,
    masked,
    out_grad,
    norm1_gain,
    norm1_bias,
    qkv_weight,
    query_bias,
    value_bias,
    rel_table,
    proj_weight,
    proj_bias,
    scale1,
    norm2_gain,
    norm2_bias,
    fc1_weight,
    fc1_bias,
    fc2_weight,
    fc2_bias,
    scale2,
):
    _, rows, width = tokens.shape
    slots = 2 * rows
    heads = rel_table.shape[1] // 2
    pairs = heads // 2
    share = width // 2
    hidden = fc1_weight.shape[1]
    seq = lax.axis_index("seq")
    img = lax.axis_index("img")
    core = img & 1
    line = img >> 2
    x_bit = (img >> 1) & 1
    place = jnp.stack(
        [
            seq,
            core,
            rest_label(ORDER_A)(x_bit, line, seq),
            rest_label(ORDER_B)(x_bit, line, seq),
            rest_label(ORDER_Q)(x_bit, line, seq),
        ]
    ).astype(jnp.int32)
    own = tokens.reshape(rows, width)
    other = swapped(own, "y")
    cot = (out_grad.astype(F32) * masked.astype(F32)[..., None]).astype(BF).reshape(rows, width)
    vecs = jnp.stack(
        [norm1_gain, norm1_bias, proj_bias, scale1, norm2_gain, norm2_bias, fc2_bias, scale2]
    )
    strips = run(
        strips_kernel, place, (1,), [full(rel_table.shape[::-1])], [full((2 * heads, 2, STRIP_WIDTH))],
        [shape((2 * heads, 2, STRIP_WIDTH), F32)],
        [pltpu.VMEM((16, 2432), F32), pltpu.VMEM((2, 16, STRIP_WIDTH), F32)], (rel_table.T,), 0,
    )[0]
    even_mask = jnp.asarray(even_places())

    qkv, hidden1 = run(
        qkv_kernel, place, (3,),
        [
            full((rows, width)), full((rows, width)), full((8, width)),
            spec((width, share), lambda t, p: (0, 2 * t + p[0])),
            spec((1, share), lambda t, p: (0, p[0])), spec((1, share), lambda t, p: (0, p[0])),
        ],
        [spec((1, slots, share), lambda t, p: (t, 0, 0)), full((slots, width))],
        [shape((3, slots, share), BF), shape((slots, width), BF)],
        [],
        (own, other, vecs, qkv_weight, query_bias.reshape(1, width), value_bias.reshape(1, width)),
        2 * slots * width * 3 * share,
    )
    pair_rows = spec((slots, LANES), lambda n, p: (0, n))
    pair_half = spec((rows, LANES), lambda n, p: (0, n))
    pair_qkv = spec((3, slots, LANES), lambda n, p: (0, 0, n))
    pair_expo = spec((2, slots, slots), lambda n, p: (n, 0, 0))
    attn_own, attn_send, expo, inv = run(
        attend_kernel, place, (pairs,),
        [pair_qkv, full((2 * heads, 2, STRIP_WIDTH)), full((STRIP, STRIP_WIDTH))],
        [pair_half, pair_half, pair_expo, pair_rows],
        [
            shape((rows, share), BF), shape((rows, share), BF),
            shape((heads, slots, slots), BF), shape((slots, share), F32),
        ],
        [pltpu.VMEM((2, STRIP, STRIP_WIDTH), F32), pltpu.VMEM((slots, LANES), F32)],
        (qkv, strips, even_mask),
        16 * slots * slots * 64 * heads,
    )
    attn_other = swapped(attn_send, "y")
    parts = 4
    part = hidden // parts
    whole = full((rows, width))
    sliced = spec((rows, part), lambda c, p: (0, c))
    (
        act, d_pre, fc1_bias_part, hidden2, resid, d_ffn, attn_low, d_mixed, d_resid,
        grad_own, grad_send, small_ffn,
    ) = run(
        ffn_kernel, place, (parts,),
        [
            whole, whole, full((rows, share)), full((rows, share)), full((8, width)),
            full((width, width)), spec((width, part), lambda c, p: (0, c)),
            spec((1, part), lambda c, p: (0, c)), spec((part, width), lambda c, p: (c, 0)),
            spec((share, width), lambda c, p: (p[0], 0)), spec((share, width), lambda c, p: (1 - p[0], 0)),
        ],
        [
            sliced, sliced, spec((1, part), lambda c, p: (0, c)), whole, whole, whole, whole, whole, whole,
            full((rows, share)), full((rows, share)), full((8, width)),
        ],
        [
            shape((rows, hidden), BF), shape((rows, hidden), BF), shape((1, hidden), F32),
            shape((rows, width), BF), shape((rows, width), F32), shape((rows, width), BF),
            shape((rows, width), BF), shape((rows, width), BF), shape((rows, width), F32),
            shape((rows, share), BF), shape((rows, share), BF), shape((8, width), F32),
        ],
        [pltpu.VMEM((rows, width), F32), pltpu.VMEM((rows, width), F32)],
        (
            own, cot, attn_own, attn_other, vecs, proj_weight, fc1_weight, fc1_bias.reshape(1, hidden),
            fc2_weight, proj_weight, proj_weight,
        ),
        2 * rows * width * (3 * hidden + 2 * width),
    )
    grad_other = swapped(grad_send, "y")
    block = (16, 240, share)
    keep_a, send_a = run(
        functools.partial(fc2_grad_kernel, rest=rest_label(ORDER_A)), place, (parts,),
        [sliced, whole, whole, whole], [full(block), full(block)],
        [shape(block, BF), shape(block, BF)],
        [pltpu.VMEM((part, width), F32)], (act, d_ffn, attn_low, d_mixed),
        2 * rows * width * hidden,
        after=(grad_send,),
    )
    terms_a = [keep_a, swapped(send_a, "core")]
    block = (16, 48, 4 * share)
    keep_b, send_b = run(
        functools.partial(fc1_grad_kernel, rest=rest_label(ORDER_B)), place, (parts,),
        [whole, sliced], [full(block), full(block)],
        [shape(block, BF), shape(block, BF)],
        [pltpu.VMEM((width, part), F32)], (hidden2, d_pre),
        2 * rows * width * (hidden + width), after=(send_a, grad_other),
    )
    terms_b = [keep_b, swapped(send_b, "core")]
    out_a1 = half_out(place, terms_a, (send_b,))
    terms_a = half_in(terms_a, out_a1, ORDER_A[1])

    def attend_back(pair, after):
        pair_expo = spec((2, slots, slots), lambda n, p: (pair, 0, 0))
        pair_rows = spec((slots, LANES), lambda n, p: (0, pair))
        pair_half = spec((rows, LANES), lambda n, p: (0, pair))
        return run(
            attend_back_kernel, place, (1,),
            [
                spec((3, slots, LANES), lambda n, p: (0, 0, pair)), pair_expo, pair_half, pair_half,
                pair_half, pair_half, pair_rows, full((STRIP, STRIP_WIDTH)),
            ],
            [full((3, slots, LANES)), full((1, 2, 2, STRIP_WIDTH))],
            [shape((3, slots, LANES), BF), shape((1, 2, 2, STRIP_WIDTH), F32)],
            [
                pltpu.VMEM((slots, LANES), F32), pltpu.VMEM((slots, LANES), F32),
                pltpu.VMEM((2, slots, slots), BF), pltpu.VMEM((2, STRIP, STRIP_WIDTH), F32),
                pltpu.VMEM((slots, LANES), F32),
            ],
            (qkv, expo, attn_own, attn_send, grad_own, grad_other, inv, even_mask),
            32 * slots * slots * 64 * 2, after=after,
        )

    dqkv0, strip0 = attend_back(0, (out_a1, send_b))
    out_b1 = half_out(place, terms_b, (dqkv0,))
    terms_b = half_in(terms_b, out_b1, ORDER_B[1])
    dqkv1, strip1 = attend_back(1, (dqkv0, out_b1))
    dqkv2, strip2 = attend_back(2, (dqkv1,))
    dqkv = (dqkv0, dqkv1, dqkv2)
    third = [spec((1, slots, LANES), lambda t, p: (t, 0, 0))] * 3
    dh_keep, dh_send, small_last = run(
        hidden1_grad_kernel, place, (3,),
        [*third, spec((width, share), lambda t, p: (0, 2 * t + p[0])), whole, whole],
        [whole, whole, full((8, width))],
        [shape((rows, width), F32), shape((rows, width), BF), shape((8, width), F32)],
        [pltpu.VMEM((slots, width), F32), pltpu.VMEM((slots, share), BF)], (*dqkv, qkv_weight, own, other),
        2 * slots * width * 3 * share,
    )
    block = (8, 48, 3 * share)
    keep_q, send_q = run(
        functools.partial(qkv_grad_kernel, rest=rest_label(ORDER_Q)), place, (3,),
        [full((slots, width)), *third], [full(block), full(block)],
        [shape(block, BF), shape(block, BF)],
        [pltpu.VMEM((width, share), F32), pltpu.VMEM((slots, share), BF)], (hidden1, *dqkv), 2 * slots * width * 3 * share,
        after=(dh_send,),
    )
    terms_q = [keep_q, swapped(send_q, "core")]
    result, small_result = run(
        result_kernel, place, (parts,),
        [sliced, spec((part, width), lambda c, p: (c, 0)), whole, whole, full((8, width))],
        [whole, full((8, width))],
        [shape((rows, width), BF), shape((8, width), F32)],
        [pltpu.VMEM((rows, width), F32)], (act, fc2_weight, resid, cot, vecs),
        2 * rows * width * hidden, after=(send_q,),
    )
    packed = run(
        pack_kernel, place, (1,),
        [*[full((1, 2, 2, STRIP_WIDTH))] * 3, full((8, width)), full((1, hidden)), full((8, width)), full((8, width))],
        [full((128, 256))], [shape((128, 256), F32)], [],
        (strip0, strip1, strip2, small_ffn, fc1_bias_part, small_last, small_result), 0,
    )[0]
    out_a2 = half_out(place, terms_a, (packed,))
    terms_a = half_in(terms_a, out_a2, "z1")
    out_b2 = half_out(place, terms_b, (out_a2,))
    terms_b = half_in(terms_b, out_b2, "x")
    out_q1 = half_out(place, terms_q, (out_b2,))
    terms_q = half_in(terms_q, out_q1, "x")
    mate = swapped(packed, "core")
    dh_recv = swapped(dh_send, "y")
    out_a3 = half_out(place, terms_a, (out_q1,))
    terms_a = half_in(terms_a, out_a3, "z2")
    out_b3 = half_out(place, terms_b, (out_a3,))
    terms_b = half_in(terms_b, out_b3, "z1")
    out_q2 = half_out(place, terms_q, (out_b3,))
    terms_q = half_in(terms_q, out_q2, "z1")
    packed = summed(place, packed, mate, (out_q2,))
    mate = swapped(packed, "x")
    tokens_grad = run(
        tokens_grad_kernel, place, (1,),
        [whole, whole, whole, whole, full((8, width))], [whole],
        [shape((rows, width), BF)], [], (dh_keep, dh_recv, own, d_resid, vecs), 0,
        after=(packed,),
    )[0]
    packed = summed(place, packed, mate, (tokens_grad,))
    mate = swapped(packed, "z1")
    out_a4 = half_out(place, terms_a, (packed,))
    terms_a = half_in(terms_a, out_a4, "y")
    out_b4 = half_out(place, terms_b, (out_a4,))
    terms_b = half_in(terms_b, out_b4, "z2")
    out_q3 = half_out(place, terms_q, (out_b4,))
    terms_q = half_in(terms_q, out_q3, "z2")
    packed = summed(place, packed, mate, (out_q3,))
    mate = swapped(packed, "z2")
    packed = summed(place, packed, mate)
    mate = swapped(packed, "y")
    fc2_proj = added(terms_a)
    fc1_grad = added(terms_b)
    qkv_part = added(terms_q)
    fc2_grad = fc2_proj[:192]
    proj_grad = fc2_proj[192:]
    on_left = seq == 0
    given = jnp.where(on_left, qkv_part[:, 2 * share :], qkv_part[:, :share]).astype(BF)
    taken = swapped(given, "y").astype(F32)
    qkv_grad = jnp.where(
        on_left,
        jnp.concatenate([qkv_part[:, :share], taken, qkv_part[:, share : 2 * share]], axis=1),
        jnp.concatenate([qkv_part[:, share : 2 * share], taken, qkv_part[:, 2 * share :]], axis=1),
    )

    vector = shape((1, width), F32)
    table_grad, *small = run(
        unpack_kernel, place, (1,), [full((128, 256))] * 2,
        [full(rel_table.shape[::-1]), *[full((1, width))] * 10, full((1, hidden))],
        [shape(rel_table.shape[::-1], F32), *[vector] * 10, shape((1, hidden), F32)],
        [pltpu.VMEM((16, 2432), F32), pltpu.VMEM((2, 16, STRIP_WIDTH), F32)], (packed, mate), 0,
    )
    small = [part.reshape(-1) for part in small]
    return (
        result.reshape(tokens.shape),
        tokens_grad.reshape(tokens.shape),
        small[6],
        small[7],
        qkv_grad,
        small[8],
        small[9],
        table_grad.T,
        proj_grad,
        small[3],
        small[2],
        small[0],
        small[1],
        fc1_grad,
        small[10],
        fc2_grad,
        small[4],
        small[5],
    )


def solution(mesh):
    in_specs = (
        P("img", "seq", None),
        P("img", "seq"),
        P("img", "seq", None),
        P(),
        P(),
        P(),
        P(),
        P(),
        P(),
        P(),
        P(),
        P(),
        P(),
        P(),
        P(),
        P(),
        P(),
        P(),
        P(),
    )
    out_specs = (
        P("img", "seq", None),
        P("img", "seq", None),
        P(),
        P(),
        P("img", "seq"),
        P(),
        P(),
        P(),
        P("img", "seq"),
        P(),
        P(),
        P(),
        P(),
        P("img", "seq"),
        P(),
        P("img", "seq"),
        P(),
        P(),
    )
    sizes = dict(mesh.shape)
    body = split_body if (sizes["img"], sizes["seq"]) == (16, 2) else general_body
    return jax.shard_map(body, mesh=mesh, in_specs=in_specs, out_specs=out_specs, check_vma=False)
```

```python
import functools

import jax
import jax.numpy as jnp
import numpy as np
from jax import lax
from jax.experimental import pallas as pl
from jax.experimental.pallas import tpu as pltpu
from jax.sharding import PartitionSpec as P

GRID = 24


EPSILON = 1e-06
NEGATIVE = -1e30
ROOT_HALF = 0.7071067811865476
GAUSS_NORM = 0.3989422804014327


def passed_along(value, axis, steps):
    count = lax.axis_size(axis)
    pairs = [(source, (source + steps) % count) for source in range(count)]
    return lax.ppermute(value, axis, pairs)


def gap_onehot():
    span_width = 2 * GRID - 1
    grid_ids = jnp.arange(GRID, dtype=jnp.int32)
    gaps = grid_ids[:, None, None] - grid_ids[None, :, None] + GRID - 1
    return (gaps == jnp.arange(span_width, dtype=jnp.int32)[None, None, :]).astype(jnp.float32)


def bias_full(rel_table, all_slots):
    highest = lax.Precision.HIGHEST
    span_width = 2 * GRID - 1
    far_index = span_width * span_width
    cells = GRID * GRID
    head_count = rel_table.shape[1]
    spare = all_slots - 1 - cells
    selector = gap_onehot()
    patch_table = rel_table[0:far_index].reshape(span_width, span_width, head_count)
    row_pick = jnp.einsum("pqa,abh->pqbh", selector, patch_table, precision=highest)
    spread = jnp.einsum("pqbh,rsb->hprqs", row_pick, selector, precision=highest)
    patch_bias = spread.reshape(head_count, cells, cells)
    patch_bias = jnp.concatenate(
        [
            patch_bias,
            jnp.broadcast_to(patch_bias[:, cells - 1 : cells, :], (head_count, spare, cells)),
        ],
        axis=1,
    )
    patch_bias = jnp.concatenate(
        [
            patch_bias,
            jnp.broadcast_to(
                patch_bias[:, :, cells - 1 : cells], (head_count, cells + spare, spare)
            ),
        ],
        axis=2,
    )
    top_row = jnp.broadcast_to(rel_table[far_index][:, None, None], (head_count, 1, all_slots - 1))
    left_col = jnp.broadcast_to(
        rel_table[far_index + 1][:, None, None], (head_count, all_slots - 1, 1)
    )
    corner = rel_table[far_index + 2][:, None, None]
    upper = jnp.concatenate([corner, top_row], axis=2)
    lower = jnp.concatenate([left_col, patch_bias], axis=2)
    return jnp.concatenate([upper, lower], axis=1)


def table_back(grad_full):
    highest = lax.Precision.HIGHEST
    span_width = 2 * GRID - 1
    cells = GRID * GRID
    head_count = grad_full.shape[0]
    corner = grad_full[:, 0, 0]
    far_grad = jnp.sum(grad_full[:, 0, 1:], axis=1)
    near_grad = jnp.sum(grad_full[:, 1:, 0], axis=1)
    patch_grad = grad_full[:, 1:, 1:]
    patch_grad = jnp.concatenate(
        [
            patch_grad[:, 0 : cells - 1, :],
            jnp.sum(patch_grad[:, cells - 1 :, :], axis=1, keepdims=True),
        ],
        axis=1,
    )
    patch_grad = jnp.concatenate(
        [
            patch_grad[:, :, 0 : cells - 1],
            jnp.sum(patch_grad[:, :, cells - 1 :], axis=2, keepdims=True),
        ],
        axis=2,
    )
    selector = gap_onehot()
    spread = patch_grad.reshape(head_count, GRID, GRID, GRID, GRID)
    row_sums = jnp.einsum("hprqs,rsb->pqbh", spread, selector, precision=highest)
    patch_table = jnp.einsum("pqa,pqbh->abh", selector, row_sums, precision=highest)
    tail = jnp.stack([far_grad, near_grad, corner], axis=0)
    return jnp.concatenate([patch_table.reshape(span_width * span_width, head_count), tail], axis=0)


def gelu_value(argument):
    return 0.5 * argument * (1.0 + lax.erf(argument * ROOT_HALF))


def gelu_slope(argument):
    return (
        0.5 * (1.0 + lax.erf(argument * ROOT_HALF))
        + argument * jnp.exp(-0.5 * argument * argument) * GAUSS_NORM
    )


def normalize(values, gain, shift):
    center = values - jnp.mean(values, axis=-1, keepdims=True)
    inverse = lax.rsqrt(jnp.mean(center * center, axis=-1, keepdims=True) + EPSILON)
    normed = center * inverse
    return (normed * gain + shift, normed, inverse)


def normalize_back(grad_out, normed, inverse, gain):
    signal = grad_out * gain
    inner = (
        signal
        - jnp.mean(signal, axis=-1, keepdims=True)
        - normed * jnp.mean(signal * normed, axis=-1, keepdims=True)
    )
    return (inverse * inner, jnp.sum(grad_out * normed, axis=0), jnp.sum(grad_out, axis=0))


def general_body(
    tokens,
    masked,
    out_grad,
    norm1_gain,
    norm1_bias,
    qkv_weight,
    query_bias,
    value_bias,
    rel_table,
    proj_weight,
    proj_bias,
    scale1,
    norm2_gain,
    norm2_bias,
    fc1_weight,
    fc1_bias,
    fc2_weight,
    fc2_bias,
    scale2,
):
    images, local_rows, model_width = tokens.shape
    head_count = rel_table.shape[1]
    head_size = model_width // head_count
    head_scale = head_size ** (-0.5)
    cycle_size = lax.axis_size("seq")
    position = lax.axis_index("seq")
    all_slots = local_rows * cycle_size
    key_pos = jnp.arange(all_slots, dtype=jnp.int32)
    position_bias = lax.dynamic_slice_in_dim(
        bias_full(rel_table, all_slots), position * local_rows, local_rows, 1
    )
    key_valid = key_pos <= GRID * GRID
    flat_rows = images * local_rows
    head_shape = (images, local_rows, head_count, head_size)
    inputs = tokens.astype(jnp.float32).reshape(flat_rows, model_width)
    normed1, centred1, inverse1 = normalize(inputs, norm1_gain, norm1_bias)
    hidden1 = normed1.astype(jnp.bfloat16)
    projected = jnp.dot(hidden1, qkv_weight, preferred_element_type=jnp.float32)
    queries = ((projected[:, 0:model_width] + query_bias) * head_scale).astype(jnp.bfloat16)
    keys_local = (
        projected[:, model_width : 2 * model_width]
        .astype(jnp.bfloat16)
        .reshape(images, local_rows, model_width)
    )
    values_local = (
        (projected[:, 2 * model_width :] + value_bias)
        .astype(jnp.bfloat16)
        .reshape(images, local_rows, model_width)
    )
    query_heads = queries.reshape(head_shape)

    def block_scores(key_block, offset):
        key_count = key_block.shape[1]
        key_heads = key_block.reshape(images, key_count, head_count, head_size)
        logits = jnp.einsum(
            "gqhd,gkhd->ghqk", query_heads, key_heads, preferred_element_type=jnp.float32
        )
        logits = logits + lax.dynamic_slice_in_dim(position_bias, offset, key_count, 2)[None]
        usable = lax.dynamic_slice_in_dim(key_valid, offset, key_count, 0)
        return (jnp.where(usable, logits, NEGATIVE), usable)

    row_max = jnp.full((images, head_count, local_rows), NEGATIVE, jnp.float32)
    key_block = lax.all_gather(keys_local, "seq", axis=1, tiled=True)
    value_block = lax.all_gather(values_local, "seq", axis=1, tiled=True)
    key_count = key_block.shape[1]
    scores, usable = block_scores(key_block, jnp.int32(0))
    new_max = jnp.maximum(row_max, jnp.max(scores, axis=-1))
    weights = jnp.where(usable, jnp.exp(scores - new_max[..., None]), 0.0)
    totals = jnp.sum(weights, axis=-1)
    value_heads = value_block.reshape(images, key_count, head_count, head_size)
    update = jnp.einsum(
        "ghqk,gkhd->gqhd",
        weights.astype(jnp.bfloat16),
        value_heads,
        preferred_element_type=jnp.float32,
    )
    weighted = update
    row_max, totals, weighted = (new_max, totals, weighted)
    log_total = row_max + jnp.log(totals)
    attended = weighted / jnp.transpose(totals, (0, 2, 1))[..., None]
    attn_low = attended.reshape(flat_rows, model_width).astype(jnp.bfloat16)
    mixed_out = jnp.dot(attn_low, proj_weight, preferred_element_type=jnp.float32) + proj_bias
    residual1 = inputs + scale1 * mixed_out
    normed2, centred2, inverse2 = normalize(residual1, norm2_gain, norm2_bias)
    hidden2 = normed2.astype(jnp.bfloat16)
    pre_act = jnp.dot(hidden2, fc1_weight, preferred_element_type=jnp.float32) + fc1_bias
    activated = gelu_value(pre_act).astype(jnp.bfloat16)
    ffn_out = jnp.dot(activated, fc2_weight, preferred_element_type=jnp.float32) + fc2_bias
    result = (residual1 + scale2 * ffn_out).astype(jnp.bfloat16).reshape(tokens.shape)
    cotangent = (out_grad.astype(jnp.float32) * masked.astype(jnp.float32)[..., None]).reshape(
        flat_rows, model_width
    )
    d_ffn = (scale2 * cotangent).astype(jnp.bfloat16)
    scale2_grad = jnp.sum(cotangent * ffn_out, axis=0)
    fc2_bias_grad = jnp.sum(d_ffn.astype(jnp.float32), axis=0)
    fc2_weight_grad = jnp.einsum("nf,nd->fd", activated, d_ffn, preferred_element_type=jnp.float32)
    d_act = jnp.einsum("nd,fd->nf", d_ffn, fc2_weight, preferred_element_type=jnp.float32)
    d_pre = (d_act * gelu_slope(pre_act)).astype(jnp.bfloat16)
    fc1_bias_grad = jnp.sum(d_pre.astype(jnp.float32), axis=0)
    fc1_weight_grad = jnp.einsum("nd,nf->df", hidden2, d_pre, preferred_element_type=jnp.float32)
    d_hidden2 = jnp.einsum("nf,df->nd", d_pre, fc1_weight, preferred_element_type=jnp.float32)
    back_two, norm2_gain_grad, norm2_bias_grad = normalize_back(
        d_hidden2, centred2, inverse2, norm2_gain
    )
    d_resid1 = cotangent + back_two
    d_mixed = (scale1 * d_resid1).astype(jnp.bfloat16)
    scale1_grad = jnp.sum(d_resid1 * mixed_out, axis=0)
    proj_bias_grad = jnp.sum(d_mixed.astype(jnp.float32), axis=0)
    proj_weight_grad = jnp.einsum(
        "nc,nd->cd", attn_low, d_mixed, preferred_element_type=jnp.float32
    )
    d_attn = jnp.einsum(
        "nd,cd->nc", d_mixed, proj_weight, preferred_element_type=jnp.float32
    ).astype(jnp.bfloat16)
    d_attn_heads = d_attn.reshape(head_shape)
    row_delta = jnp.transpose(
        jnp.sum(d_attn_heads.astype(jnp.float32) * attended, axis=-1), (0, 2, 1)
    )

    def back_block(key_block, value_block, offset):
        key_count = key_block.shape[1]
        scores, usable = block_scores(key_block, offset)
        prob_full = jnp.where(usable, jnp.exp(scores - log_total[..., None]), 0.0)
        prob_low = prob_full.astype(jnp.bfloat16)
        key_heads = key_block.reshape(images, key_count, head_count, head_size)
        value_heads = value_block.reshape(images, key_count, head_count, head_size)
        d_value = jnp.einsum(
            "ghqk,gqhd->gkhd", prob_low, d_attn_heads, preferred_element_type=jnp.float32
        )
        d_probs = jnp.einsum(
            "gqhd,gkhd->ghqk", d_attn_heads, value_heads, preferred_element_type=jnp.float32
        )
        d_scores = (prob_full * (d_probs - row_delta[..., None])).astype(jnp.bfloat16)
        d_query = jnp.einsum(
            "ghqk,gkhd->gqhd", d_scores, key_heads, preferred_element_type=jnp.float32
        )
        d_key = jnp.einsum(
            "ghqk,gqhd->gkhd", d_scores, query_heads, preferred_element_type=jnp.float32
        )
        table_part = jnp.sum(d_scores.astype(jnp.float32), axis=0)
        return (
            d_query,
            d_key.reshape(images, key_count, model_width),
            d_value.reshape(images, key_count, model_width),
            table_part,
        )

    def turn_grads(grad_pair):
        return (
            passed_along(grad_pair[0].astype(jnp.bfloat16), "seq", 1).astype(jnp.float32),
            passed_along(grad_pair[1].astype(jnp.bfloat16), "seq", 1).astype(jnp.float32),
        )

    def cycle_step(turn_index, cycle_state):
        key_block, value_block, d_key_acc, d_value_acc, d_query_acc, table_acc = cycle_state
        owner_rank = (position - turn_index) % cycle_size
        offset = owner_rank * local_rows
        d_query, d_key, d_value, table_part = back_block(key_block, value_block, offset)
        table_acc = lax.dynamic_update_slice_in_dim(table_acc, table_part, offset, 2)
        d_key_acc, d_value_acc = turn_grads((d_key_acc + d_key, d_value_acc + d_value))
        key_block, value_block = passed_along((key_block, value_block), "seq", 1)
        return (key_block, value_block, d_key_acc, d_value_acc, d_query_acc + d_query, table_acc)

    kv_zeros = jnp.zeros((images, local_rows, model_width), jnp.float32)
    initial = (
        keys_local,
        values_local,
        kv_zeros,
        kv_zeros,
        jnp.zeros(head_shape, jnp.float32),
        jnp.zeros((head_count, local_rows, all_slots), jnp.float32),
    )
    cycle_state = lax.fori_loop(0, cycle_size - 1, cycle_step, initial)
    key_block, value_block, d_key_acc, d_value_acc, d_query_acc, table_acc = cycle_state
    offset = (position + 1) % cycle_size * local_rows
    d_query, d_key, d_value, table_part = back_block(key_block, value_block, offset)
    table_acc = lax.dynamic_update_slice_in_dim(table_acc, table_part, offset, 2)
    d_key_all, d_value_all = turn_grads((d_key_acc + d_key, d_value_acc + d_value))
    d_query_all = d_query_acc + d_query
    d_query_low = d_query_all.reshape(flat_rows, model_width).astype(jnp.bfloat16) * head_scale
    d_key_low = d_key_all.reshape(flat_rows, model_width).astype(jnp.bfloat16)
    d_value_low = d_value_all.reshape(flat_rows, model_width).astype(jnp.bfloat16)
    d_qkv = jnp.concatenate([d_query_low, d_key_low, d_value_low], axis=1)
    qkv_weight_grad = jnp.einsum("nd,ne->de", hidden1, d_qkv, preferred_element_type=jnp.float32)
    query_bias_grad = jnp.sum(d_query_low.astype(jnp.float32), axis=0)
    value_bias_grad = jnp.sum(d_value_low.astype(jnp.float32), axis=0)
    d_hidden1 = jnp.einsum("ne,de->nd", d_qkv, qkv_weight, preferred_element_type=jnp.float32)
    back_one, norm1_gain_grad, norm1_bias_grad = normalize_back(
        d_hidden1, centred1, inverse1, norm1_gain
    )
    tokens_grad = (d_resid1 + back_one).astype(jnp.bfloat16).reshape(tokens.shape)
    grad_square = lax.dynamic_update_slice_in_dim(
        jnp.zeros((head_count, all_slots, all_slots), jnp.float32),
        table_acc,
        position * local_rows,
        1,
    )
    table_grad = table_back(grad_square)
    half_summed = (
        lax.psum_scatter(
            qkv_weight_grad.astype(jnp.bfloat16), "img", scatter_dimension=0, tiled=True
        ).astype(jnp.float32),
        lax.psum_scatter(
            proj_weight_grad.astype(jnp.bfloat16), "img", scatter_dimension=0, tiled=True
        ).astype(jnp.float32),
        lax.psum_scatter(
            fc1_weight_grad.astype(jnp.bfloat16), "img", scatter_dimension=0, tiled=True
        ).astype(jnp.float32),
        lax.psum_scatter(
            fc2_weight_grad.astype(jnp.bfloat16), "img", scatter_dimension=0, tiled=True
        ).astype(jnp.float32),
    )
    summed = (
        lax.psum_scatter(
            half_summed[0].astype(jnp.bfloat16), "seq", scatter_dimension=1, tiled=True
        ).astype(jnp.float32),
        lax.psum_scatter(
            half_summed[1].astype(jnp.bfloat16), "seq", scatter_dimension=1, tiled=True
        ).astype(jnp.float32),
        lax.psum_scatter(
            half_summed[2].astype(jnp.bfloat16), "seq", scatter_dimension=1, tiled=True
        ).astype(jnp.float32),
        lax.psum_scatter(
            half_summed[3].astype(jnp.bfloat16), "seq", scatter_dimension=1, tiled=True
        ).astype(jnp.float32),
    )
    smalls = lax.psum(
        (
            table_grad,
            norm1_gain_grad,
            norm1_bias_grad,
            query_bias_grad,
            value_bias_grad,
            proj_bias_grad,
            scale1_grad,
            norm2_gain_grad,
            norm2_bias_grad,
            fc1_bias_grad,
            fc2_bias_grad,
            scale2_grad,
        ),
        ("img", "seq"),
    )
    return (
        result,
        tokens_grad,
        smalls[1],
        smalls[2],
        summed[0],
        smalls[3],
        smalls[4],
        smalls[0],
        summed[1],
        smalls[5],
        smalls[6],
        smalls[7],
        smalls[8],
        summed[2],
        smalls[9],
        summed[3],
        smalls[10],
        smalls[11],
    )


LANES = 128
RATE = 1.15e9
STRIP = 24
STRIP_WIDTH = 1280
MEGA = 1 << 20
NT = (((1,), (1,)), ((), ()))
TN = (((0,), (0,)), ((), ()))
NN = (((1,), (0,)), ((), ()))
BF = jnp.bfloat16
F32 = jnp.float32


def mul(left, right, dims=NN):
    return lax.dot_general(left, right, dims, preferred_element_type=F32)


def bits_of(img, seq):
    line = img >> 2
    return {"core": img & 1, "x": (img >> 1) & 1, "z1": line & 1, "z2": line >> 1, "y": seq}


def label_of(img, seq, order):
    bits = bits_of(img, seq)
    total = 0
    for name in order:
        total = total * 2 + bits[name]
    return total


def swap_pairs(*names):
    order = ("core", "x", "z1", "z2", "y")
    where = {label_of(img, seq, order): img * 2 + seq for img in range(16) for seq in range(2)}
    flip = sum(1 << (len(order) - 1 - order.index(name)) for name in names)
    return [(device, where[label ^ flip]) for label, device in where.items()]


def swapped(value, *names):
    return lax.ppermute(value, ("img", "seq"), swap_pairs(*names))


def added(terms):
    return sum(term[0].astype(F32) for term in terms)


def layer_norm(values):
    center = values - jnp.mean(values, axis=-1, keepdims=True)
    inverse = lax.rsqrt(jnp.mean(center * center, axis=-1, keepdims=True) + EPSILON)
    return center * inverse, inverse


def layer_norm_back(grad_out, normed, inverse, gain):
    signal = grad_out * gain
    return inverse * (
        signal
        - jnp.mean(signal, axis=-1, keepdims=True)
        - normed * jnp.mean(signal * normed, axis=-1, keepdims=True)
    )


def spec(block, index):
    return pl.BlockSpec(block, index)


def full(shape):
    zeros = (0,) * len(shape)
    return pl.BlockSpec(shape, lambda *_: zeros)


SIZES = {
    "strips_kernel": (1.7, 6),
    "qkv_kernel": (3.5, 12),
    "attend_kernel": (11.0, 16),
    "ffn_kernel": (9.5, 26),
    "fc2_grad_kernel": (5.4, 26),
    "fc1_grad_kernel": (4.6, 24),
    "attend_back_kernel": (4.4, 16),
    "hidden1_grad_kernel": (4.2, 14),
    "qkv_grad_kernel": (3.2, 16),
    "result_kernel": (4.0, 12),
    "tokens_grad_kernel": (2.0, 12),
}


def run(kernel, place, grid, in_specs, out_specs, out_shapes, scratch, operands, flops, after=(), us=None):
    held = len(operands)
    inner = kernel
    cost, vmem = SIZES.get(getattr(kernel, "func", kernel).__name__, (1.5, 10))
    us = us or cost

    def kernel(place_ref, *refs):
        inner(place_ref, *refs[:held], *refs[held + len(after) :])

    in_specs = [*in_specs, *[pl.BlockSpec(memory_space=pl.ANY)] * len(after)]
    return pl.pallas_call(
        kernel,
        grid_spec=pltpu.PrefetchScalarGridSpec(
            num_scalar_prefetch=1,
            grid=grid,
            in_specs=in_specs,
            out_specs=out_specs,
            scratch_shapes=scratch,
        ),
        out_shape=out_shapes,
        compiler_params=pltpu.CompilerParams(vmem_limit_bytes=vmem * MEGA),
        cost_estimate=pl.CostEstimate(flops=int(us * RATE), bytes_accessed=1, transcendentals=0),
    )(place, *operands, *after)


def add_kernel(place, *refs):
    refs[-1][...] = sum(ref[...].astype(F32) for ref in refs[:-1]).astype(BF)


def half_out(place, terms, after=()):
    size = terms[-1].shape[0] // 2
    block = (min(size, 4), *terms[0].shape[1:])
    count = size // block[0]
    return run(
        add_kernel, place, (count,), [spec(block, lambda n, p: (n + count, 0, 0))] * len(terms),
        [spec(block, lambda n, p: (n, 0, 0))], [shape((size, *block[1:]), BF)], [], tuple(terms), 0,
        after=after,
    )[0]


def rest_of(place, terms, after=()):
    size = terms[-1].shape[0] // 2
    block = (min(size, 4), *terms[0].shape[1:])
    same = spec(block, lambda n, p: (n, 0, 0))
    return run(
        add_kernel, place, (size // block[0],), [same] * len(terms), [same],
        [shape((size, *block[1:]), BF)], [], tuple(terms), 0, after=after,
    )[0]


def sum_kernel(place, left, right, out):
    out[...] = left[...] + right[...]


def summed(place, left, right, after=()):
    return run(
        sum_kernel, place, (1,), [full(left.shape)] * 2, [full(left.shape)],
        [shape(left.shape, F32)], [], (left, right), 0, after=after,
    )[0]


def shape(dims, dtype):
    return jax.ShapeDtypeStruct(dims, dtype)


def qkv_kernel(place, own, other, vecs, weight, qb, vb, qkv_out, hidden_out):
    step = pl.program_id(0)
    rows = own.shape[0]

    @pl.when(step == 0)
    def _():
        for source, side in ((own, place[0]), (other, 1 - place[0])):
            normed, _ = layer_norm(source[...].astype(F32))
            low = (normed * vecs[0:1, :] + vecs[1:2, :]).astype(BF)
            hidden_out[pl.ds(pl.multiple_of(side * rows, 64), rows), :] = low

    wide = mul(hidden_out[...], weight[...])
    shift = jnp.where(step == 0, qb[...], jnp.where(step == 2, vb[...], 0.0))
    factor = jnp.where(step == 0, 0.125, 1.0)
    qkv_out[0] = ((wide + shift) * factor).astype(BF)


def window(strip, block):
    off = (STRIP - block) * STRIP
    base = off // LANES * LANES
    held = strip[:, base : base + 6 * LANES]
    if off - base:
        held = pltpu.roll(held, 6 * LANES - (off - base), axis=1)
    return held[:, : 5 * LANES]


CHUNKS = tuple((start * 144, 144) for start in range(4)) + ((576, 64),)


def attend_kernel(place, qkv, strips, even_mask, own_out, send_out, expo_out, inv_out, strip, attended):
    slots = qkv.shape[1]
    half = slots // 2
    side = place[0]
    lane = lax.broadcasted_iota(jnp.int32, (1, LANES), 1)
    first = lane < LANES // 2
    masks = (jnp.where(first, 1.0, 0.0).astype(BF), jnp.where(first, 0.0, 1.0).astype(BF))
    keys = [qkv[1] * m for m in masks]
    values = [qkv[2] * m for m in masks]
    picks = even_mask[...] > 0.5
    at = side * 6 + 2 * pl.program_id(0)
    for head in range(2):
        rolled = [
            pltpu.roll(
                jnp.broadcast_to(strips[at + head, par : par + 1, :], (STRIP, STRIP_WIDTH)),
                1,
                axis=1,
                stride=1,
                stride_axis=0,
            )
            for par in range(2)
        ]
        strip[head] = jnp.where(picks, rolled[0], rolled[1])
    block_lane = lax.broadcasted_iota(jnp.int32, (STRIP, LANES), 1)
    block_row = lax.broadcasted_iota(jnp.int32, (STRIP, LANES), 0)
    for start, count in CHUNKS:
        query = qkv[0, start : start + count, :]
        total = None
        scale = None
        for head in range(2):
            lone = strips[at + head, 0:1, 1152:1280]
            far = lone[:, 0:1]
            near = lone[:, 1:2]
            corner = lone[:, 2:3]
            biases = []
            for block in range(start // STRIP, -(-(start + count) // STRIP)):
                if start == 576:
                    row = window(strip.at[head, 0:8, :], STRIP)[0:1, :]
                    piece = jnp.broadcast_to(row, (count, 5 * LANES))
                    ids = lax.broadcasted_iota(jnp.int32, (count, LANES), 1)
                else:
                    piece = window(strip.at[head], block)
                    ids = block_lane
                left = jnp.where(ids == 0, near, piece[:, :LANES])
                if block == 0:
                    piece = jnp.concatenate(
                        [
                            jnp.where(
                                block_row == 0, jnp.where(ids == 0, corner, far), left
                            )
                        ]
                        + [
                            jnp.where(block_row == 0, far, piece[:, n * LANES : (n + 1) * LANES])
                            for n in range(1, 4)
                        ]
                        + [
                            jnp.where(
                                ids > 64, NEGATIVE, jnp.where(block_row == 0, far, piece[:, 4 * LANES :])
                            )
                        ],
                        axis=1,
                    )
                else:
                    piece = jnp.concatenate(
                        [
                            left,
                            piece[:, LANES : 4 * LANES],
                            jnp.where(ids > 64, NEGATIVE, piece[:, 4 * LANES :]),
                        ],
                        axis=1,
                    )
                biases.append(piece)
                if start == 576:
                    break
            scores = mul(query, keys[head], NT) + jnp.concatenate(biases, axis=0)
            top = jnp.max(scores, axis=1, keepdims=True)
            expo = jnp.exp(scores - top)
            inverse = 1.0 / jnp.sum(expo, axis=1, keepdims=True)
            low = expo.astype(BF)
            expo_out[head, start : start + count, :] = low
            part = mul(low, values[head]) * inverse
            total = part if head == 0 else total + part
            spread = jnp.broadcast_to(inverse, (count, LANES))
            scale = spread if head == 0 else jnp.where(first, scale, spread)
        attended[start : start + count, :] = total
        inv_out[start : start + count, :] = scale
    own_out[...] = attended[pl.ds(pl.multiple_of(side * half, 64), half), :].astype(BF)
    send_out[...] = attended[pl.ds(pl.multiple_of((1 - side) * half, 64), half), :].astype(BF)


def attend_back_kernel(
    place, qkv, expo, attn_own, attn_send, grad_own, grad_other, inv, even_mask,
    dqkv_out, strip_out, grad_all, attn_all, d_scores, strip, dq_all,
):
    slots = qkv.shape[1]
    half = slots // 2
    here = pl.ds(pl.multiple_of(place[0] * half, 64), half)
    there = pl.ds(pl.multiple_of((1 - place[0]) * half, 64), half)
    lane = lax.broadcasted_iota(jnp.int32, (1, LANES), 1)
    first = lane < LANES // 2
    masks = (jnp.where(first, 1.0, 0.0).astype(BF), jnp.where(first, 0.0, 1.0).astype(BF))
    scaled = grad_own[...].astype(F32) * inv[here, :]
    grad_all[here, :] = scaled
    attn_all[here, :] = scaled * attn_own[...].astype(F32)
    scaled = grad_other[...].astype(F32) * inv[there, :]
    grad_all[there, :] = scaled
    attn_all[there, :] = scaled * attn_send[...].astype(F32)
    keys = [qkv[1] * m for m in masks]
    values = [qkv[2] * m for m in masks]
    block_lane = lax.broadcasted_iota(jnp.int32, (STRIP, LANES), 1)
    block_row = lax.broadcasted_iota(jnp.int32, (STRIP, LANES), 0)
    strip[...] = jnp.zeros_like(strip)
    columns = [jnp.zeros((8, LANES), F32) for _ in range(2)]
    tops = [None, None]
    zeros = jnp.zeros((STRIP, LANES), F32)
    for start, count in CHUNKS:
        grads = grad_all[start : start + count, :].astype(BF)
        products = attn_all[start : start + count, :]
        total = None
        for head in range(2):
            chosen = first if head == 0 else jnp.logical_not(first)
            delta = jnp.sum(jnp.where(chosen, products, 0.0), axis=1, keepdims=True)
            d_probs = mul(grads, values[head], NT)
            d_score = expo[head, start : start + count, :].astype(F32) * (d_probs - delta)
            low = d_score.astype(BF)
            d_scores[head, start : start + count, :] = low
            part = mul(low, keys[head])
            total = part if head == 0 else total + part
            if start == 576:
                for tile in range(count // 8):
                    columns[head] = columns[head] + d_score[8 * tile : 8 * tile + 8, :LANES]
                line = jnp.sum(d_score, axis=0, keepdims=True)
                line = jnp.concatenate([jnp.where(lane == 0, 0.0, line[:, :LANES]), line[:, LANES:]], axis=1)
                strip[head, 0:1, : 5 * LANES] = strip[head, 0:1, : 5 * LANES] + line
            else:
                for block in range(start // STRIP, (start + count) // STRIP):
                    at = block * STRIP - start
                    piece = d_score[at : at + STRIP, :]
                    left = piece[:, :LANES]
                    rest = piece[:, LANES:]
                    if block == 0:
                        tops[head] = piece[0:1, :]
                        left = jnp.where(block_row == 0, 0.0, left)
                        rest = jnp.concatenate(
                            [
                                jnp.where(block_row == 0, 0.0, rest[:, n * LANES : (n + 1) * LANES])
                                for n in range(4)
                            ],
                            axis=1,
                        )
                    columns[head] = columns[head] + left[0:8] + left[8:16] + left[16:24]
                    piece = jnp.concatenate(
                        [jnp.where(block_lane == 0, 0.0, left), rest, zeros], axis=1
                    )
                    off = (STRIP - block) * STRIP
                    base = off // LANES * LANES
                    if off - base:
                        piece = pltpu.roll(piece, off - base, axis=1)
                    strip[head, :, base : base + 6 * LANES] = (
                        strip[head, :, base : base + 6 * LANES] + piece
                    )
        dq_all[start : start + count, :] = total
    dqkv_out[0] = dq_all[...].astype(BF) * BF(0.125)
    d_key = None
    d_value = None
    low_grads = grad_all[...].astype(BF)
    for head in range(2):
        part = mul(d_scores[head], qkv[0] * masks[head], TN)
        d_key = part if head == 0 else d_key + part
        part = mul(expo[head], low_grads * masks[head], TN)
        d_value = part if head == 0 else d_value + part
    dqkv_out[1] = d_key.astype(BF)
    dqkv_out[2] = d_value.astype(BF)
    picks = even_mask[...] > 0.5
    row_id = lax.broadcasted_iota(jnp.int32, (STRIP, STRIP_WIDTH), 0)
    wide_lane = lax.broadcasted_iota(jnp.int32, (1, STRIP_WIDTH), 1)
    for head in range(2):
        held = strip[head]
        lines = []
        for par in range(2):
            part = jnp.where(picks, held, 0.0) if par == 0 else jnp.where(picks, 0.0, held)
            part = pltpu.roll(part, STRIP_WIDTH - 1, axis=1)
            for bit in (1, 2, 4, 8, 16):
                part = jnp.where(
                    (row_id & bit) > 0, pltpu.roll(part, STRIP_WIDTH - bit, axis=1), part
                )
            lines.append(jnp.sum(part, axis=0, keepdims=True))
        near = jnp.sum(jnp.where(lane == 0, columns[head], 0.0)).reshape(1, 1)
        corner = tops[head][:, 0:1]
        far = jnp.sum(tops[head], axis=1, keepdims=True) - corner
        line = lines[0]
        line = jnp.where(wide_lane >= 1152, 0.0, line)
        line = jnp.where(wide_lane == 1152, far, line)
        line = jnp.where(wide_lane == 1153, near, line)
        line = jnp.where(wide_lane == 1154, corner, line)
        strip_out[0, head, 0:1, :] = line
        strip_out[0, head, 1:2, :] = lines[1]


def ffn_kernel(
    place, tokens, cot, attn_own, attn_other, vecs, proj, fc1, fc1_bias, fc2, proj_own, proj_other,
    act_out, d_pre_out, fc1_bias_out, hidden_out, resid_out, d_ffn_out, attn_out, d_mixed_out, d_resid_out,
    grad_own_out, grad_send_out, small_out, mixed_held, d_hidden,
):
    step = pl.program_id(0)
    width = attn_own.shape[1]

    @pl.when(step == 0)
    def _():
        attn_out[:, pl.ds(pl.multiple_of(place[0] * width, LANES), width)] = attn_own[...]
        attn_out[:, pl.ds(pl.multiple_of((1 - place[0]) * width, LANES), width)] = attn_other[...]
        mixed = mul(attn_out[...], proj[...]) + vecs[2:3, :]
        mixed_held[...] = mixed
        resid = tokens[...].astype(F32) + vecs[3:4, :] * mixed
        resid_out[...] = resid
        normed, _ = layer_norm(resid)
        hidden_out[...] = (normed * vecs[4:5, :] + vecs[5:6, :]).astype(BF)
        d_ffn = (vecs[7:8, :] * cot[...].astype(F32)).astype(BF)
        d_ffn_out[...] = d_ffn
        d_hidden[...] = jnp.zeros_like(d_hidden)

    pre = mul(hidden_out[...], fc1[...]) + fc1_bias[...]
    gate = 0.5 * (1.0 + lax.erf(pre * ROOT_HALF))
    act_out[...] = (pre * gate).astype(BF)
    slope = gate + pre * jnp.exp(-0.5 * pre * pre) * GAUSS_NORM
    d_pre = (mul(d_ffn_out[...], fc2[...], NT) * slope).astype(BF)
    d_pre_out[...] = d_pre
    fc1_bias_out[...] = jnp.sum(d_pre.astype(F32), axis=0, keepdims=True)
    d_hidden[...] += mul(d_pre, fc1[...], NT)

    @pl.when(step == pl.num_programs(0) - 1)
    def _():
        grad = d_hidden[...]
        mixed = mixed_held[...]
        normed, inverse = layer_norm(resid_out[...])
        d_resid = cot[...].astype(F32) + layer_norm_back(grad, normed, inverse, vecs[4:5, :])
        d_resid_out[...] = d_resid
        d_mixed = (vecs[3:4, :] * d_resid).astype(BF)
        d_mixed_out[...] = d_mixed
        small_out[0:1, :] = jnp.sum(grad * normed, axis=0, keepdims=True)
        small_out[1:2, :] = jnp.sum(grad, axis=0, keepdims=True)
        small_out[2:3, :] = jnp.sum(d_resid * mixed, axis=0, keepdims=True)
        small_out[3:4, :] = jnp.sum(d_mixed.astype(F32), axis=0, keepdims=True)
        small_out[4:5, :] = jnp.sum(d_ffn_out[...].astype(F32), axis=0, keepdims=True)
        small_out[5:8, :] = jnp.zeros((3, small_out.shape[1]), F32)
        grad_own_out[...] = mul(d_mixed, proj_own[...], NT).astype(BF)
        grad_send_out[...] = mul(d_mixed, proj_other[...], NT).astype(BF)


def fc2_grad_kernel(place, act, d_ffn, attn, d_mixed, keep_out, send_out, held, *, rest):
    step = pl.program_id(0)
    held[...] = mul(act[...], d_ffn[...], TN)
    core = place[1]
    for pair in range(2):
        for seq in range(2):
            at = rest(pair, step, seq) ^ place[2]
            columns = slice(384 * seq, 384 * seq + 384)
            low = pl.multiple_of(384 * pair + 192 * core, 64)
            high = pl.multiple_of(384 * pair + 192 * (1 - core), 64)
            keep_out[at, :192] = held[pl.ds(low, 192), columns].astype(BF)
            send_out[at, :192] = held[pl.ds(high, 192), columns].astype(BF)

    @pl.when(step == pl.num_programs(0) - 1)
    def _():
        held[...] = mul(attn[...], d_mixed[...], TN)
        for pair in range(8):
            low = pl.multiple_of(96 * pair + 48 * core, 16)
            high = pl.multiple_of(96 * pair + 48 * (1 - core), 16)
            for side in range(2):
                at = rest(pair % 2, pair // 2, side) ^ place[2]
                columns = slice(384 * side, 384 * side + 384)
                keep_out[at, 192:] = held[pl.ds(low, 48), columns].astype(BF)
                send_out[at, 192:] = held[pl.ds(high, 48), columns].astype(BF)


def fc1_grad_kernel(place, hidden, d_pre, keep_out, send_out, held, *, rest):
    step = pl.program_id(0)
    core = place[1]
    held[...] = mul(hidden[...], d_pre[...], TN)
    seq = step // 2
    lanes = pl.ds(pl.multiple_of((step % 2) * 768, LANES), 768)
    for pair in range(8):
        at = rest(pair % 2, pair // 2, seq) ^ place[3]
        low = pl.multiple_of(96 * pair + 48 * core, 16)
        high = pl.multiple_of(96 * pair + 48 * (1 - core), 16)
        keep_out[at, :, lanes] = held[pl.ds(low, 48), :].astype(BF)
        send_out[at, :, lanes] = held[pl.ds(high, 48), :].astype(BF)


def result_kernel(place, act, fc2, resid, cot, vecs, result_out, small_out, total):
    step = pl.program_id(0)

    @pl.when(step == 0)
    def _():
        total[...] = jnp.zeros_like(total)

    total[...] += mul(act[...], fc2[...])

    @pl.when(step == pl.num_programs(0) - 1)
    def _():
        ffn = total[...] + vecs[6:7, :]
        result_out[...] = (resid[...] + vecs[7:8, :] * ffn).astype(BF)
        small_out[0:1, :] = jnp.sum(cot[...].astype(F32) * ffn, axis=0, keepdims=True)
        small_out[1:8, :] = jnp.zeros((7, small_out.shape[1]), F32)


def hidden1_grad_kernel(
    place, dqkv0, dqkv1, dqkv2, weight, own, other, keep_out, send_out, small_out, total, joined
):
    step = pl.program_id(0)
    rows = own.shape[0]
    here = pl.ds(pl.multiple_of(place[0] * rows, 64), rows)
    there = pl.ds(pl.multiple_of((1 - place[0]) * rows, 64), rows)

    @pl.when(step == 0)
    def _():
        total[...] = jnp.zeros_like(total)
        small_out[...] = jnp.zeros_like(small_out)

    for n, part in enumerate((dqkv0, dqkv1, dqkv2)):
        joined[:, LANES * n : LANES * (n + 1)] = part[0]
    grads = joined[...]
    total[...] += mul(grads, weight[...], NT)
    line = jnp.sum(grads.astype(F32), axis=0, keepdims=True)

    @pl.when(step == 0)
    def _():
        small_out[2:3, :384] = line

    @pl.when(step == 2)
    def _():
        small_out[2:3, 384:] = line
        mine = total[here, :]
        theirs = total[there, :]
        keep_out[...] = mine
        send_out[...] = theirs.astype(BF)
        normed_mine, _ = layer_norm(own[...].astype(F32))
        normed_theirs, _ = layer_norm(other[...].astype(F32))
        small_out[0:1, :] = jnp.sum(mine * normed_mine, axis=0, keepdims=True) + jnp.sum(
            theirs * normed_theirs, axis=0, keepdims=True
        )
        small_out[1:2, :] = jnp.sum(mine, axis=0, keepdims=True) + jnp.sum(
            theirs, axis=0, keepdims=True
        )


def qkv_grad_kernel(
    place, hidden, dqkv0, dqkv1, dqkv2, keep_out, send_out, held, joined, *, rest
):
    step = pl.program_id(0)
    core = place[1]
    for n, part in enumerate((dqkv0, dqkv1, dqkv2)):
        joined[:, LANES * n : LANES * (n + 1)] = part[0]
    held[...] = mul(hidden[...], joined[...], TN)
    lanes = pl.ds(pl.multiple_of(step * 384, LANES), 384)
    for pair in range(8):
        at = rest(pair % 2, pair // 2, 0) ^ place[4]
        low = pl.multiple_of(96 * pair + 48 * core, 16)
        high = pl.multiple_of(96 * pair + 48 * (1 - core), 16)
        keep_out[at, :, lanes] = held[pl.ds(low, 48), :].astype(BF)
        send_out[at, :, lanes] = held[pl.ds(high, 48), :].astype(BF)


def tokens_grad_kernel(place, keep, recv, own, d_resid, vecs, grad_out):
    grad = keep[...] + recv[...].astype(F32)
    normed, inverse = layer_norm(own[...].astype(F32))
    back = layer_norm_back(grad, normed, inverse, vecs[0:1, :])
    grad_out[...] = (d_resid[...] + back).astype(BF)


def rest_label(order):
    def rest(x_bit, line, seq):
        bits = {"x": x_bit, "z1": line & 1, "z2": line >> 1, "y": seq}
        total = 0
        for name in order[1:]:
            total = total * 2 + bits[name]
        return total

    return rest


ORDER_A = ("core", "x", "z1", "z2", "y")
ORDER_B = ("core", "y", "x", "z1", "z2")
ORDER_Q = ("core", "x", "z1", "z2")


SPAN = 2 * GRID - 1
CELLS = SPAN * SPAN


def flips():
    row = lax.broadcasted_iota(jnp.int32, (LANES, LANES), 0)
    lane = lax.broadcasted_iota(jnp.int32, (LANES, LANES), 1)
    return jnp.where(row + lane == LANES - 1, 1.0, 0.0)


def exact(left, right, dims):
    return lax.dot_general(
        left, right, dims, precision=lax.Precision.HIGHEST, preferred_element_type=F32
    )


def moved_window(source, start, target):
    base = start // LANES * LANES
    place = target % LANES
    held = source[:, base : base + 2 * LANES]
    turn = (place - (start - base)) % (2 * LANES)
    if turn:
        held = pltpu.roll(held, turn, axis=1)
    lane = lax.broadcasted_iota(jnp.int32, (1, 2 * LANES), 1)
    return jnp.where((lane >= place) & (lane < place + SPAN), held, 0.0)


def strips_kernel(place, table, strips_out, flat, sides):
    heads = table.shape[0]
    flat[...] = jnp.zeros_like(flat)
    flat[:heads, : CELLS + 3] = table[...]
    turned = pltpu.roll(flat[:, : 18 * LANES], 18 * LANES - CELLS, axis=1)
    tail = turned[:, :LANES]
    for n in range(18):
        block = 17 - n
        flat[:, LANES * n : LANES * (n + 1)] = exact(
            turned[:, LANES * block : LANES * (block + 1)], flips(), NN
        )
    sides[...] = jnp.zeros_like(sides)
    for b in range(SPAN):
        base = 24 * b // LANES * LANES
        part = moved_window(flat, SPAN * b, 24 * b)
        sides[b % 2, :, base : base + 2 * LANES] += part
    lane = lax.broadcasted_iota(jnp.int32, (16, LANES), 1)
    sides[0, :, 1152:1280] = jnp.where(lane < 3, tail, 0.0)
    for head in range(heads):
        for par in range(2):
            strips_out[head, par : par + 1, :] = sides[par, head : head + 1, :]


def pack_kernel(place, strip0, strip1, strip2, ffn, fc1_bias, last, result, packed):
    packed[...] = jnp.zeros_like(packed)
    for n in range(5):
        lanes = slice(256 * n, 256 * n + 256)
        for pair, strip in enumerate((strip0, strip1, strip2)):
            for head in range(2):
                for par in range(2):
                    row = 16 * n + 6 * par + 2 * pair + head
                    packed[row : row + 1, :] = strip[0, head, par : par + 1, lanes]
    for n in range(3):
        lanes = slice(256 * n, 256 * n + 256)
        row = 80 + 16 * n
        packed[row : row + 5, :] = ffn[0:5, lanes]
        packed[row + 5 : row + 6, :] = result[0:1, lanes]
        packed[row + 6 : row + 9, :] = last[0:3, lanes]
        for part in range(4):
            packed[row + 9 + part : row + 10 + part, :] = fc1_bias[
                :, 768 * part + 256 * n : 768 * part + 256 * n + 256
            ]


def unpack_kernel(
    place, packed, mate, table_out, norm2_gain, norm2_bias, scale1, proj_bias, fc2_bias, scale2,
    norm1_gain, norm1_bias, query_bias, value_bias, fc1_bias, flat, sides,
):
    heads = table_out.shape[0]
    half = heads // 2
    left = place[0] == 0
    flat[...] = jnp.zeros_like(flat)
    for n in range(5):
        lanes = slice(256 * n, 256 * n + 256)
        for par in range(2):
            rows = slice(16 * n + half * par, 16 * n + half * par + half)
            mine = packed[rows, :]
            theirs = mate[rows, :]
            sides[par, 0:half, lanes] = jnp.where(left, mine, theirs)
            sides[par, half:heads, lanes] = jnp.where(left, theirs, mine)
    for b in range(SPAN):
        target = SPAN * b
        base = target // LANES * LANES
        part = moved_window(sides.at[b % 2], 24 * b, target)
        flat[:, base : base + 2 * LANES] += part
    lane = lax.broadcasted_iota(jnp.int32, (16, LANES), 1)
    blocks = [
        exact(flat[:, LANES * (17 - n) : LANES * (18 - n)], flips(), NN) for n in range(18)
    ]
    blocks[0] = jnp.where(lane < 3, sides[0, :, 1152:1280], blocks[0])
    turned = pltpu.roll(jnp.concatenate(blocks, axis=1), CELLS, axis=1)
    table_out[...] = turned[:heads, : CELLS + 3]
    outs = (norm2_gain, norm2_bias, scale1, proj_bias, fc2_bias, scale2, norm1_gain, norm1_bias)
    for n in range(3):
        lanes = slice(256 * n, 256 * n + 256)
        for at, out in enumerate(outs):
            row = 80 + 16 * n + at
            out[lanes] = (packed[row : row + 1, :] + mate[row : row + 1, :]).reshape(256)
        for part in range(4):
            row = 89 + 16 * n + part
            fc1_bias[768 * part + 256 * n : 768 * part + 256 * n + 256] = (
                packed[row : row + 1, :] + mate[row : row + 1, :]
            ).reshape(256)
    for source, side in ((packed, place[0]), (mate, 1 - place[0])):
        line = jnp.concatenate([source[88 + 16 * n : 89 + 16 * n, :] for n in range(3)], axis=1)
        lanes = pl.ds(pl.multiple_of(side * 384, LANES), 384)
        query_bias[lanes] = line[:, :384].reshape(384)
        value_bias[lanes] = line[:, 384:].reshape(384)


def even_places():
    lane = np.arange(STRIP_WIDTH)[None, :]
    row = np.arange(STRIP)[:, None]
    turn = (lane - 1) // STRIP
    return np.where(row == 0, turn % 2 == 0, turn % 2 == 1).astype(np.float32)


def split_body(
    tokens,
    masked,
    out_grad,
    norm1_gain,
    norm1_bias,
    qkv_weight,
    query_bias,
    value_bias,
    rel_table,
    proj_weight,
    proj_bias,
    scale1,
    norm2_gain,
    norm2_bias,
    fc1_weight,
    fc1_bias,
    fc2_weight,
    fc2_bias,
    scale2,
):
    _, rows, width = tokens.shape
    slots = 2 * rows
    heads = rel_table.shape[1] // 2
    pairs = heads // 2
    share = width // 2
    hidden = fc1_weight.shape[1]
    seq = lax.axis_index("seq")
    img = lax.axis_index("img")
    core = img & 1
    line = img >> 2
    x_bit = (img >> 1) & 1
    place = jnp.stack(
        [
            seq,
            core,
            rest_label(ORDER_A)(x_bit, line, seq),
            rest_label(ORDER_B)(x_bit, line, seq),
            rest_label(ORDER_Q)(x_bit, line, seq),
        ]
    ).astype(jnp.int32)
    own = tokens.reshape(rows, width)
    other = swapped(own, "y")
    cot = (out_grad.astype(F32) * masked.astype(F32)[..., None]).astype(BF).reshape(rows, width)
    vecs = jnp.stack(
        [norm1_gain, norm1_bias, proj_bias, scale1, norm2_gain, norm2_bias, fc2_bias, scale2]
    )
    strips = run(
        strips_kernel, place, (1,), [full(rel_table.shape[::-1])], [full((2 * heads, 2, STRIP_WIDTH))],
        [shape((2 * heads, 2, STRIP_WIDTH), F32)],
        [pltpu.VMEM((16, 2432), F32), pltpu.VMEM((2, 16, STRIP_WIDTH), F32)], (rel_table.T,), 0,
    )[0]
    even_mask = jnp.asarray(even_places())

    qkv, hidden1 = run(
        qkv_kernel, place, (3,),
        [
            full((rows, width)), full((rows, width)), full((8, width)),
            spec((width, share), lambda t, p: (0, 2 * t + p[0])),
            spec((1, share), lambda t, p: (0, p[0])), spec((1, share), lambda t, p: (0, p[0])),
        ],
        [spec((1, slots, share), lambda t, p: (t, 0, 0)), full((slots, width))],
        [shape((3, slots, share), BF), shape((slots, width), BF)],
        [],
        (own, other, vecs, qkv_weight, query_bias.reshape(1, width), value_bias.reshape(1, width)),
        2 * slots * width * 3 * share,
    )
    pair_rows = spec((slots, LANES), lambda n, p: (0, n))
    pair_half = spec((rows, LANES), lambda n, p: (0, n))
    pair_qkv = spec((3, slots, LANES), lambda n, p: (0, 0, n))
    pair_expo = spec((2, slots, slots), lambda n, p: (n, 0, 0))
    attn_own, attn_send, expo, inv = run(
        attend_kernel, place, (pairs,),
        [pair_qkv, full((2 * heads, 2, STRIP_WIDTH)), full((STRIP, STRIP_WIDTH))],
        [pair_half, pair_half, pair_expo, pair_rows],
        [
            shape((rows, share), BF), shape((rows, share), BF),
            shape((heads, slots, slots), BF), shape((slots, share), F32),
        ],
        [pltpu.VMEM((2, STRIP, STRIP_WIDTH), F32), pltpu.VMEM((slots, LANES), F32)],
        (qkv, strips, even_mask),
        16 * slots * slots * 64 * heads,
    )
    attn_other = swapped(attn_send, "y")
    parts = 4
    part = hidden // parts
    whole = full((rows, width))
    sliced = spec((rows, part), lambda c, p: (0, c))
    (
        act, d_pre, fc1_bias_part, hidden2, resid, d_ffn, attn_low, d_mixed, d_resid,
        grad_own, grad_send, small_ffn,
    ) = run(
        ffn_kernel, place, (parts,),
        [
            whole, whole, full((rows, share)), full((rows, share)), full((8, width)),
            full((width, width)), spec((width, part), lambda c, p: (0, c)),
            spec((1, part), lambda c, p: (0, c)), spec((part, width), lambda c, p: (c, 0)),
            spec((share, width), lambda c, p: (p[0], 0)), spec((share, width), lambda c, p: (1 - p[0], 0)),
        ],
        [
            sliced, sliced, spec((1, part), lambda c, p: (0, c)), whole, whole, whole, whole, whole, whole,
            full((rows, share)), full((rows, share)), full((8, width)),
        ],
        [
            shape((rows, hidden), BF), shape((rows, hidden), BF), shape((1, hidden), F32),
            shape((rows, width), BF), shape((rows, width), F32), shape((rows, width), BF),
            shape((rows, width), BF), shape((rows, width), BF), shape((rows, width), F32),
            shape((rows, share), BF), shape((rows, share), BF), shape((8, width), F32),
        ],
        [pltpu.VMEM((rows, width), F32), pltpu.VMEM((rows, width), F32)],
        (
            own, cot, attn_own, attn_other, vecs, proj_weight, fc1_weight, fc1_bias.reshape(1, hidden),
            fc2_weight, proj_weight, proj_weight,
        ),
        2 * rows * width * (3 * hidden + 2 * width),
    )
    grad_other = swapped(grad_send, "y")
    block = (16, 240, share)
    keep_a, send_a = run(
        functools.partial(fc2_grad_kernel, rest=rest_label(ORDER_A)), place, (parts,),
        [sliced, whole, whole, whole], [full(block), full(block)],
        [shape(block, BF), shape(block, BF)],
        [pltpu.VMEM((part, width), F32)], (act, d_ffn, attn_low, d_mixed),
        2 * rows * width * hidden,
        after=(grad_send,),
    )
    terms_a = [keep_a, swapped(send_a, "core")]
    block = (16, 48, 4 * share)
    keep_b, send_b = run(
        functools.partial(fc1_grad_kernel, rest=rest_label(ORDER_B)), place, (parts,),
        [whole, sliced], [full(block), full(block)],
        [shape(block, BF), shape(block, BF)],
        [pltpu.VMEM((width, part), F32)], (hidden2, d_pre),
        2 * rows * width * (hidden + width), after=(send_a,),
    )
    terms_b = [keep_b, swapped(send_b, "core")]

    out_a1 = half_out(place, terms_a, (send_b,))
    terms_a = [rest_of(place, terms_a, (out_a1,)), swapped(out_a1, ORDER_A[1])]

    def attend_back(pair, after):
        pair_expo = spec((2, slots, slots), lambda n, p: (pair, 0, 0))
        pair_rows = spec((slots, LANES), lambda n, p: (0, pair))
        pair_half = spec((rows, LANES), lambda n, p: (0, pair))
        return run(
            attend_back_kernel, place, (1,),
            [
                spec((3, slots, LANES), lambda n, p: (0, 0, pair)), pair_expo, pair_half, pair_half,
                pair_half, pair_half, pair_rows, full((STRIP, STRIP_WIDTH)),
            ],
            [full((3, slots, LANES)), full((1, 2, 2, STRIP_WIDTH))],
            [shape((3, slots, LANES), BF), shape((1, 2, 2, STRIP_WIDTH), F32)],
            [
                pltpu.VMEM((slots, LANES), F32), pltpu.VMEM((slots, LANES), F32),
                pltpu.VMEM((2, slots, slots), BF), pltpu.VMEM((2, STRIP, STRIP_WIDTH), F32),
                pltpu.VMEM((slots, LANES), F32),
            ],
            (qkv, expo, attn_own, attn_send, grad_own, grad_other, inv, even_mask),
            32 * slots * slots * 64 * 2, after=after, us=40.0 if pair == 0 else None,
        )

    dqkv0, strip0 = attend_back(0, (out_a1, terms_a[0]))
    out_b1 = half_out(place, terms_b, (dqkv0,))
    terms_b = [rest_of(place, terms_b, (out_b1,)), swapped(out_b1, ORDER_B[1])]
    dqkv1, strip1 = attend_back(1, (dqkv0, out_b1, terms_b[0]))
    dqkv2, strip2 = attend_back(2, (dqkv1,))
    dqkv = (dqkv0, dqkv1, dqkv2)
    third = [spec((1, slots, LANES), lambda t, p: (t, 0, 0))] * 3
    dh_keep, dh_send, small_last = run(
        hidden1_grad_kernel, place, (3,),
        [*third, spec((width, share), lambda t, p: (0, 2 * t + p[0])), whole, whole],
        [whole, whole, full((8, width))],
        [shape((rows, width), F32), shape((rows, width), BF), shape((8, width), F32)],
        [pltpu.VMEM((slots, width), F32), pltpu.VMEM((slots, share), BF)], (*dqkv, qkv_weight, own, other),
        2 * slots * width * 3 * share,
    )
    block = (8, 48, 3 * share)
    keep_q, send_q = run(
        functools.partial(qkv_grad_kernel, rest=rest_label(ORDER_Q)), place, (3,),
        [full((slots, width)), *third], [full(block), full(block)],
        [shape(block, BF), shape(block, BF)],
        [pltpu.VMEM((width, share), F32), pltpu.VMEM((slots, share), BF)], (hidden1, *dqkv), 2 * slots * width * 3 * share,
        after=(dh_send,),
    )
    terms_q = [keep_q, swapped(send_q, "core")]
    result, small_result = run(
        result_kernel, place, (parts,),
        [sliced, spec((part, width), lambda c, p: (c, 0)), whole, whole, full((8, width))],
        [whole, full((8, width))],
        [shape((rows, width), BF), shape((8, width), F32)],
        [pltpu.VMEM((rows, width), F32)], (act, fc2_weight, resid, cot, vecs),
        2 * rows * width * hidden, after=(send_q,),
    )
    packed = run(
        pack_kernel, place, (1,),
        [*[full((1, 2, 2, STRIP_WIDTH))] * 3, full((8, width)), full((1, hidden)), full((8, width)), full((8, width))],
        [full((128, 256))], [shape((128, 256), F32)], [],
        (strip0, strip1, strip2, small_ffn, fc1_bias_part, small_last, small_result), 0,
    )[0]
    out_a2 = half_out(place, terms_a, (packed,))
    terms_a = [*terms_a, swapped(out_a2, "z1")]
    out_b2 = half_out(place, terms_b, (out_a2,))
    terms_b = [*terms_b, swapped(out_b2, "x")]
    out_q1 = half_out(place, terms_q, (out_b2,))
    terms_q = [*terms_q, swapped(out_q1, "x")]
    mate = swapped(packed, "core")
    dh_recv = swapped(dh_send, "y")
    out_a3 = half_out(place, terms_a, (out_q1,))
    terms_a = [*terms_a, swapped(out_a3, "z2")]
    out_b3 = half_out(place, terms_b, (out_a3,))
    terms_b = [*terms_b, swapped(out_b3, "z1")]
    out_q2 = half_out(place, terms_q, (out_b3,))
    terms_q = [*terms_q, swapped(out_q2, "z1")]
    packed = summed(place, packed, mate, (out_q2,))
    mate = swapped(packed, "x")
    tokens_grad = run(
        tokens_grad_kernel, place, (1,),
        [whole, whole, whole, whole, full((8, width))], [whole],
        [shape((rows, width), BF)], [], (dh_keep, dh_recv, own, d_resid, vecs), 0,
        after=(packed,),
    )[0]
    packed = summed(place, packed, mate, (tokens_grad,))
    mate = swapped(packed, "z1")
    out_a4 = half_out(place, terms_a, (packed,))
    terms_a = [*terms_a, swapped(out_a4, "y")]
    out_b4 = half_out(place, terms_b, (out_a4,))
    terms_b = [*terms_b, swapped(out_b4, "z2")]
    out_q3 = half_out(place, terms_q, (out_b4,))
    terms_q = [*terms_q, swapped(out_q3, "z2")]
    packed = summed(place, packed, mate, (out_q3,))
    mate = swapped(packed, "z2")
    packed = summed(place, packed, mate)
    mate = swapped(packed, "y")
    fc2_proj = added(terms_a)
    fc1_grad = added(terms_b)
    qkv_part = added(terms_q)
    fc2_grad = fc2_proj[:192]
    proj_grad = fc2_proj[192:]
    on_left = seq == 0
    given = jnp.where(on_left, qkv_part[:, 2 * share :], qkv_part[:, :share]).astype(BF)
    taken = swapped(given, "y").astype(F32)
    qkv_grad = jnp.where(
        on_left,
        jnp.concatenate([qkv_part[:, :share], taken, qkv_part[:, share : 2 * share]], axis=1),
        jnp.concatenate([qkv_part[:, share : 2 * share], taken, qkv_part[:, 2 * share :]], axis=1),
    )

    vector = shape((width,), F32)
    table_grad, *small = run(
        unpack_kernel, place, (1,), [full((128, 256))] * 2,
        [full(rel_table.shape[::-1]), *[full((width,))] * 10, full((hidden,))],
        [shape(rel_table.shape[::-1], F32), *[vector] * 10, shape((hidden,), F32)],
        [pltpu.VMEM((16, 2432), F32), pltpu.VMEM((2, 16, STRIP_WIDTH), F32)], (packed, mate), 0,
    )
    return (
        result.reshape(tokens.shape),
        tokens_grad.reshape(tokens.shape),
        small[6],
        small[7],
        qkv_grad,
        small[8],
        small[9],
        table_grad.T,
        proj_grad,
        small[3],
        small[2],
        small[0],
        small[1],
        fc1_grad,
        small[10],
        fc2_grad,
        small[4],
        small[5],
    )


def solution(mesh):
    in_specs = (
        P("img", "seq", None),
        P("img", "seq"),
        P("img", "seq", None),
        P(),
        P(),
        P(),
        P(),
        P(),
        P(),
        P(),
        P(),
        P(),
        P(),
        P(),
        P(),
        P(),
        P(),
        P(),
        P(),
    )
    out_specs = (
        P("img", "seq", None),
        P("img", "seq", None),
        P(),
        P(),
        P("img", "seq"),
        P(),
        P(),
        P(),
        P("img", "seq"),
        P(),
        P(),
        P(),
        P(),
        P("img", "seq"),
        P(),
        P("img", "seq"),
        P(),
        P(),
    )
    sizes = dict(mesh.shape)
    body = split_body if (sizes["img"], sizes["seq"]) == (16, 2) else general_body
    return jax.shard_map(body, mesh=mesh, in_specs=in_specs, out_specs=out_specs, check_vma=False)
```

```python
import functools

import jax
import jax.numpy as jnp
import numpy as np
from jax import lax
from jax.experimental import pallas as pl
from jax.experimental.pallas import tpu as pltpu
from jax.sharding import PartitionSpec as P

GRID = 24


EPSILON = 1e-06
NEGATIVE = -1e30
ROOT_HALF = 0.7071067811865476
GAUSS_NORM = 0.3989422804014327


def passed_along(value, axis, steps):
    count = lax.axis_size(axis)
    pairs = [(source, (source + steps) % count) for source in range(count)]
    return lax.ppermute(value, axis, pairs)


def gap_onehot():
    span_width = 2 * GRID - 1
    grid_ids = jnp.arange(GRID, dtype=jnp.int32)
    gaps = grid_ids[:, None, None] - grid_ids[None, :, None] + GRID - 1
    return (gaps == jnp.arange(span_width, dtype=jnp.int32)[None, None, :]).astype(jnp.float32)


def bias_full(rel_table, all_slots):
    highest = lax.Precision.HIGHEST
    span_width = 2 * GRID - 1
    far_index = span_width * span_width
    cells = GRID * GRID
    head_count = rel_table.shape[1]
    spare = all_slots - 1 - cells
    selector = gap_onehot()
    patch_table = rel_table[0:far_index].reshape(span_width, span_width, head_count)
    row_pick = jnp.einsum("pqa,abh->pqbh", selector, patch_table, precision=highest)
    spread = jnp.einsum("pqbh,rsb->hprqs", row_pick, selector, precision=highest)
    patch_bias = spread.reshape(head_count, cells, cells)
    patch_bias = jnp.concatenate(
        [
            patch_bias,
            jnp.broadcast_to(patch_bias[:, cells - 1 : cells, :], (head_count, spare, cells)),
        ],
        axis=1,
    )
    patch_bias = jnp.concatenate(
        [
            patch_bias,
            jnp.broadcast_to(
                patch_bias[:, :, cells - 1 : cells], (head_count, cells + spare, spare)
            ),
        ],
        axis=2,
    )
    top_row = jnp.broadcast_to(rel_table[far_index][:, None, None], (head_count, 1, all_slots - 1))
    left_col = jnp.broadcast_to(
        rel_table[far_index + 1][:, None, None], (head_count, all_slots - 1, 1)
    )
    corner = rel_table[far_index + 2][:, None, None]
    upper = jnp.concatenate([corner, top_row], axis=2)
    lower = jnp.concatenate([left_col, patch_bias], axis=2)
    return jnp.concatenate([upper, lower], axis=1)


def table_back(grad_full):
    highest = lax.Precision.HIGHEST
    span_width = 2 * GRID - 1
    cells = GRID * GRID
    head_count = grad_full.shape[0]
    corner = grad_full[:, 0, 0]
    far_grad = jnp.sum(grad_full[:, 0, 1:], axis=1)
    near_grad = jnp.sum(grad_full[:, 1:, 0], axis=1)
    patch_grad = grad_full[:, 1:, 1:]
    patch_grad = jnp.concatenate(
        [
            patch_grad[:, 0 : cells - 1, :],
            jnp.sum(patch_grad[:, cells - 1 :, :], axis=1, keepdims=True),
        ],
        axis=1,
    )
    patch_grad = jnp.concatenate(
        [
            patch_grad[:, :, 0 : cells - 1],
            jnp.sum(patch_grad[:, :, cells - 1 :], axis=2, keepdims=True),
        ],
        axis=2,
    )
    selector = gap_onehot()
    spread = patch_grad.reshape(head_count, GRID, GRID, GRID, GRID)
    row_sums = jnp.einsum("hprqs,rsb->pqbh", spread, selector, precision=highest)
    patch_table = jnp.einsum("pqa,pqbh->abh", selector, row_sums, precision=highest)
    tail = jnp.stack([far_grad, near_grad, corner], axis=0)
    return jnp.concatenate([patch_table.reshape(span_width * span_width, head_count), tail], axis=0)


def gelu_value(argument):
    return 0.5 * argument * (1.0 + lax.erf(argument * ROOT_HALF))


def gelu_slope(argument):
    return (
        0.5 * (1.0 + lax.erf(argument * ROOT_HALF))
        + argument * jnp.exp(-0.5 * argument * argument) * GAUSS_NORM
    )


def normalize(values, gain, shift):
    center = values - jnp.mean(values, axis=-1, keepdims=True)
    inverse = lax.rsqrt(jnp.mean(center * center, axis=-1, keepdims=True) + EPSILON)
    normed = center * inverse
    return (normed * gain + shift, normed, inverse)


def normalize_back(grad_out, normed, inverse, gain):
    signal = grad_out * gain
    inner = (
        signal
        - jnp.mean(signal, axis=-1, keepdims=True)
        - normed * jnp.mean(signal * normed, axis=-1, keepdims=True)
    )
    return (inverse * inner, jnp.sum(grad_out * normed, axis=0), jnp.sum(grad_out, axis=0))


def general_body(
    tokens,
    masked,
    out_grad,
    norm1_gain,
    norm1_bias,
    qkv_weight,
    query_bias,
    value_bias,
    rel_table,
    proj_weight,
    proj_bias,
    scale1,
    norm2_gain,
    norm2_bias,
    fc1_weight,
    fc1_bias,
    fc2_weight,
    fc2_bias,
    scale2,
):
    images, local_rows, model_width = tokens.shape
    head_count = rel_table.shape[1]
    head_size = model_width // head_count
    head_scale = head_size ** (-0.5)
    cycle_size = lax.axis_size("seq")
    position = lax.axis_index("seq")
    all_slots = local_rows * cycle_size
    key_pos = jnp.arange(all_slots, dtype=jnp.int32)
    position_bias = lax.dynamic_slice_in_dim(
        bias_full(rel_table, all_slots), position * local_rows, local_rows, 1
    )
    key_valid = key_pos <= GRID * GRID
    flat_rows = images * local_rows
    head_shape = (images, local_rows, head_count, head_size)
    inputs = tokens.astype(jnp.float32).reshape(flat_rows, model_width)
    normed1, centred1, inverse1 = normalize(inputs, norm1_gain, norm1_bias)
    hidden1 = normed1.astype(jnp.bfloat16)
    projected = jnp.dot(hidden1, qkv_weight, preferred_element_type=jnp.float32)
    queries = ((projected[:, 0:model_width] + query_bias) * head_scale).astype(jnp.bfloat16)
    keys_local = (
        projected[:, model_width : 2 * model_width]
        .astype(jnp.bfloat16)
        .reshape(images, local_rows, model_width)
    )
    values_local = (
        (projected[:, 2 * model_width :] + value_bias)
        .astype(jnp.bfloat16)
        .reshape(images, local_rows, model_width)
    )
    query_heads = queries.reshape(head_shape)

    def block_scores(key_block, offset):
        key_count = key_block.shape[1]
        key_heads = key_block.reshape(images, key_count, head_count, head_size)
        logits = jnp.einsum(
            "gqhd,gkhd->ghqk", query_heads, key_heads, preferred_element_type=jnp.float32
        )
        logits = logits + lax.dynamic_slice_in_dim(position_bias, offset, key_count, 2)[None]
        usable = lax.dynamic_slice_in_dim(key_valid, offset, key_count, 0)
        return (jnp.where(usable, logits, NEGATIVE), usable)

    row_max = jnp.full((images, head_count, local_rows), NEGATIVE, jnp.float32)
    key_block = lax.all_gather(keys_local, "seq", axis=1, tiled=True)
    value_block = lax.all_gather(values_local, "seq", axis=1, tiled=True)
    key_count = key_block.shape[1]
    scores, usable = block_scores(key_block, jnp.int32(0))
    new_max = jnp.maximum(row_max, jnp.max(scores, axis=-1))
    weights = jnp.where(usable, jnp.exp(scores - new_max[..., None]), 0.0)
    totals = jnp.sum(weights, axis=-1)
    value_heads = value_block.reshape(images, key_count, head_count, head_size)
    update = jnp.einsum(
        "ghqk,gkhd->gqhd",
        weights.astype(jnp.bfloat16),
        value_heads,
        preferred_element_type=jnp.float32,
    )
    weighted = update
    row_max, totals, weighted = (new_max, totals, weighted)
    log_total = row_max + jnp.log(totals)
    attended = weighted / jnp.transpose(totals, (0, 2, 1))[..., None]
    attn_low = attended.reshape(flat_rows, model_width).astype(jnp.bfloat16)
    mixed_out = jnp.dot(attn_low, proj_weight, preferred_element_type=jnp.float32) + proj_bias
    residual1 = inputs + scale1 * mixed_out
    normed2, centred2, inverse2 = normalize(residual1, norm2_gain, norm2_bias)
    hidden2 = normed2.astype(jnp.bfloat16)
    pre_act = jnp.dot(hidden2, fc1_weight, preferred_element_type=jnp.float32) + fc1_bias
    activated = gelu_value(pre_act).astype(jnp.bfloat16)
    ffn_out = jnp.dot(activated, fc2_weight, preferred_element_type=jnp.float32) + fc2_bias
    result = (residual1 + scale2 * ffn_out).astype(jnp.bfloat16).reshape(tokens.shape)
    cotangent = (out_grad.astype(jnp.float32) * masked.astype(jnp.float32)[..., None]).reshape(
        flat_rows, model_width
    )
    d_ffn = (scale2 * cotangent).astype(jnp.bfloat16)
    scale2_grad = jnp.sum(cotangent * ffn_out, axis=0)
    fc2_bias_grad = jnp.sum(d_ffn.astype(jnp.float32), axis=0)
    fc2_weight_grad = jnp.einsum("nf,nd->fd", activated, d_ffn, preferred_element_type=jnp.float32)
    d_act = jnp.einsum("nd,fd->nf", d_ffn, fc2_weight, preferred_element_type=jnp.float32)
    d_pre = (d_act * gelu_slope(pre_act)).astype(jnp.bfloat16)
    fc1_bias_grad = jnp.sum(d_pre.astype(jnp.float32), axis=0)
    fc1_weight_grad = jnp.einsum("nd,nf->df", hidden2, d_pre, preferred_element_type=jnp.float32)
    d_hidden2 = jnp.einsum("nf,df->nd", d_pre, fc1_weight, preferred_element_type=jnp.float32)
    back_two, norm2_gain_grad, norm2_bias_grad = normalize_back(
        d_hidden2, centred2, inverse2, norm2_gain
    )
    d_resid1 = cotangent + back_two
    d_mixed = (scale1 * d_resid1).astype(jnp.bfloat16)
    scale1_grad = jnp.sum(d_resid1 * mixed_out, axis=0)
    proj_bias_grad = jnp.sum(d_mixed.astype(jnp.float32), axis=0)
    proj_weight_grad = jnp.einsum(
        "nc,nd->cd", attn_low, d_mixed, preferred_element_type=jnp.float32
    )
    d_attn = jnp.einsum(
        "nd,cd->nc", d_mixed, proj_weight, preferred_element_type=jnp.float32
    ).astype(jnp.bfloat16)
    d_attn_heads = d_attn.reshape(head_shape)
    row_delta = jnp.transpose(
        jnp.sum(d_attn_heads.astype(jnp.float32) * attended, axis=-1), (0, 2, 1)
    )

    def back_block(key_block, value_block, offset):
        key_count = key_block.shape[1]
        scores, usable = block_scores(key_block, offset)
        prob_full = jnp.where(usable, jnp.exp(scores - log_total[..., None]), 0.0)
        prob_low = prob_full.astype(jnp.bfloat16)
        key_heads = key_block.reshape(images, key_count, head_count, head_size)
        value_heads = value_block.reshape(images, key_count, head_count, head_size)
        d_value = jnp.einsum(
            "ghqk,gqhd->gkhd", prob_low, d_attn_heads, preferred_element_type=jnp.float32
        )
        d_probs = jnp.einsum(
            "gqhd,gkhd->ghqk", d_attn_heads, value_heads, preferred_element_type=jnp.float32
        )
        d_scores = (prob_full * (d_probs - row_delta[..., None])).astype(jnp.bfloat16)
        d_query = jnp.einsum(
            "ghqk,gkhd->gqhd", d_scores, key_heads, preferred_element_type=jnp.float32
        )
        d_key = jnp.einsum(
            "ghqk,gqhd->gkhd", d_scores, query_heads, preferred_element_type=jnp.float32
        )
        table_part = jnp.sum(d_scores.astype(jnp.float32), axis=0)
        return (
            d_query,
            d_key.reshape(images, key_count, model_width),
            d_value.reshape(images, key_count, model_width),
            table_part,
        )

    def turn_grads(grad_pair):
        return (
            passed_along(grad_pair[0].astype(jnp.bfloat16), "seq", 1).astype(jnp.float32),
            passed_along(grad_pair[1].astype(jnp.bfloat16), "seq", 1).astype(jnp.float32),
        )

    def cycle_step(turn_index, cycle_state):
        key_block, value_block, d_key_acc, d_value_acc, d_query_acc, table_acc = cycle_state
        owner_rank = (position - turn_index) % cycle_size
        offset = owner_rank * local_rows
        d_query, d_key, d_value, table_part = back_block(key_block, value_block, offset)
        table_acc = lax.dynamic_update_slice_in_dim(table_acc, table_part, offset, 2)
        d_key_acc, d_value_acc = turn_grads((d_key_acc + d_key, d_value_acc + d_value))
        key_block, value_block = passed_along((key_block, value_block), "seq", 1)
        return (key_block, value_block, d_key_acc, d_value_acc, d_query_acc + d_query, table_acc)

    kv_zeros = jnp.zeros((images, local_rows, model_width), jnp.float32)
    initial = (
        keys_local,
        values_local,
        kv_zeros,
        kv_zeros,
        jnp.zeros(head_shape, jnp.float32),
        jnp.zeros((head_count, local_rows, all_slots), jnp.float32),
    )
    cycle_state = lax.fori_loop(0, cycle_size - 1, cycle_step, initial)
    key_block, value_block, d_key_acc, d_value_acc, d_query_acc, table_acc = cycle_state
    offset = (position + 1) % cycle_size * local_rows
    d_query, d_key, d_value, table_part = back_block(key_block, value_block, offset)
    table_acc = lax.dynamic_update_slice_in_dim(table_acc, table_part, offset, 2)
    d_key_all, d_value_all = turn_grads((d_key_acc + d_key, d_value_acc + d_value))
    d_query_all = d_query_acc + d_query
    d_query_low = d_query_all.reshape(flat_rows, model_width).astype(jnp.bfloat16) * head_scale
    d_key_low = d_key_all.reshape(flat_rows, model_width).astype(jnp.bfloat16)
    d_value_low = d_value_all.reshape(flat_rows, model_width).astype(jnp.bfloat16)
    d_qkv = jnp.concatenate([d_query_low, d_key_low, d_value_low], axis=1)
    qkv_weight_grad = jnp.einsum("nd,ne->de", hidden1, d_qkv, preferred_element_type=jnp.float32)
    query_bias_grad = jnp.sum(d_query_low.astype(jnp.float32), axis=0)
    value_bias_grad = jnp.sum(d_value_low.astype(jnp.float32), axis=0)
    d_hidden1 = jnp.einsum("ne,de->nd", d_qkv, qkv_weight, preferred_element_type=jnp.float32)
    back_one, norm1_gain_grad, norm1_bias_grad = normalize_back(
        d_hidden1, centred1, inverse1, norm1_gain
    )
    tokens_grad = (d_resid1 + back_one).astype(jnp.bfloat16).reshape(tokens.shape)
    grad_square = lax.dynamic_update_slice_in_dim(
        jnp.zeros((head_count, all_slots, all_slots), jnp.float32),
        table_acc,
        position * local_rows,
        1,
    )
    table_grad = table_back(grad_square)
    half_summed = (
        lax.psum_scatter(
            qkv_weight_grad.astype(jnp.bfloat16), "img", scatter_dimension=0, tiled=True
        ).astype(jnp.float32),
        lax.psum_scatter(
            proj_weight_grad.astype(jnp.bfloat16), "img", scatter_dimension=0, tiled=True
        ).astype(jnp.float32),
        lax.psum_scatter(
            fc1_weight_grad.astype(jnp.bfloat16), "img", scatter_dimension=0, tiled=True
        ).astype(jnp.float32),
        lax.psum_scatter(
            fc2_weight_grad.astype(jnp.bfloat16), "img", scatter_dimension=0, tiled=True
        ).astype(jnp.float32),
    )
    summed = (
        lax.psum_scatter(
            half_summed[0].astype(jnp.bfloat16), "seq", scatter_dimension=1, tiled=True
        ).astype(jnp.float32),
        lax.psum_scatter(
            half_summed[1].astype(jnp.bfloat16), "seq", scatter_dimension=1, tiled=True
        ).astype(jnp.float32),
        lax.psum_scatter(
            half_summed[2].astype(jnp.bfloat16), "seq", scatter_dimension=1, tiled=True
        ).astype(jnp.float32),
        lax.psum_scatter(
            half_summed[3].astype(jnp.bfloat16), "seq", scatter_dimension=1, tiled=True
        ).astype(jnp.float32),
    )
    smalls = lax.psum(
        (
            table_grad,
            norm1_gain_grad,
            norm1_bias_grad,
            query_bias_grad,
            value_bias_grad,
            proj_bias_grad,
            scale1_grad,
            norm2_gain_grad,
            norm2_bias_grad,
            fc1_bias_grad,
            fc2_bias_grad,
            scale2_grad,
        ),
        ("img", "seq"),
    )
    return (
        result,
        tokens_grad,
        smalls[1],
        smalls[2],
        summed[0],
        smalls[3],
        smalls[4],
        smalls[0],
        summed[1],
        smalls[5],
        smalls[6],
        smalls[7],
        smalls[8],
        summed[2],
        smalls[9],
        summed[3],
        smalls[10],
        smalls[11],
    )


LANES = 128
RATE = 1.15e9
STRIP = 24
STRIP_WIDTH = 1280
MEGA = 1 << 20
NT = (((1,), (1,)), ((), ()))
TN = (((0,), (0,)), ((), ()))
NN = (((1,), (0,)), ((), ()))
BF = jnp.bfloat16
F32 = jnp.float32


def mul(left, right, dims=NN):
    return lax.dot_general(left, right, dims, preferred_element_type=F32)


def bits_of(img, seq):
    line = img >> 2
    return {"core": img & 1, "x": (img >> 1) & 1, "z1": line & 1, "z2": line >> 1, "y": seq}


def label_of(img, seq, order):
    bits = bits_of(img, seq)
    total = 0
    for name in order:
        total = total * 2 + bits[name]
    return total


def swap_pairs(*names):
    order = ("core", "x", "z1", "z2", "y")
    where = {label_of(img, seq, order): img * 2 + seq for img in range(16) for seq in range(2)}
    flip = sum(1 << (len(order) - 1 - order.index(name)) for name in names)
    return [(device, where[label ^ flip]) for label, device in where.items()]


def swapped(value, *names):
    return lax.ppermute(value, ("img", "seq"), swap_pairs(*names))


def added(terms):
    return sum(term[0].astype(F32) for term in terms)


def layer_norm(values):
    center = values - jnp.mean(values, axis=-1, keepdims=True)
    inverse = lax.rsqrt(jnp.mean(center * center, axis=-1, keepdims=True) + EPSILON)
    return center * inverse, inverse


def layer_norm_back(grad_out, normed, inverse, gain):
    signal = grad_out * gain
    return inverse * (
        signal
        - jnp.mean(signal, axis=-1, keepdims=True)
        - normed * jnp.mean(signal * normed, axis=-1, keepdims=True)
    )


def spec(block, index):
    return pl.BlockSpec(block, index)


def full(shape):
    zeros = (0,) * len(shape)
    return pl.BlockSpec(shape, lambda *_: zeros, pipeline_mode=pl.Buffered(1))


SIZES = {
    "strips_kernel": (1.7, 5),
    "qkv_kernel": (1.9, 10),
    "attend_kernel": (9.0, 15),
    "ffn_kernel": (5.5, 16),
    "ffn_back_kernel": (4.5, 14),
    "d_act_kernel": (2.5, 12),
    "fc2_grad_kernel": (4.6, 14),
    "fc1_grad_kernel": (5.5, 14),
    "attend_back_kernel": (4.4, 14),
    "hidden1_grad_kernel": (4.2, 12),
    "qkv_grad_kernel": (3.2, 12),
    "result_kernel": (40.0, 10),
    "tokens_grad_kernel": (2.0, 10),
}


def run(kernel, place, grid, in_specs, out_specs, out_shapes, scratch, operands, flops, after=(), us=None, reuse=()):
    held = len(operands)
    inner = kernel
    cost, vmem = SIZES.get(getattr(kernel, "func", kernel).__name__, (0.01, 10))
    us = us or cost

    def kernel(place_ref, *refs):
        inner(place_ref, *refs[:held], *refs[held + len(after) :])

    in_specs = [*in_specs, *[pl.BlockSpec(memory_space=pl.ANY)] * len(after)]
    return pl.pallas_call(
        kernel,
        grid_spec=pltpu.PrefetchScalarGridSpec(
            num_scalar_prefetch=1,
            grid=grid,
            in_specs=in_specs,
            out_specs=out_specs,
            scratch_shapes=scratch,
        ),
        out_shape=out_shapes,
        input_output_aliases={1 + held + i: o for i, o in reuse},
        compiler_params=pltpu.CompilerParams(vmem_limit_bytes=vmem * MEGA),
        cost_estimate=pl.CostEstimate(flops=int(us * RATE), bytes_accessed=1, transcendentals=0),
    )(place, *operands, *after)


def add_kernel(place, *refs):
    refs[-1][...] = sum(ref[...].astype(F32) for ref in refs[:-1]).astype(BF)


def half_sum(place, terms, side, after=(), column=0, columns=None):
    size = terms[-1].shape[0] // 2
    _, height, columns = (*terms[0].shape[:2], columns or terms[0].shape[2])
    block = (min(size, 4), height, columns)
    count = size // block[0]
    return run(
        add_kernel, place, (count,),
        [spec(block, lambda n, p: (n + side * count, 0, column))] * len(terms),
        [spec(block, lambda n, p: (n, 0, 0))], [shape((size, *block[1:]), BF)], [], tuple(terms), 0,
        after=after,
    )[0]


def half_out(place, terms, after=(), **how):
    return half_sum(place, terms, 1, after, **how)


def rest_of(place, terms, after=(), **how):
    return half_sum(place, terms, 0, after, **how)


def join_kernel(place, *refs):
    cut = refs[0].shape[1]
    for n, out in enumerate(refs[-2:]):
        first, second, third, fourth = refs[4 * n : 4 * n + 4]
        out[:, :cut, :] = (first[...].astype(F32) + second[...].astype(F32)).astype(BF)
        out[:, cut:, :] = (third[...].astype(F32) + fourth[...].astype(F32)).astype(BF)


def joined_halves(place, terms, others, after=()):
    size = terms[0].shape[0] // 2
    tall, low = terms[0].shape[1:], others[0].shape[1:]
    total = (size, tall[0] + low[0], tall[1])
    specs = [
        spec((size, *part), lambda n, p, side=side: (side, 0, 0))
        for side in (1, 0)
        for part in (tall, tall, low, low)
    ]
    return run(
        join_kernel, place, (1,), specs, [full(total)] * 2, [shape(total, BF)] * 2, [],
        (*terms, *others) * 2, 0, after=after,
    )


def x_part(place, terms, side, after=()):
    line, _, seqs, *block = terms[0].shape
    return run(
        add_kernel, place, (line,),
        [spec((None, None, seqs, *block), lambda n, p: (n, side, 0, 0, 0))] * len(terms),
        [spec((seqs, None, *block), lambda n, p: (0, n, 0, 0))], [shape((seqs, line, *block), BF)], [],
        tuple(terms), 0, after=after,
    )[0].reshape(line * seqs, *block)


NOTE = (32, 1024)


def note_sum(left, right):
    return (left.astype(F32) + right.astype(F32)).astype(BF)


def qs_first_kernel(place, keep, recv, note, mate, send_out, rest_out):
    count, height, _ = keep.shape
    half = count // 2
    total = note_sum(note[...], mate[...])
    for out, base in ((send_out, half), (rest_out, 0)):
        for n in range(half):
            out[height * n : height * (n + 1), :] = note_sum(keep[base + n], recv[base + n])
        out[height * half :, :] = jnp.zeros((NOTE[0], out.shape[1]), BF)
        out[height * half :, : NOTE[1]] = total


def qs_next_kernel(place, keep, recv, send_out, rest_out):
    part = send_out.shape[0] - NOTE[0]
    total = note_sum(keep[...], recv[...])
    for out, base in ((send_out, part), (rest_out, 0)):
        out[:part, :] = total[base : base + part, :]
        out[part:, :] = total[2 * part :, :]


def qs_last_kernel(place, keep, recv, keep_out, line_out, side_out, cross_out, note_out, total):
    share = side_out.shape[1]
    height = side_out.shape[0]
    stay = pl.ds(pl.multiple_of(place[0] * share, LANES), 2 * share)
    leave = pl.ds(pl.multiple_of((1 - place[0]) * 2 * share, LANES), share)
    total[...] = keep[...].astype(F32) + recv[...].astype(F32)
    keep_out[...] = total[:height, stay]
    side_out[...] = total[:height, leave].astype(BF)
    cross_out[...] = total[height : 2 * height, leave].astype(BF)
    note = total[2 * height :, : NOTE[1]].astype(BF)
    note_out[...] = note
    line_out[...] = jnp.zeros_like(line_out)
    line_out[:height, : 2 * share] = total[height : 2 * height, stay].astype(BF)
    line_out[height:, :] = note


def qs_join_kernel(place, keep, line, side, cross, note, out, note_out):
    height, share = side.shape
    both = keep[...] + line[:height, : 2 * share].astype(F32)
    out[:, :share] = both[:, :share]
    out[:, share : 2 * share] = side[...].astype(F32) + cross[...].astype(F32)
    out[:, 2 * share :] = both[:, share:]
    note_out[...] = note_sum(note[...], line[height:, :])


def shape(dims, dtype):
    return jax.ShapeDtypeStruct(dims, dtype)


def qkv_kernel(place, source, vecs, weight, qb, vb, qkv_out, hidden_out):
    step = pl.program_id(0)

    @pl.when(step == 0)
    def _():
        normed, _ = layer_norm(source[...].astype(F32))
        hidden_out[...] = (normed * vecs[0:1, :] + vecs[1:2, :]).astype(BF)

    wide = mul(hidden_out[...], weight[...])
    shift = jnp.where(step == 0, qb[...], jnp.where(step == 2, vb[...], 0.0))
    factor = jnp.where(step == 0, 0.125, 1.0)
    qkv_out[0] = ((wide + shift) * factor).astype(BF)


def window(strip, block):
    off = (STRIP - block) * STRIP
    base = off // LANES * LANES
    held = strip[:, base : base + 6 * LANES]
    if off - base:
        held = pltpu.roll(held, 6 * LANES - (off - base), axis=1)
    return held[:, : 5 * LANES]


FORWARD_CHUNKS = ((0, 288), (288, 288), (576, 64))
CHUNKS = tuple((start * 144, 144) for start in range(4)) + ((576, 64),)


def attend_kernel(place, qkv, strips, even_mask, own_out, send_out, expo_out, inv_out, strip, attended):
    slots = qkv.shape[1]
    half = slots // 2
    side = place[0]
    lane = lax.broadcasted_iota(jnp.int32, (1, LANES), 1)
    first = lane < LANES // 2
    masks = (jnp.where(first, 1.0, 0.0).astype(BF), jnp.where(first, 0.0, 1.0).astype(BF))
    keys = [qkv[1] * m for m in masks]
    values = [qkv[2] * m for m in masks]
    picks = even_mask[...] > 0.5
    at = side * 6 + 2 * pl.program_id(0)
    for head in range(2):
        rolled = [
            pltpu.roll(
                jnp.broadcast_to(strips[at + head, par : par + 1, :], (STRIP, STRIP_WIDTH)),
                1,
                axis=1,
                stride=1,
                stride_axis=0,
            )
            for par in range(2)
        ]
        strip[head] = jnp.where(picks, rolled[0], rolled[1])
    block_lane = lax.broadcasted_iota(jnp.int32, (STRIP, LANES), 1)
    block_row = lax.broadcasted_iota(jnp.int32, (STRIP, LANES), 0)
    for start, count in FORWARD_CHUNKS:
        query = qkv[0, start : start + count, :]
        total = None
        scale = None
        for head in range(2):
            lone = strips[at + head, 0:1, 1152:1280]
            far = lone[:, 0:1]
            near = lone[:, 1:2]
            corner = lone[:, 2:3]
            biases = []
            for block in range(start // STRIP, min(start + count, 576) // STRIP):
                piece = window(strip.at[head], block)
                left = jnp.where(block_lane == 0, near, piece[:, :LANES])
                middle = piece[:, LANES : 4 * LANES]
                right = piece[:, 4 * LANES :]
                if block == 0:
                    top_row = block_row == 0
                    left = jnp.where(top_row, jnp.where(block_lane == 0, corner, far), left)
                    middle = jnp.concatenate(
                        [
                            jnp.where(top_row, far, middle[:, n * LANES : (n + 1) * LANES])
                            for n in range(3)
                        ],
                        axis=1,
                    )
                    right = jnp.where(top_row, far, right)
                right = jnp.where(block_lane > 64, NEGATIVE, right)
                biases.append(jnp.concatenate([left, middle, right], axis=1))
            if start + count > 576:
                row = window(strip.at[head, 0:8, :], STRIP)[0:1, :]
                row = jnp.concatenate(
                    [
                        jnp.where(lane == 0, near, row[:, :LANES]),
                        row[:, LANES : 4 * LANES],
                        jnp.where(lane > 64, NEGATIVE, row[:, 4 * LANES :]),
                    ],
                    axis=1,
                )
                biases.append(jnp.broadcast_to(row, (start + count - 576, 5 * LANES)))
            scores = mul(query, keys[head], NT) + jnp.concatenate(biases, axis=0)
            top = jnp.max(scores, axis=1, keepdims=True)
            expo = jnp.exp(scores - top)
            inverse = 1.0 / jnp.sum(expo, axis=1, keepdims=True)
            low = expo.astype(BF)
            expo_out[head, start : start + count, :] = low
            part = mul(low, values[head]) * inverse
            total = part if head == 0 else total + part
            spread = jnp.broadcast_to(inverse, (count, LANES))
            scale = spread if head == 0 else jnp.where(first, scale, spread)
        attended[start : start + count, :] = total
        inv_out[start : start + count, :] = scale
    own_out[...] = attended[pl.ds(pl.multiple_of(side * half, 64), half), :].astype(BF)
    send_out[...] = attended[pl.ds(pl.multiple_of((1 - side) * half, 64), half), :].astype(BF)


def attend_back_kernel(
    place, qkv, expo, attn_own, attn_send, grad_own, grad_other, inv, even_mask,
    dqkv_out, strip_out, grad_all, attn_all, d_scores, strip, dq_all,
):
    slots = qkv.shape[1]
    half = slots // 2
    here = pl.ds(pl.multiple_of(place[0] * half, 64), half)
    there = pl.ds(pl.multiple_of((1 - place[0]) * half, 64), half)
    lane = lax.broadcasted_iota(jnp.int32, (1, LANES), 1)
    first = lane < LANES // 2
    masks = (jnp.where(first, 1.0, 0.0).astype(BF), jnp.where(first, 0.0, 1.0).astype(BF))
    scaled = grad_own[...].astype(F32) * inv[here, :]
    grad_all[here, :] = scaled
    attn_all[here, :] = scaled * attn_own[...].astype(F32)
    scaled = grad_other[...].astype(F32) * inv[there, :]
    grad_all[there, :] = scaled
    attn_all[there, :] = scaled * attn_send[...].astype(F32)
    keys = [qkv[1] * m for m in masks]
    values = [qkv[2] * m for m in masks]
    block_lane = lax.broadcasted_iota(jnp.int32, (STRIP, LANES), 1)
    block_row = lax.broadcasted_iota(jnp.int32, (STRIP, LANES), 0)
    strip[...] = jnp.zeros_like(strip)
    columns = [jnp.zeros((8, LANES), F32) for _ in range(2)]
    tops = [None, None]
    zeros = jnp.zeros((STRIP, LANES), F32)
    for start, count in CHUNKS:
        grads = grad_all[start : start + count, :].astype(BF)
        products = attn_all[start : start + count, :]
        total = None
        for head in range(2):
            chosen = first if head == 0 else jnp.logical_not(first)
            delta = jnp.sum(jnp.where(chosen, products, 0.0), axis=1, keepdims=True)
            d_probs = mul(grads, values[head], NT)
            d_score = expo[head, start : start + count, :].astype(F32) * (d_probs - delta)
            low = d_score.astype(BF)
            d_scores[head, start : start + count, :] = low
            part = mul(low, keys[head])
            total = part if head == 0 else total + part
            if start == 576:
                for tile in range(count // 8):
                    columns[head] = columns[head] + d_score[8 * tile : 8 * tile + 8, :LANES]
                line = jnp.sum(d_score, axis=0, keepdims=True)
                line = jnp.concatenate([jnp.where(lane == 0, 0.0, line[:, :LANES]), line[:, LANES:]], axis=1)
                strip[head, 0:1, : 5 * LANES] = strip[head, 0:1, : 5 * LANES] + line
            else:
                for block in range(start // STRIP, (start + count) // STRIP):
                    at = block * STRIP - start
                    piece = d_score[at : at + STRIP, :]
                    left = piece[:, :LANES]
                    rest = piece[:, LANES:]
                    if block == 0:
                        tops[head] = piece[0:1, :]
                        left = jnp.where(block_row == 0, 0.0, left)
                        rest = jnp.concatenate(
                            [
                                jnp.where(block_row == 0, 0.0, rest[:, n * LANES : (n + 1) * LANES])
                                for n in range(4)
                            ],
                            axis=1,
                        )
                    columns[head] = columns[head] + left[0:8] + left[8:16] + left[16:24]
                    piece = jnp.concatenate(
                        [jnp.where(block_lane == 0, 0.0, left), rest, zeros], axis=1
                    )
                    off = (STRIP - block) * STRIP
                    base = off // LANES * LANES
                    if off - base:
                        piece = pltpu.roll(piece, off - base, axis=1)
                    strip[head, :, base : base + 6 * LANES] = (
                        strip[head, :, base : base + 6 * LANES] + piece
                    )
        dq_all[start : start + count, :] = total
    dqkv_out[0] = dq_all[...].astype(BF) * BF(0.125)
    turned_query = qkv[0].astype(F32).T.astype(BF)
    turned_grads = grad_all[...].T.astype(BF)
    half_lanes = LANES // 2
    for at, left, right in ((1, turned_query, d_scores), (2, turned_grads, expo)):
        sides = [
            mul(left[half_lanes * head : half_lanes * (head + 1), :], right[head])
            for head in range(2)
        ]
        dqkv_out[at] = jnp.concatenate(sides, axis=0).T.astype(BF)
    picks = even_mask[...] > 0.5
    row_id = lax.broadcasted_iota(jnp.int32, (STRIP, STRIP_WIDTH), 0)
    wide_lane = lax.broadcasted_iota(jnp.int32, (1, STRIP_WIDTH), 1)
    for head in range(2):
        held = strip[head]
        lines = []
        for par in range(2):
            part = jnp.where(picks, held, 0.0) if par == 0 else jnp.where(picks, 0.0, held)
            part = pltpu.roll(part, STRIP_WIDTH - 1, axis=1)
            for bit in (1, 2, 4, 8, 16):
                part = jnp.where(
                    (row_id & bit) > 0, pltpu.roll(part, STRIP_WIDTH - bit, axis=1), part
                )
            lines.append(jnp.sum(part, axis=0, keepdims=True))
        near = jnp.sum(jnp.where(lane == 0, columns[head], 0.0)).reshape(1, 1)
        corner = tops[head][:, 0:1]
        far = jnp.sum(tops[head], axis=1, keepdims=True) - corner
        line = lines[0]
        line = jnp.where(wide_lane >= 1152, 0.0, line)
        line = jnp.where(wide_lane == 1152, far, line)
        line = jnp.where(wide_lane == 1153, near, line)
        line = jnp.where(wide_lane == 1154, corner, line)
        strip_out[0, head, 0:1, :] = line
        strip_out[0, head, 1:2, :] = lines[1]


def d_act_kernel(place, cot, vecs, fc2, d_ffn_out, d_act_out):
    @pl.when(pl.program_id(0) == 0)
    def _():
        d_ffn_out[...] = (vecs[7:8, :] * cot[...].astype(F32)).astype(BF)

    d_act_out[...] = mul(d_ffn_out[...], fc2[...], NT).astype(BF)


def ffn_kernel(
    place, tokens, attn_own, attn_other, vecs, proj, fc1, fc1_bias, d_act,
    act_out, d_pre_out, fc1_bias_out, hidden_out, resid_out, attn_out, mixed_out,
):
    width = attn_own.shape[1]

    @pl.when(pl.program_id(0) == 0)
    def _():
        attn_out[:, pl.ds(pl.multiple_of(place[0] * width, LANES), width)] = attn_own[...]
        attn_out[:, pl.ds(pl.multiple_of((1 - place[0]) * width, LANES), width)] = attn_other[...]
        mixed = mul(attn_out[...], proj[...]) + vecs[2:3, :]
        mixed_out[...] = mixed
        resid = tokens[...].astype(F32) + vecs[3:4, :] * mixed
        resid_out[...] = resid
        normed, _ = layer_norm(resid)
        hidden_out[...] = (normed * vecs[4:5, :] + vecs[5:6, :]).astype(BF)

    pre = mul(hidden_out[...], fc1[...]) + fc1_bias[...]
    gate = 0.5 * (1.0 + lax.erf(pre * ROOT_HALF))
    act_out[...] = (pre * gate).astype(BF)
    slope = gate + pre * jnp.exp(-0.5 * pre * pre) * GAUSS_NORM
    d_pre = (d_act[...].astype(F32) * slope).astype(BF)
    d_pre_out[...] = d_pre
    fc1_bias_out[...] = jnp.sum(d_pre.astype(F32), axis=0, keepdims=True)


def ffn_back_kernel(
    place, d_pre, fc1, cot, d_ffn, resid, mixed_in, vecs, proj_own, proj_other,
    d_mixed_out, d_resid_out, grad_own_out, grad_send_out, small_out, d_hidden,
):
    step = pl.program_id(0)
    part = mul(d_pre[...], fc1[...], NT)

    @pl.when(step == 0)
    def _():
        d_hidden[...] = part

    @pl.when(step > 0)
    def _():
        d_hidden[...] += part

    @pl.when(step == pl.num_programs(0) - 1)
    def _():
        grad = d_hidden[...]
        mixed = mixed_in[...]
        normed, inverse = layer_norm(resid[...])
        d_resid = cot[...].astype(F32) + layer_norm_back(grad, normed, inverse, vecs[4:5, :])
        d_resid_out[...] = d_resid
        d_mixed = (vecs[3:4, :] * d_resid).astype(BF)
        d_mixed_out[...] = d_mixed
        grad_send_out[...] = mul(d_mixed, proj_other[...], NT).astype(BF)
        grad_own_out[...] = mul(d_mixed, proj_own[...], NT).astype(BF)
        small_out[0:1, :] = jnp.sum(grad * normed, axis=0, keepdims=True)
        small_out[1:2, :] = jnp.sum(grad, axis=0, keepdims=True)
        small_out[2:3, :] = jnp.sum(d_resid * mixed, axis=0, keepdims=True)
        small_out[3:4, :] = jnp.sum(d_mixed.astype(F32), axis=0, keepdims=True)
        small_out[4:5, :] = jnp.sum(d_ffn[...].astype(F32), axis=0, keepdims=True)
        small_out[5:8, :] = jnp.zeros((3, small_out.shape[1]), F32)


def fc2_grad_kernel(place, act, d_ffn, keep_out, send_out, held):
    core = place[1]
    held[...] = mul(act[...], d_ffn[...], TN)
    for pair in range(2):
        for seq in range(2):
            at = (0, pair ^ place[6], seq ^ place[0])
            columns = slice(384 * seq, 384 * seq + 384)
            low = pl.multiple_of(384 * pair + 192 * core, 64)
            high = pl.multiple_of(384 * pair + 192 * (1 - core), 64)
            keep_out[at] = held[pl.ds(low, 192), columns].astype(BF)
            send_out[at] = held[pl.ds(high, 192), columns].astype(BF)


def fc1_grad_kernel(place, hidden, d_pre, attn, d_mixed, keep_out, send_out, held, *, rest):
    step = pl.program_id(0)
    core = place[1]
    held[...] = mul(hidden[...], d_pre[...], TN)
    seq = step // 2
    lanes = pl.ds(pl.multiple_of((step % 2) * 768, LANES), 768)
    for pair in range(8):
        at = rest(pair % 2, pair // 2, seq) ^ place[3]
        low = pl.multiple_of(96 * pair + 48 * core, 16)
        high = pl.multiple_of(96 * pair + 48 * (1 - core), 16)
        keep_out[at, :, lanes] = held[pl.ds(low, 48), :].astype(BF)
        send_out[at, :, lanes] = held[pl.ds(high, 48), :].astype(BF)

    @pl.when(step == pl.num_programs(0) - 1)
    def _():
        held[...] = mul(attn[...], d_mixed[...], TN)
        for pair in range(8):
            low = pl.multiple_of(96 * pair + 48 * core, 16)
            high = pl.multiple_of(96 * pair + 48 * (1 - core), 16)
            for side in range(2):
                at = rest_label(ORDER_A)(pair % 2, pair // 2, side) ^ place[2]
                columns = slice(384 * side, 384 * side + 384)
                keep_out[at, :, 1536:1920] = held[pl.ds(low, 48), columns].astype(BF)
                send_out[at, :, 1536:1920] = held[pl.ds(high, 48), columns].astype(BF)


def result_kernel(place, act, fc2, resid, cot, vecs, result_out, small_out, total):
    step = pl.program_id(0)

    @pl.when(step == 0)
    def _():
        total[...] = jnp.zeros_like(total)

    total[...] += mul(act[...], fc2[...])

    @pl.when(step == pl.num_programs(0) - 1)
    def _():
        ffn = total[...] + vecs[6:7, :]
        result_out[...] = (resid[...] + vecs[7:8, :] * ffn).astype(BF)
        small_out[0:1, :] = jnp.sum(cot[...].astype(F32) * ffn, axis=0, keepdims=True)
        small_out[1:8, :] = jnp.zeros((7, small_out.shape[1]), F32)


def hidden1_grad_kernel(
    place, dqkv0, dqkv1, dqkv2, weight, own, other, keep_out, send_out, small_out, total, joined
):
    step = pl.program_id(0)
    rows = own.shape[0]
    here = pl.ds(pl.multiple_of(place[0] * rows, 64), rows)
    there = pl.ds(pl.multiple_of((1 - place[0]) * rows, 64), rows)

    @pl.when(step == 0)
    def _():
        total[...] = jnp.zeros_like(total)
        small_out[...] = jnp.zeros_like(small_out)

    for n, part in enumerate((dqkv0, dqkv1, dqkv2)):
        joined[:, LANES * n : LANES * (n + 1)] = part[0]
    grads = joined[...]
    total[...] += mul(grads, weight[...], NT)
    line = jnp.sum(grads.astype(F32), axis=0, keepdims=True)

    @pl.when(step == 0)
    def _():
        small_out[2:3, :384] = line

    @pl.when(step == 2)
    def _():
        small_out[2:3, 384:] = line
        mine = total[here, :]
        theirs = total[there, :]
        keep_out[...] = mine
        send_out[...] = theirs.astype(BF)
        normed_mine, _ = layer_norm(own[...].astype(F32))
        normed_theirs, _ = layer_norm(other[...].astype(F32))
        small_out[0:1, :] = jnp.sum(mine * normed_mine, axis=0, keepdims=True) + jnp.sum(
            theirs * normed_theirs, axis=0, keepdims=True
        )
        small_out[1:2, :] = jnp.sum(mine, axis=0, keepdims=True) + jnp.sum(
            theirs, axis=0, keepdims=True
        )


def qkv_grad_kernel(
    place, hidden, dqkv0, dqkv1, dqkv2, keep_out, send_out, held, joined, *, rest
):
    core = place[1]
    for n, part in enumerate((dqkv0, dqkv1, dqkv2)):
        joined[:, LANES * n : LANES * (n + 1)] = part[0]
    held[...] = mul(hidden[...], joined[...], TN)
    for pair in range(8):
        at = rest(pair % 2, pair // 2, 0) ^ place[4]
        low = pl.multiple_of(96 * pair + 48 * core, 16)
        high = pl.multiple_of(96 * pair + 48 * (1 - core), 16)
        keep_out[at] = held[pl.ds(low, 48), :].astype(BF)
        send_out[at] = held[pl.ds(high, 48), :].astype(BF)


def tokens_grad_kernel(place, keep, recv, own, d_resid, vecs, grad_out):
    grad = keep[...] + recv[...].astype(F32)
    normed, inverse = layer_norm(own[...].astype(F32))
    back = layer_norm_back(grad, normed, inverse, vecs[0:1, :])
    grad_out[...] = (d_resid[...] + back).astype(BF)


def rest_label(order):
    def rest(x_bit, line, seq):
        bits = {"x": x_bit, "z1": line & 1, "z2": line >> 1, "y": seq}
        total = 0
        for name in order[1:]:
            total = total * 2 + bits[name]
        return total

    return rest


ORDER_A = ("core", "x", "y", "z1", "z2")
ORDER_B = ("core", "z1", "x", "y", "z2")
ORDER_Q = ("core", "x", "z1", "z2")


SPAN = 2 * GRID - 1
CELLS = SPAN * SPAN


def flips():
    row = lax.broadcasted_iota(jnp.int32, (LANES, LANES), 0)
    lane = lax.broadcasted_iota(jnp.int32, (LANES, LANES), 1)
    return jnp.where(row + lane == LANES - 1, 1.0, 0.0)


def exact(left, right, dims):
    return lax.dot_general(
        left, right, dims, precision=lax.Precision.HIGHEST, preferred_element_type=F32
    )


def moved_window(source, start, target):
    base = start // LANES * LANES
    place = target % LANES
    held = source[:, base : base + 2 * LANES]
    turn = (place - (start - base)) % (2 * LANES)
    if turn:
        held = pltpu.roll(held, turn, axis=1)
    lane = lax.broadcasted_iota(jnp.int32, (1, 2 * LANES), 1)
    return jnp.where((lane >= place) & (lane < place + SPAN), held, 0.0)


def strips_kernel(place, table, strips_out, flat, sides):
    heads = table.shape[0]
    flat[...] = jnp.zeros_like(flat)
    flat[:heads, : CELLS + 3] = table[...]
    turned = pltpu.roll(flat[:, : 18 * LANES], 18 * LANES - CELLS, axis=1)
    tail = turned[:, :LANES]
    for n in range(18):
        block = 17 - n
        flat[:, LANES * n : LANES * (n + 1)] = exact(
            turned[:, LANES * block : LANES * (block + 1)], flips(), NN
        )
    sides[...] = jnp.zeros_like(sides)
    for b in range(SPAN):
        base = 24 * b // LANES * LANES
        part = moved_window(flat, SPAN * b, 24 * b)
        sides[b % 2, :, base : base + 2 * LANES] += part
    lane = lax.broadcasted_iota(jnp.int32, (16, LANES), 1)
    sides[0, :, 1152:1280] = jnp.where(lane < 3, tail, 0.0)
    for head in range(heads):
        for par in range(2):
            strips_out[head, par : par + 1, :] = sides[par, head : head + 1, :]


def pack_kernel(place, strip0, strip1, strip2, ffn, fc1_bias, last, result, packed_out, packed):
    packed[...] = jnp.zeros_like(packed)
    for n in range(5):
        lanes = slice(256 * n, 256 * n + 256)
        for pair, strip in enumerate((strip0, strip1, strip2)):
            for head in range(2):
                for par in range(2):
                    row = 16 * n + 6 * par + 2 * pair + head
                    packed[row : row + 1, :] = strip[0, head, par : par + 1, lanes]
    for n in range(3):
        lanes = slice(256 * n, 256 * n + 256)
        row = 80 + 16 * n
        packed[row : row + 5, :] = ffn[0:5, lanes]
        packed[row + 5 : row + 6, :] = result[0:1, lanes]
        packed[row + 6 : row + 9, :] = last[0:3, lanes]
        for part in range(4):
            packed[row + 9 + part : row + 10 + part, :] = fc1_bias[
                :, 768 * part + 256 * n : 768 * part + 256 * n + 256
            ]
    for n in range(8):
        packed_out[16 * (n // 4) : 16 * (n // 4) + 16, 256 * (n % 4) : 256 * (n % 4) + 256] = packed[
            16 * n : 16 * n + 16, :
        ].astype(BF)


def unpack_kernel(
    place, packed_in, mate_in, table_out, norm2_gain, norm2_bias, scale1, proj_bias, fc2_bias, scale2,
    norm1_gain, norm1_bias, query_bias, value_bias, fc1_bias, flat, sides, packed, mate,
):
    for held, source in ((packed, packed_in), (mate, mate_in)):
        for n in range(8):
            held[16 * n : 16 * n + 16, :] = source[
                16 * (n // 4) : 16 * (n // 4) + 16, 256 * (n % 4) : 256 * (n % 4) + 256
            ].astype(F32)
    heads = table_out.shape[0]
    half = heads // 2
    left = place[0] == 0
    flat[...] = jnp.zeros_like(flat)
    for n in range(5):
        lanes = slice(256 * n, 256 * n + 256)
        for par in range(2):
            rows = slice(16 * n + half * par, 16 * n + half * par + half)
            mine = packed[rows, :]
            theirs = mate[rows, :]
            sides[par, 0:half, lanes] = jnp.where(left, mine, theirs)
            sides[par, half:heads, lanes] = jnp.where(left, theirs, mine)
    for b in range(SPAN):
        target = SPAN * b
        base = target // LANES * LANES
        part = moved_window(sides.at[b % 2], 24 * b, target)
        flat[:, base : base + 2 * LANES] += part
    lane = lax.broadcasted_iota(jnp.int32, (16, LANES), 1)
    blocks = [
        exact(flat[:, LANES * (17 - n) : LANES * (18 - n)], flips(), NN) for n in range(18)
    ]
    blocks[0] = jnp.where(lane < 3, sides[0, :, 1152:1280], blocks[0])
    turned = pltpu.roll(jnp.concatenate(blocks, axis=1), CELLS, axis=1)
    table_out[...] = turned[:heads, : CELLS + 3]
    outs = (norm2_gain, norm2_bias, scale1, proj_bias, fc2_bias, scale2, norm1_gain, norm1_bias)
    for n in range(3):
        lanes = slice(256 * n, 256 * n + 256)
        for at, out in enumerate(outs):
            row = 80 + 16 * n + at
            out[lanes] = (packed[row : row + 1, :] + mate[row : row + 1, :]).reshape(256)
        for part in range(4):
            row = 89 + 16 * n + part
            fc1_bias[768 * part + 256 * n : 768 * part + 256 * n + 256] = (
                packed[row : row + 1, :] + mate[row : row + 1, :]
            ).reshape(256)
    for source, side in ((packed, place[0]), (mate, 1 - place[0])):
        line = jnp.concatenate([source[88 + 16 * n : 89 + 16 * n, :] for n in range(3)], axis=1)
        lanes = pl.ds(pl.multiple_of(side * 384, LANES), 384)
        query_bias[lanes] = line[:, :384].reshape(384)
        value_bias[lanes] = line[:, 384:].reshape(384)


def even_places():
    lane = np.arange(STRIP_WIDTH)[None, :]
    row = np.arange(STRIP)[:, None]
    turn = (lane - 1) // STRIP
    return np.where(row == 0, turn % 2 == 0, turn % 2 == 1).astype(np.float32)


def split_body(
    tokens,
    masked,
    out_grad,
    norm1_gain,
    norm1_bias,
    qkv_weight,
    query_bias,
    value_bias,
    rel_table,
    proj_weight,
    proj_bias,
    scale1,
    norm2_gain,
    norm2_bias,
    fc1_weight,
    fc1_bias,
    fc2_weight,
    fc2_bias,
    scale2,
):
    _, rows, width = tokens.shape
    slots = 2 * rows
    heads = rel_table.shape[1] // 2
    pairs = heads // 2
    share = width // 2
    hidden = fc1_weight.shape[1]
    seq = lax.axis_index("seq")
    img = lax.axis_index("img")
    core = img & 1
    line = img >> 2
    x_bit = (img >> 1) & 1
    place = jnp.stack(
        [
            seq,
            core,
            rest_label(ORDER_A)(x_bit, line, seq),
            rest_label(ORDER_B)(x_bit, line, seq),
            rest_label(ORDER_Q)(x_bit, line, seq),
            line,
            x_bit,
        ]
    ).astype(jnp.int32)
    own = tokens.reshape(rows, width)
    other = swapped(own, "y")
    cot = (out_grad.astype(F32) * masked.astype(F32)[..., None]).astype(BF).reshape(rows, width)
    vecs = jnp.stack(
        [norm1_gain, norm1_bias, proj_bias, scale1, norm2_gain, norm2_bias, fc2_bias, scale2]
    )
    strips = run(
        strips_kernel, place, (1,), [full(rel_table.shape[::-1])], [full((2 * heads, 2, STRIP_WIDTH))],
        [shape((2 * heads, 2, STRIP_WIDTH), F32)],
        [pltpu.VMEM((16, 2432), F32), pltpu.VMEM((2, 16, STRIP_WIDTH), F32)], (rel_table.T,), 0,
    )[0]
    even_mask = jnp.asarray(even_places())

    def qkv_rows(source, mine, held):
        def side(p):
            return p[0] if mine else 1 - p[0]

        return run(
            qkv_kernel, place, (3,),
            [
                full((rows, width)), full((8, width)),
                spec((width, share), lambda t, p: (0, 2 * t + p[0])),
                spec((1, share), lambda t, p: (0, p[0])), spec((1, share), lambda t, p: (0, p[0])),
            ],
            [
                spec((1, rows, share), lambda t, p: (t, side(p), 0)),
                spec((rows, width), lambda t, p: (side(p), 0)),
            ],
            [shape((3, slots, share), BF), shape((slots, width), BF)],
            [],
            (source, vecs, qkv_weight, query_bias.reshape(1, width), value_bias.reshape(1, width)),
            0, after=held, reuse=() if mine else ((0, 0), (1, 1)),
        )

    qkv, hidden1 = qkv_rows(other, False, qkv_rows(own, True, ()))
    pair_rows = spec((slots, LANES), lambda n, p: (0, n))
    pair_half = spec((rows, LANES), lambda n, p: (0, n))
    pair_qkv = spec((3, slots, LANES), lambda n, p: (0, 0, n))
    pair_expo = spec((2, slots, slots), lambda n, p: (n, 0, 0))
    attn_own, attn_send, expo, inv = run(
        attend_kernel, place, (pairs,),
        [pair_qkv, full((2 * heads, 2, STRIP_WIDTH)), full((STRIP, STRIP_WIDTH))],
        [pair_half, pair_half, pair_expo, pair_rows],
        [
            shape((rows, share), BF), shape((rows, share), BF),
            shape((heads, slots, slots), BF), shape((slots, share), F32),
        ],
        [pltpu.VMEM((2, STRIP, STRIP_WIDTH), F32), pltpu.VMEM((slots, LANES), F32)],
        (qkv, strips, even_mask),
        16 * slots * slots * 64 * heads,
    )
    attn_other = swapped(attn_send, "y")
    parts = 4
    part = hidden // parts
    whole = full((rows, width))
    sliced = spec((rows, part), lambda c, p: (0, c))
    d_ffn, d_act = run(
        d_act_kernel, place, (parts,),
        [whole, full((8, width)), spec((part, width), lambda c, p: (c, 0))],
        [whole, sliced], [shape((rows, width), BF), shape((rows, hidden), BF)], [],
        (cot, vecs, fc2_weight), 0, after=(attn_send,),
    )
    act, d_pre, fc1_bias_part, hidden2, resid, attn_low, mixed = run(
        ffn_kernel, place, (parts,),
        [
            whole, full((rows, share)), full((rows, share)), full((8, width)),
            full((width, width)), spec((width, part), lambda c, p: (0, c)),
            spec((1, part), lambda c, p: (0, c)), sliced,
        ],
        [sliced, sliced, spec((1, part), lambda c, p: (0, c)), whole, whole, whole, whole],
        [
            shape((rows, hidden), BF), shape((rows, hidden), BF), shape((1, hidden), F32),
            shape((rows, width), BF), shape((rows, width), F32), shape((rows, width), BF),
            shape((rows, width), F32),
        ],
        [],
        (own, attn_own, attn_other, vecs, proj_weight, fc1_weight, fc1_bias.reshape(1, hidden), d_act),
        0,
    )
    cube = (4, 2, 2, 192, share)

    def line_place(c, p):
        far = c ^ p[5]
        return (far & 1) * 2 + (far >> 1), 0, 0, 0, 0

    block = spec((1, *cube[1:]), line_place)
    keep_a, send_a = run(
        fc2_grad_kernel, place, (parts,), [sliced, whole], [block, block],
        [shape(cube, BF), shape(cube, BF)], [pltpu.VMEM((part, width), F32)], (act, d_ffn), 0,
    )
    terms_a = [keep_a, swapped(send_a, "core")]
    d_mixed, d_resid, grad_own, grad_send, small_ffn = run(
        ffn_back_kernel, place, (parts,),
        [
            sliced, spec((width, part), lambda c, p: (0, c)), whole, whole, whole, whole, full((8, width)),
            spec((share, width), lambda c, p: (p[0], 0)), spec((share, width), lambda c, p: (1 - p[0], 0)),
        ],
        [whole, whole, full((rows, share)), full((rows, share)), full((8, width))],
        [
            shape((rows, width), BF), shape((rows, width), F32), shape((rows, share), BF),
            shape((rows, share), BF), shape((8, width), F32),
        ],
        [pltpu.VMEM((rows, width), F32)],
        (d_pre, fc1_weight, cot, d_ffn, resid, mixed, vecs, proj_weight, proj_weight), 0, after=(send_a,),
    )
    grad_other = swapped(grad_send, "y")
    out_a1 = x_part(place, terms_a, 1, (grad_send,))
    terms_a = [x_part(place, terms_a, 0, (out_a1,)), swapped(out_a1, ORDER_A[1])]
    block = (16, 48, 5 * share)
    keep_b, send_b = run(
        functools.partial(fc1_grad_kernel, rest=rest_label(ORDER_B)), place, (parts,),
        [whole, sliced, whole, whole], [full(block), full(block)],
        [shape(block, BF), shape(block, BF)],
        [pltpu.VMEM((width, part), F32)], (hidden2, d_pre, attn_low, d_mixed), 0, after=(out_a1, terms_a[0]),
    )
    terms_b = [keep_b, swapped(send_b, "core")]

    def attend_back(pair, after):
        pair_expo = spec((2, slots, slots), lambda n, p: (pair, 0, 0))
        pair_rows = spec((slots, LANES), lambda n, p: (0, pair))
        pair_half = spec((rows, LANES), lambda n, p: (0, pair))
        return run(
            attend_back_kernel, place, (1,),
            [
                spec((3, slots, LANES), lambda n, p: (0, 0, pair)), pair_expo, pair_half, pair_half,
                pair_half, pair_half, pair_rows, full((STRIP, STRIP_WIDTH)),
            ],
            [full((3, slots, LANES)), full((1, 2, 2, STRIP_WIDTH))],
            [shape((3, slots, LANES), BF), shape((1, 2, 2, STRIP_WIDTH), F32)],
            [
                pltpu.VMEM((slots, LANES), F32), pltpu.VMEM((slots, LANES), F32),
                pltpu.VMEM((2, slots, slots), BF), pltpu.VMEM((2, STRIP, STRIP_WIDTH), F32),
                pltpu.VMEM((slots, LANES), F32),
            ],
            (qkv, expo, attn_own, attn_send, grad_own, grad_other, inv, even_mask),
            32 * slots * slots * 64 * 2, after=after, us=40.0 if pair == 0 else None,
        )

    dqkv0, strip0 = attend_back(0, (send_b,))
    out_p1 = half_out(place, terms_b, (dqkv0,), column=4, columns=share)
    terms_p = [
        rest_of(place, terms_b, (out_p1,), column=4, columns=share),
        swapped(out_p1, ORDER_A[1]),
    ]
    out_b1 = half_out(place, terms_b, (out_p1,), columns=4 * share)
    terms_b = [rest_of(place, terms_b, (out_b1,), columns=4 * share), swapped(out_b1, ORDER_B[1])]
    dqkv1, strip1 = attend_back(1, (dqkv0, out_b1, terms_b[0], terms_p[0]))
    dqkv2, strip2 = attend_back(2, (dqkv1,))
    dqkv = (dqkv0, dqkv1, dqkv2)
    third = [spec((1, slots, LANES), lambda t, p: (t, 0, 0))] * 3
    dh_keep, dh_send, small_last = run(
        hidden1_grad_kernel, place, (3,),
        [*third, spec((width, share), lambda t, p: (0, 2 * t + p[0])), whole, whole],
        [whole, whole, full((8, width))],
        [shape((rows, width), F32), shape((rows, width), BF), shape((8, width), F32)],
        [pltpu.VMEM((slots, width), F32), pltpu.VMEM((slots, share), BF)], (*dqkv, qkv_weight, own, other),
        2 * slots * width * 3 * share,
    )
    block = (8, 48, 3 * share)
    keep_q, send_q = run(
        functools.partial(qkv_grad_kernel, rest=rest_label(ORDER_Q)), place, (3,),
        [full((slots, width)), *third], [spec((8, 48, share), lambda t, p: (0, 0, t))] * 2,
        [shape(block, BF), shape(block, BF)],
        [pltpu.VMEM((width, share), F32), pltpu.VMEM((slots, share), BF)], (hidden1, *dqkv), 2 * slots * width * 3 * share,
        after=(dh_send,),
    )
    recv_q = swapped(send_q, "core")
    out_a2, rest_a = joined_halves(place, terms_a, terms_p, (send_q,))
    terms_a = [rest_a, swapped(out_a2, "y")]
    result, small_result = run(
        result_kernel, place, (parts,),
        [sliced, spec((part, width), lambda c, p: (c, 0)), whole, whole, full((8, width))],
        [whole, full((8, width))],
        [shape((rows, width), BF), shape((8, width), F32)],
        [pltpu.VMEM((rows, width), F32)], (act, fc2_weight, resid, cot, vecs),
        2 * rows * width * hidden, after=(out_a2, rest_a),
    )
    packed = run(
        pack_kernel, place, (1,),
        [*[full((1, 2, 2, STRIP_WIDTH))] * 3, full((8, width)), full((1, hidden)), full((8, width)), full((8, width))],
        [full(NOTE)], [shape(NOTE, BF)], [pltpu.VMEM((128, 256), F32)],
        (strip0, strip1, strip2, small_ffn, fc1_bias_part, small_last, small_result), 0,
    )[0]
    mate = swapped(packed, "core")
    out_b2 = half_out(place, terms_b, (packed,))
    terms_b = [*terms_b, swapped(out_b2, "x")]

    def wide(blocks, columns):
        return (48 * blocks + NOTE[0], columns)

    send, rest = run(
        qs_first_kernel, place, (1,),
        [full((8, 48, 3 * share))] * 2 + [full(NOTE)] * 2, [full(wide(4, 3 * share))] * 2,
        [shape(wide(4, 3 * share), BF)] * 2, [], (keep_q, recv_q, packed, mate), 0, after=(out_b2,),
    )
    recv = swapped(send, "x")
    out_a3 = half_out(place, terms_a, (send,))
    terms_a = [*terms_a, swapped(out_a3, "z1")]
    out_b3 = half_out(place, terms_b, (out_a3,))
    terms_b = [*terms_b, swapped(out_b3, "y")]
    dh_late = run(
        add_kernel, place, (1,), [whole], [whole], [shape((rows, width), BF)], [], (dh_send,), 0,
        after=(out_b3,),
    )[0]
    dh_recv = swapped(dh_late, "y")
    out_a4 = half_out(place, terms_a, (dh_late,))
    terms_a = [*terms_a, swapped(out_a4, "z2")]
    send, rest = run(
        qs_next_kernel, place, (1,), [full(wide(4, 3 * share))] * 2, [full(wide(2, 3 * share))] * 2,
        [shape(wide(2, 3 * share), BF)] * 2, [], (rest, recv), 0, after=(out_a4,),
    )
    recv = swapped(send, "z1")
    out_b4 = half_out(place, terms_b, (send,))
    terms_b = [*terms_b, swapped(out_b4, "z2")]
    q_keep, q_line, q_side, q_cross, note = run(
        qs_last_kernel, place, (1,), [full(wide(2, 3 * share))] * 2,
        [
            full((48, 2 * share)), full(wide(1, NOTE[1])), full((48, share)), full((48, share)), full(NOTE),
        ],
        [
            shape((48, 2 * share), F32), shape(wide(1, NOTE[1]), BF), shape((48, share), BF),
            shape((48, share), BF), shape(NOTE, BF),
        ],
        [pltpu.VMEM(wide(2, 3 * share), F32)], (rest, recv), 0, after=(out_b4,),
    )
    q_sends = (swapped(q_line, "z2"), swapped(q_side, "y"), swapped(q_cross, "z2", "y"))
    qkv_grad, packed = run(
        qs_join_kernel, place, (1,),
        [full((48, 2 * share)), full(wide(1, NOTE[1])), full((48, share)), full((48, share)), full(NOTE)],
        [full((48, 3 * share)), full(NOTE)], [shape((48, 3 * share), F32), shape(NOTE, BF)], [],
        (q_keep, *q_sends, note), 0,
    )
    mate = swapped(packed, "y")
    tokens_grad = run(
        tokens_grad_kernel, place, (1,),
        [whole, whole, whole, whole, full((8, width))], [whole],
        [shape((rows, width), BF)], [], (dh_keep, dh_recv, own, d_resid, vecs), 0,
        after=(packed,),
    )[0]
    fc2_proj = added(terms_a)
    fc1_grad = added(terms_b)
    fc2_grad = fc2_proj[:192]
    proj_grad = fc2_proj[192:]
    vector = shape((width,), F32)
    table_grad, *small = run(
        unpack_kernel, place, (1,), [full(NOTE)] * 2,
        [full(rel_table.shape[::-1]), *[full((width,))] * 10, full((hidden,))],
        [shape(rel_table.shape[::-1], F32), *[vector] * 10, shape((hidden,), F32)],
        [
            pltpu.VMEM((16, 2432), F32), pltpu.VMEM((2, 16, STRIP_WIDTH), F32),
            pltpu.VMEM((128, 256), F32), pltpu.VMEM((128, 256), F32),
        ], (packed, mate), 0,
    )
    return (
        result.reshape(tokens.shape),
        tokens_grad.reshape(tokens.shape),
        small[6],
        small[7],
        qkv_grad,
        small[8],
        small[9],
        table_grad.T,
        proj_grad,
        small[3],
        small[2],
        small[0],
        small[1],
        fc1_grad,
        small[10],
        fc2_grad,
        small[4],
        small[5],
    )


def solution(mesh):
    in_specs = (
        P("img", "seq", None),
        P("img", "seq"),
        P("img", "seq", None),
        P(),
        P(),
        P(),
        P(),
        P(),
        P(),
        P(),
        P(),
        P(),
        P(),
        P(),
        P(),
        P(),
        P(),
        P(),
        P(),
    )
    out_specs = (
        P("img", "seq", None),
        P("img", "seq", None),
        P(),
        P(),
        P("img", "seq"),
        P(),
        P(),
        P(),
        P("img", "seq"),
        P(),
        P(),
        P(),
        P(),
        P("img", "seq"),
        P(),
        P("img", "seq"),
        P(),
        P(),
    )
    sizes = dict(mesh.shape)
    body = split_body if (sizes["img"], sizes["seq"]) == (16, 2) else general_body
    return jax.shard_map(body, mesh=mesh, in_specs=in_specs, out_specs=out_specs, check_vma=False)
```

```python
import functools

import jax
import jax.numpy as jnp
import numpy as np
from jax import lax
from jax.experimental import pallas as pl
from jax.experimental.pallas import tpu as pltpu
from jax.sharding import PartitionSpec as P

GRID = 24


EPSILON = 1e-06
NEGATIVE = -1e30
ROOT_HALF = 0.7071067811865476
GAUSS_NORM = 0.3989422804014327


def passed_along(value, axis, steps):
    count = lax.axis_size(axis)
    pairs = [(source, (source + steps) % count) for source in range(count)]
    return lax.ppermute(value, axis, pairs)


def gap_onehot():
    span_width = 2 * GRID - 1
    grid_ids = jnp.arange(GRID, dtype=jnp.int32)
    gaps = grid_ids[:, None, None] - grid_ids[None, :, None] + GRID - 1
    return (gaps == jnp.arange(span_width, dtype=jnp.int32)[None, None, :]).astype(jnp.float32)


def bias_full(rel_table, all_slots):
    highest = lax.Precision.HIGHEST
    span_width = 2 * GRID - 1
    far_index = span_width * span_width
    cells = GRID * GRID
    head_count = rel_table.shape[1]
    spare = all_slots - 1 - cells
    selector = gap_onehot()
    patch_table = rel_table[0:far_index].reshape(span_width, span_width, head_count)
    row_pick = jnp.einsum("pqa,abh->pqbh", selector, patch_table, precision=highest)
    spread = jnp.einsum("pqbh,rsb->hprqs", row_pick, selector, precision=highest)
    patch_bias = spread.reshape(head_count, cells, cells)
    patch_bias = jnp.concatenate(
        [
            patch_bias,
            jnp.broadcast_to(patch_bias[:, cells - 1 : cells, :], (head_count, spare, cells)),
        ],
        axis=1,
    )
    patch_bias = jnp.concatenate(
        [
            patch_bias,
            jnp.broadcast_to(
                patch_bias[:, :, cells - 1 : cells], (head_count, cells + spare, spare)
            ),
        ],
        axis=2,
    )
    top_row = jnp.broadcast_to(rel_table[far_index][:, None, None], (head_count, 1, all_slots - 1))
    left_col = jnp.broadcast_to(
        rel_table[far_index + 1][:, None, None], (head_count, all_slots - 1, 1)
    )
    corner = rel_table[far_index + 2][:, None, None]
    upper = jnp.concatenate([corner, top_row], axis=2)
    lower = jnp.concatenate([left_col, patch_bias], axis=2)
    return jnp.concatenate([upper, lower], axis=1)


def table_back(grad_full):
    highest = lax.Precision.HIGHEST
    span_width = 2 * GRID - 1
    cells = GRID * GRID
    head_count = grad_full.shape[0]
    corner = grad_full[:, 0, 0]
    far_grad = jnp.sum(grad_full[:, 0, 1:], axis=1)
    near_grad = jnp.sum(grad_full[:, 1:, 0], axis=1)
    patch_grad = grad_full[:, 1:, 1:]
    patch_grad = jnp.concatenate(
        [
            patch_grad[:, 0 : cells - 1, :],
            jnp.sum(patch_grad[:, cells - 1 :, :], axis=1, keepdims=True),
        ],
        axis=1,
    )
    patch_grad = jnp.concatenate(
        [
            patch_grad[:, :, 0 : cells - 1],
            jnp.sum(patch_grad[:, :, cells - 1 :], axis=2, keepdims=True),
        ],
        axis=2,
    )
    selector = gap_onehot()
    spread = patch_grad.reshape(head_count, GRID, GRID, GRID, GRID)
    row_sums = jnp.einsum("hprqs,rsb->pqbh", spread, selector, precision=highest)
    patch_table = jnp.einsum("pqa,pqbh->abh", selector, row_sums, precision=highest)
    tail = jnp.stack([far_grad, near_grad, corner], axis=0)
    return jnp.concatenate([patch_table.reshape(span_width * span_width, head_count), tail], axis=0)


def gelu_value(argument):
    return 0.5 * argument * (1.0 + lax.erf(argument * ROOT_HALF))


def gelu_slope(argument):
    return (
        0.5 * (1.0 + lax.erf(argument * ROOT_HALF))
        + argument * jnp.exp(-0.5 * argument * argument) * GAUSS_NORM
    )


def normalize(values, gain, shift):
    center = values - jnp.mean(values, axis=-1, keepdims=True)
    inverse = lax.rsqrt(jnp.mean(center * center, axis=-1, keepdims=True) + EPSILON)
    normed = center * inverse
    return (normed * gain + shift, normed, inverse)


def normalize_back(grad_out, normed, inverse, gain):
    signal = grad_out * gain
    inner = (
        signal
        - jnp.mean(signal, axis=-1, keepdims=True)
        - normed * jnp.mean(signal * normed, axis=-1, keepdims=True)
    )
    return (inverse * inner, jnp.sum(grad_out * normed, axis=0), jnp.sum(grad_out, axis=0))


def general_body(
    tokens,
    masked,
    out_grad,
    norm1_gain,
    norm1_bias,
    qkv_weight,
    query_bias,
    value_bias,
    rel_table,
    proj_weight,
    proj_bias,
    scale1,
    norm2_gain,
    norm2_bias,
    fc1_weight,
    fc1_bias,
    fc2_weight,
    fc2_bias,
    scale2,
):
    images, local_rows, model_width = tokens.shape
    head_count = rel_table.shape[1]
    head_size = model_width // head_count
    head_scale = head_size ** (-0.5)
    cycle_size = lax.axis_size("seq")
    position = lax.axis_index("seq")
    all_slots = local_rows * cycle_size
    key_pos = jnp.arange(all_slots, dtype=jnp.int32)
    position_bias = lax.dynamic_slice_in_dim(
        bias_full(rel_table, all_slots), position * local_rows, local_rows, 1
    )
    key_valid = key_pos <= GRID * GRID
    flat_rows = images * local_rows
    head_shape = (images, local_rows, head_count, head_size)
    inputs = tokens.astype(jnp.float32).reshape(flat_rows, model_width)
    normed1, centred1, inverse1 = normalize(inputs, norm1_gain, norm1_bias)
    hidden1 = normed1.astype(jnp.bfloat16)
    projected = jnp.dot(hidden1, qkv_weight, preferred_element_type=jnp.float32)
    queries = ((projected[:, 0:model_width] + query_bias) * head_scale).astype(jnp.bfloat16)
    keys_local = (
        projected[:, model_width : 2 * model_width]
        .astype(jnp.bfloat16)
        .reshape(images, local_rows, model_width)
    )
    values_local = (
        (projected[:, 2 * model_width :] + value_bias)
        .astype(jnp.bfloat16)
        .reshape(images, local_rows, model_width)
    )
    query_heads = queries.reshape(head_shape)

    def block_scores(key_block, offset):
        key_count = key_block.shape[1]
        key_heads = key_block.reshape(images, key_count, head_count, head_size)
        logits = jnp.einsum(
            "gqhd,gkhd->ghqk", query_heads, key_heads, preferred_element_type=jnp.float32
        )
        logits = logits + lax.dynamic_slice_in_dim(position_bias, offset, key_count, 2)[None]
        usable = lax.dynamic_slice_in_dim(key_valid, offset, key_count, 0)
        return (jnp.where(usable, logits, NEGATIVE), usable)

    row_max = jnp.full((images, head_count, local_rows), NEGATIVE, jnp.float32)
    key_block = lax.all_gather(keys_local, "seq", axis=1, tiled=True)
    value_block = lax.all_gather(values_local, "seq", axis=1, tiled=True)
    key_count = key_block.shape[1]
    scores, usable = block_scores(key_block, jnp.int32(0))
    new_max = jnp.maximum(row_max, jnp.max(scores, axis=-1))
    weights = jnp.where(usable, jnp.exp(scores - new_max[..., None]), 0.0)
    totals = jnp.sum(weights, axis=-1)
    value_heads = value_block.reshape(images, key_count, head_count, head_size)
    update = jnp.einsum(
        "ghqk,gkhd->gqhd",
        weights.astype(jnp.bfloat16),
        value_heads,
        preferred_element_type=jnp.float32,
    )
    weighted = update
    row_max, totals, weighted = (new_max, totals, weighted)
    log_total = row_max + jnp.log(totals)
    attended = weighted / jnp.transpose(totals, (0, 2, 1))[..., None]
    attn_low = attended.reshape(flat_rows, model_width).astype(jnp.bfloat16)
    mixed_out = jnp.dot(attn_low, proj_weight, preferred_element_type=jnp.float32) + proj_bias
    residual1 = inputs + scale1 * mixed_out
    normed2, centred2, inverse2 = normalize(residual1, norm2_gain, norm2_bias)
    hidden2 = normed2.astype(jnp.bfloat16)
    pre_act = jnp.dot(hidden2, fc1_weight, preferred_element_type=jnp.float32) + fc1_bias
    activated = gelu_value(pre_act).astype(jnp.bfloat16)
    ffn_out = jnp.dot(activated, fc2_weight, preferred_element_type=jnp.float32) + fc2_bias
    result = (residual1 + scale2 * ffn_out).astype(jnp.bfloat16).reshape(tokens.shape)
    cotangent = (out_grad.astype(jnp.float32) * masked.astype(jnp.float32)[..., None]).reshape(
        flat_rows, model_width
    )
    d_ffn = (scale2 * cotangent).astype(jnp.bfloat16)
    scale2_grad = jnp.sum(cotangent * ffn_out, axis=0)
    fc2_bias_grad = jnp.sum(d_ffn.astype(jnp.float32), axis=0)
    fc2_weight_grad = jnp.einsum("nf,nd->fd", activated, d_ffn, preferred_element_type=jnp.float32)
    d_act = jnp.einsum("nd,fd->nf", d_ffn, fc2_weight, preferred_element_type=jnp.float32)
    d_pre = (d_act * gelu_slope(pre_act)).astype(jnp.bfloat16)
    fc1_bias_grad = jnp.sum(d_pre.astype(jnp.float32), axis=0)
    fc1_weight_grad = jnp.einsum("nd,nf->df", hidden2, d_pre, preferred_element_type=jnp.float32)
    d_hidden2 = jnp.einsum("nf,df->nd", d_pre, fc1_weight, preferred_element_type=jnp.float32)
    back_two, norm2_gain_grad, norm2_bias_grad = normalize_back(
        d_hidden2, centred2, inverse2, norm2_gain
    )
    d_resid1 = cotangent + back_two
    d_mixed = (scale1 * d_resid1).astype(jnp.bfloat16)
    scale1_grad = jnp.sum(d_resid1 * mixed_out, axis=0)
    proj_bias_grad = jnp.sum(d_mixed.astype(jnp.float32), axis=0)
    proj_weight_grad = jnp.einsum(
        "nc,nd->cd", attn_low, d_mixed, preferred_element_type=jnp.float32
    )
    d_attn = jnp.einsum(
        "nd,cd->nc", d_mixed, proj_weight, preferred_element_type=jnp.float32
    ).astype(jnp.bfloat16)
    d_attn_heads = d_attn.reshape(head_shape)
    row_delta = jnp.transpose(
        jnp.sum(d_attn_heads.astype(jnp.float32) * attended, axis=-1), (0, 2, 1)
    )

    def back_block(key_block, value_block, offset):
        key_count = key_block.shape[1]
        scores, usable = block_scores(key_block, offset)
        prob_full = jnp.where(usable, jnp.exp(scores - log_total[..., None]), 0.0)
        prob_low = prob_full.astype(jnp.bfloat16)
        key_heads = key_block.reshape(images, key_count, head_count, head_size)
        value_heads = value_block.reshape(images, key_count, head_count, head_size)
        d_value = jnp.einsum(
            "ghqk,gqhd->gkhd", prob_low, d_attn_heads, preferred_element_type=jnp.float32
        )
        d_probs = jnp.einsum(
            "gqhd,gkhd->ghqk", d_attn_heads, value_heads, preferred_element_type=jnp.float32
        )
        d_scores = (prob_full * (d_probs - row_delta[..., None])).astype(jnp.bfloat16)
        d_query = jnp.einsum(
            "ghqk,gkhd->gqhd", d_scores, key_heads, preferred_element_type=jnp.float32
        )
        d_key = jnp.einsum(
            "ghqk,gqhd->gkhd", d_scores, query_heads, preferred_element_type=jnp.float32
        )
        table_part = jnp.sum(d_scores.astype(jnp.float32), axis=0)
        return (
            d_query,
            d_key.reshape(images, key_count, model_width),
            d_value.reshape(images, key_count, model_width),
            table_part,
        )

    def turn_grads(grad_pair):
        return (
            passed_along(grad_pair[0].astype(jnp.bfloat16), "seq", 1).astype(jnp.float32),
            passed_along(grad_pair[1].astype(jnp.bfloat16), "seq", 1).astype(jnp.float32),
        )

    def cycle_step(turn_index, cycle_state):
        key_block, value_block, d_key_acc, d_value_acc, d_query_acc, table_acc = cycle_state
        owner_rank = (position - turn_index) % cycle_size
        offset = owner_rank * local_rows
        d_query, d_key, d_value, table_part = back_block(key_block, value_block, offset)
        table_acc = lax.dynamic_update_slice_in_dim(table_acc, table_part, offset, 2)
        d_key_acc, d_value_acc = turn_grads((d_key_acc + d_key, d_value_acc + d_value))
        key_block, value_block = passed_along((key_block, value_block), "seq", 1)
        return (key_block, value_block, d_key_acc, d_value_acc, d_query_acc + d_query, table_acc)

    kv_zeros = jnp.zeros((images, local_rows, model_width), jnp.float32)
    initial = (
        keys_local,
        values_local,
        kv_zeros,
        kv_zeros,
        jnp.zeros(head_shape, jnp.float32),
        jnp.zeros((head_count, local_rows, all_slots), jnp.float32),
    )
    cycle_state = lax.fori_loop(0, cycle_size - 1, cycle_step, initial)
    key_block, value_block, d_key_acc, d_value_acc, d_query_acc, table_acc = cycle_state
    offset = (position + 1) % cycle_size * local_rows
    d_query, d_key, d_value, table_part = back_block(key_block, value_block, offset)
    table_acc = lax.dynamic_update_slice_in_dim(table_acc, table_part, offset, 2)
    d_key_all, d_value_all = turn_grads((d_key_acc + d_key, d_value_acc + d_value))
    d_query_all = d_query_acc + d_query
    d_query_low = d_query_all.reshape(flat_rows, model_width).astype(jnp.bfloat16) * head_scale
    d_key_low = d_key_all.reshape(flat_rows, model_width).astype(jnp.bfloat16)
    d_value_low = d_value_all.reshape(flat_rows, model_width).astype(jnp.bfloat16)
    d_qkv = jnp.concatenate([d_query_low, d_key_low, d_value_low], axis=1)
    qkv_weight_grad = jnp.einsum("nd,ne->de", hidden1, d_qkv, preferred_element_type=jnp.float32)
    query_bias_grad = jnp.sum(d_query_low.astype(jnp.float32), axis=0)
    value_bias_grad = jnp.sum(d_value_low.astype(jnp.float32), axis=0)
    d_hidden1 = jnp.einsum("ne,de->nd", d_qkv, qkv_weight, preferred_element_type=jnp.float32)
    back_one, norm1_gain_grad, norm1_bias_grad = normalize_back(
        d_hidden1, centred1, inverse1, norm1_gain
    )
    tokens_grad = (d_resid1 + back_one).astype(jnp.bfloat16).reshape(tokens.shape)
    grad_square = lax.dynamic_update_slice_in_dim(
        jnp.zeros((head_count, all_slots, all_slots), jnp.float32),
        table_acc,
        position * local_rows,
        1,
    )
    table_grad = table_back(grad_square)
    half_summed = (
        lax.psum_scatter(
            qkv_weight_grad.astype(jnp.bfloat16), "img", scatter_dimension=0, tiled=True
        ).astype(jnp.float32),
        lax.psum_scatter(
            proj_weight_grad.astype(jnp.bfloat16), "img", scatter_dimension=0, tiled=True
        ).astype(jnp.float32),
        lax.psum_scatter(
            fc1_weight_grad.astype(jnp.bfloat16), "img", scatter_dimension=0, tiled=True
        ).astype(jnp.float32),
        lax.psum_scatter(
            fc2_weight_grad.astype(jnp.bfloat16), "img", scatter_dimension=0, tiled=True
        ).astype(jnp.float32),
    )
    summed = (
        lax.psum_scatter(
            half_summed[0].astype(jnp.bfloat16), "seq", scatter_dimension=1, tiled=True
        ).astype(jnp.float32),
        lax.psum_scatter(
            half_summed[1].astype(jnp.bfloat16), "seq", scatter_dimension=1, tiled=True
        ).astype(jnp.float32),
        lax.psum_scatter(
            half_summed[2].astype(jnp.bfloat16), "seq", scatter_dimension=1, tiled=True
        ).astype(jnp.float32),
        lax.psum_scatter(
            half_summed[3].astype(jnp.bfloat16), "seq", scatter_dimension=1, tiled=True
        ).astype(jnp.float32),
    )
    smalls = lax.psum(
        (
            table_grad,
            norm1_gain_grad,
            norm1_bias_grad,
            query_bias_grad,
            value_bias_grad,
            proj_bias_grad,
            scale1_grad,
            norm2_gain_grad,
            norm2_bias_grad,
            fc1_bias_grad,
            fc2_bias_grad,
            scale2_grad,
        ),
        ("img", "seq"),
    )
    return (
        result,
        tokens_grad,
        smalls[1],
        smalls[2],
        summed[0],
        smalls[3],
        smalls[4],
        smalls[0],
        summed[1],
        smalls[5],
        smalls[6],
        smalls[7],
        smalls[8],
        summed[2],
        smalls[9],
        summed[3],
        smalls[10],
        smalls[11],
    )


LANES = 128
RATE = 1.15e9
STRIP = 24
STRIP_WIDTH = 1280
MEGA = 1 << 20
NT = (((1,), (1,)), ((), ()))
TN = (((0,), (0,)), ((), ()))
NN = (((1,), (0,)), ((), ()))
BF = jnp.bfloat16
F32 = jnp.float32


def mul(left, right, dims=NN):
    return lax.dot_general(left, right, dims, preferred_element_type=F32)


def bits_of(img, seq):
    line = img >> 2
    return {"core": img & 1, "x": (img >> 1) & 1, "z1": line & 1, "z2": line >> 1, "y": seq}


def label_of(img, seq, order):
    bits = bits_of(img, seq)
    total = 0
    for name in order:
        total = total * 2 + bits[name]
    return total


def swap_pairs(*names):
    order = ("core", "x", "z1", "z2", "y")
    where = {label_of(img, seq, order): img * 2 + seq for img in range(16) for seq in range(2)}
    flip = sum(1 << (len(order) - 1 - order.index(name)) for name in names)
    return [(device, where[label ^ flip]) for label, device in where.items()]


def swapped(value, *names):
    return lax.ppermute(value, ("img", "seq"), swap_pairs(*names))


def added(terms):
    return sum(term[0].astype(F32) for term in terms)


def layer_norm(values):
    center = values - jnp.mean(values, axis=-1, keepdims=True)
    inverse = lax.rsqrt(jnp.mean(center * center, axis=-1, keepdims=True) + EPSILON)
    return center * inverse, inverse


def layer_norm_back(grad_out, normed, inverse, gain):
    signal = grad_out * gain
    return inverse * (
        signal
        - jnp.mean(signal, axis=-1, keepdims=True)
        - normed * jnp.mean(signal * normed, axis=-1, keepdims=True)
    )


def spec(block, index):
    return pl.BlockSpec(block, index)


def full(shape):
    zeros = (0,) * len(shape)
    return pl.BlockSpec(shape, lambda *_: zeros, pipeline_mode=pl.Buffered(1))


SIZES = {
    "strips_kernel": (1.7, 5),
    "qkv_kernel": (1.9, 10),
    "attend_kernel": (9.0, 42),
    "ffn_kernel": (5.5, 16),
    "ffn_back_kernel": (4.5, 14),
    "d_act_kernel": (2.5, 12),
    "fc2_grad_kernel": (4.6, 14),
    "fc1_grad_kernel": (5.5, 14),
    "attend_back_kernel": (4.4, 14),
    "hidden1_grad_kernel": (4.2, 12),
    "join_kernel": (1.0, 12),
    "qkv_grad_kernel": (3.2, 12),
    "result_kernel": (40.0, 10),
    "tokens_grad_kernel": (2.0, 10),
}


def run(kernel, place, grid, in_specs, out_specs, out_shapes, scratch, operands, flops, after=(), us=None, reuse=()):
    held = len(operands)
    inner = kernel
    cost, vmem = SIZES.get(getattr(kernel, "func", kernel).__name__, (0.01, 10))
    us = us or cost

    def kernel(place_ref, *refs):
        inner(place_ref, *refs[:held], *refs[held + len(after) :])

    in_specs = [*in_specs, *[pl.BlockSpec(memory_space=pl.ANY)] * len(after)]
    return pl.pallas_call(
        kernel,
        grid_spec=pltpu.PrefetchScalarGridSpec(
            num_scalar_prefetch=1,
            grid=grid,
            in_specs=in_specs,
            out_specs=out_specs,
            scratch_shapes=scratch,
        ),
        out_shape=out_shapes,
        input_output_aliases={1 + held + i: o for i, o in reuse},
        compiler_params=pltpu.CompilerParams(vmem_limit_bytes=vmem * MEGA),
        cost_estimate=pl.CostEstimate(flops=int(us * RATE), bytes_accessed=1, transcendentals=0),
    )(place, *operands, *after)


def add_kernel(place, *refs):
    refs[-1][...] = sum(ref[...].astype(F32) for ref in refs[:-1]).astype(BF)


def half_sum(place, terms, side, after=(), column=0, columns=None):
    size = terms[-1].shape[0] // 2
    _, height, columns = (*terms[0].shape[:2], columns or terms[0].shape[2])
    block = (min(size, 4), height, columns)
    count = size // block[0]
    return run(
        add_kernel, place, (count,),
        [spec(block, lambda n, p: (n + side * count, 0, column))] * len(terms),
        [spec(block, lambda n, p: (n, 0, 0))], [shape((size, *block[1:]), BF)], [], tuple(terms), 0,
        after=after,
    )[0]


def half_out(place, terms, after=(), **how):
    return half_sum(place, terms, 1, after, **how)


def join_kernel(place, *refs):
    cut = refs[0].shape[1]
    for n, out in enumerate(refs[-2:]):
        six = [ref[...].astype(F32) for ref in refs[6 * n : 6 * n + 6]]
        out[:, :cut, :] = (six[0] + six[1] + six[2]).astype(BF)
        out[:, cut:, :] = (six[3] + six[4] + six[5]).astype(BF)


def joined_halves(place, terms, others, after=()):
    line, _, _, high, wide = terms[0].shape
    low = others[-1].shape[1]
    total = (line, high + low, wide)
    specs = []
    for side in (1, 0):
        cube = spec((line, None, None, high, wide), lambda n, p, side=side: (0, 0, side, 0, 0))
        specs += [cube, cube, spec((line, high, wide), lambda n, p, side=side: (side, 0, 0))]
        under = spec((line, low, wide), lambda n, p, side=side: (side, 0, 4))
        specs += [under, under, spec((line, low, wide), lambda n, p, side=side: (side, 0, 0))]
    return run(
        join_kernel, place, (1,), specs, [full(total)] * 2, [shape(total, BF)] * 2, [],
        (*terms, *others) * 2, 0, after=after,
    )


def x_part(place, terms, side, after=()):
    line, _, seqs, *block = terms[0].shape
    return run(
        add_kernel, place, (line,),
        [spec((None, None, seqs, *block), lambda n, p: (n, side, 0, 0, 0))] * len(terms),
        [spec((seqs, None, *block), lambda n, p: (0, n, 0, 0))], [shape((seqs, line, *block), BF)], [],
        tuple(terms), 0, after=after,
    )[0].reshape(line * seqs, *block)


NOTE = (32, 1024)


def note_sum(left, right):
    return (left.astype(F32) + right.astype(F32)).astype(BF)


def qs_first_kernel(place, keep, recv, note, mate, send_out, rest_out):
    count, height, _ = keep.shape
    half = count // 2
    total = note_sum(note[...], mate[...])
    for out, base in ((send_out, half), (rest_out, 0)):
        for n in range(half):
            out[height * n : height * (n + 1), :] = note_sum(keep[base + n], recv[base + n])
        out[height * half :, :] = jnp.zeros((NOTE[0], out.shape[1]), BF)
        out[height * half :, : NOTE[1]] = total


def qs_next_kernel(place, keep, recv, send_out, rest_out):
    part = send_out.shape[0] - NOTE[0]
    total = note_sum(keep[...], recv[...])
    for out, base in ((send_out, part), (rest_out, 0)):
        out[:part, :] = total[base : base + part, :]
        out[part:, :] = total[2 * part :, :]


def qs_last_kernel(place, keep, recv, keep_out, line_out, side_out, cross_out, note_out, total):
    share = side_out.shape[1]
    height = side_out.shape[0]
    stay = pl.ds(pl.multiple_of(place[0] * share, LANES), 2 * share)
    leave = pl.ds(pl.multiple_of((1 - place[0]) * 2 * share, LANES), share)
    total[...] = keep[...].astype(F32) + recv[...].astype(F32)
    keep_out[...] = total[:height, stay]
    side_out[...] = total[:height, leave].astype(BF)
    cross_out[...] = total[height : 2 * height, leave].astype(BF)
    note = total[2 * height :, : NOTE[1]].astype(BF)
    note_out[...] = note
    line_out[...] = jnp.zeros_like(line_out)
    line_out[:height, : 2 * share] = total[height : 2 * height, stay].astype(BF)
    line_out[height:, :] = note


def qs_join_kernel(place, keep, line, side, cross, note, out, note_out):
    height, share = side.shape
    both = keep[...] + line[:height, : 2 * share].astype(F32)
    out[:, :share] = both[:, :share]
    out[:, share : 2 * share] = side[...].astype(F32) + cross[...].astype(F32)
    out[:, 2 * share :] = both[:, share:]
    note_out[...] = note_sum(note[...], line[height:, :])


def shape(dims, dtype):
    return jax.ShapeDtypeStruct(dims, dtype)


def qkv_kernel(place, source, vecs, weight, qb, vb, qkv_out, hidden_out):
    step = pl.program_id(0)

    @pl.when(step == 0)
    def _():
        normed, _ = layer_norm(source[...].astype(F32))
        hidden_out[...] = (normed * vecs[0:1, :] + vecs[1:2, :]).astype(BF)

    wide = mul(hidden_out[...], weight[...])
    shift = jnp.where(step == 0, qb[...], jnp.where(step == 2, vb[...], 0.0))
    factor = jnp.where(step == 0, 0.125, 1.0)
    qkv_out[0] = ((wide + shift) * factor).astype(BF)


def window(strip, block):
    off = (STRIP - block) * STRIP
    base = off // LANES * LANES
    held = strip[:, base : base + 6 * LANES]
    if off - base:
        held = pltpu.roll(held, 6 * LANES - (off - base), axis=1)
    return held[:, : 5 * LANES]


FORWARD_CHUNKS = ((0, 288), (288, 288), (576, 64))
CHUNKS = tuple((start * 144, 144) for start in range(4)) + ((576, 64),)


def attend_kernel(place, qkv, strips, even_mask, own_out, send_out, expo_out, inv_out, strip, attended):
    slots = qkv.shape[1]
    half = slots // 2
    side = place[0]
    lane = lax.broadcasted_iota(jnp.int32, (1, LANES), 1)
    first = lane < LANES // 2
    masks = (jnp.where(first, 1.0, 0.0).astype(BF), jnp.where(first, 0.0, 1.0).astype(BF))
    keys = [qkv[1] * m for m in masks]
    values = [qkv[2] * m for m in masks]
    picks = even_mask[...] > 0.5
    at = side * 6 + 2 * pl.program_id(0)
    for head in range(2):
        rolled = [
            pltpu.roll(
                jnp.broadcast_to(strips[at + head, par : par + 1, :], (STRIP, STRIP_WIDTH)),
                1,
                axis=1,
                stride=1,
                stride_axis=0,
            )
            for par in range(2)
        ]
        strip[head] = jnp.where(picks, rolled[0], rolled[1])
    block_lane = lax.broadcasted_iota(jnp.int32, (STRIP, LANES), 1)
    block_row = lax.broadcasted_iota(jnp.int32, (STRIP, LANES), 0)
    for start, count in FORWARD_CHUNKS:
        query = qkv[0, start : start + count, :]
        total = None
        scale = None
        for head in range(2):
            lone = strips[at + head, 0:1, 1152:1280]
            far = lone[:, 0:1]
            near = lone[:, 1:2]
            corner = lone[:, 2:3]
            biases = []
            for block in range(start // STRIP, min(start + count, 576) // STRIP):
                piece = window(strip.at[head], block)
                left = jnp.where(block_lane == 0, near, piece[:, :LANES])
                middle = piece[:, LANES : 4 * LANES]
                right = piece[:, 4 * LANES :]
                if block == 0:
                    top_row = block_row == 0
                    left = jnp.where(top_row, jnp.where(block_lane == 0, corner, far), left)
                    middle = jnp.concatenate(
                        [
                            jnp.where(top_row, far, middle[:, n * LANES : (n + 1) * LANES])
                            for n in range(3)
                        ],
                        axis=1,
                    )
                    right = jnp.where(top_row, far, right)
                right = jnp.where(block_lane > 64, NEGATIVE, right)
                biases.append(jnp.concatenate([left, middle, right], axis=1))
            if start + count > 576:
                row = window(strip.at[head, 0:8, :], STRIP)[0:1, :]
                row = jnp.concatenate(
                    [
                        jnp.where(lane == 0, near, row[:, :LANES]),
                        row[:, LANES : 4 * LANES],
                        jnp.where(lane > 64, NEGATIVE, row[:, 4 * LANES :]),
                    ],
                    axis=1,
                )
                biases.append(jnp.broadcast_to(row, (start + count - 576, 5 * LANES)))
            scores = mul(query, keys[head], NT) + jnp.concatenate(biases, axis=0)
            top = jnp.max(scores, axis=1, keepdims=True)
            expo = jnp.exp(scores - top)
            inverse = 1.0 / jnp.sum(expo, axis=1, keepdims=True)
            low = expo.astype(BF)
            expo_out[head, start : start + count, :] = low
            part = mul(low, values[head]) * inverse
            total = part if head == 0 else total + part
            spread = jnp.broadcast_to(inverse, (count, LANES))
            scale = spread if head == 0 else jnp.where(first, scale, spread)
        attended[start : start + count, :] = total
        inv_out[start : start + count, :] = scale
    own_out[...] = attended[pl.ds(pl.multiple_of(side * half, 64), half), :].astype(BF)
    send_out[...] = attended[pl.ds(pl.multiple_of((1 - side) * half, 64), half), :].astype(BF)


def attend_back_kernel(
    place, qkv, expo, attn_own, attn_send, grad_own, grad_other, inv, even_mask,
    dqkv_out, strip_out, grad_all, attn_all, d_scores, strip, dq_all,
):
    slots = qkv.shape[1]
    half = slots // 2
    here = pl.ds(pl.multiple_of(place[0] * half, 64), half)
    there = pl.ds(pl.multiple_of((1 - place[0]) * half, 64), half)
    lane = lax.broadcasted_iota(jnp.int32, (1, LANES), 1)
    first = lane < LANES // 2
    masks = (jnp.where(first, 1.0, 0.0).astype(BF), jnp.where(first, 0.0, 1.0).astype(BF))
    scaled = grad_own[...].astype(F32) * inv[here, :]
    grad_all[here, :] = scaled
    attn_all[here, :] = scaled * attn_own[...].astype(F32)
    scaled = grad_other[...].astype(F32) * inv[there, :]
    grad_all[there, :] = scaled
    attn_all[there, :] = scaled * attn_send[...].astype(F32)
    keys = [qkv[1] * m for m in masks]
    values = [qkv[2] * m for m in masks]
    block_lane = lax.broadcasted_iota(jnp.int32, (STRIP, LANES), 1)
    block_row = lax.broadcasted_iota(jnp.int32, (STRIP, LANES), 0)
    strip[...] = jnp.zeros_like(strip)
    columns = [jnp.zeros((8, LANES), F32) for _ in range(2)]
    tops = [None, None]
    zeros = jnp.zeros((STRIP, LANES), F32)
    for start, count in CHUNKS:
        grads = grad_all[start : start + count, :].astype(BF)
        products = attn_all[start : start + count, :]
        total = None
        for head in range(2):
            chosen = first if head == 0 else jnp.logical_not(first)
            delta = jnp.sum(jnp.where(chosen, products, 0.0), axis=1, keepdims=True)
            d_probs = mul(grads, values[head], NT)
            d_score = expo[head, start : start + count, :].astype(F32) * (d_probs - delta)
            low = d_score.astype(BF)
            d_scores[head, start : start + count, :] = low
            part = mul(low, keys[head])
            total = part if head == 0 else total + part
            if start == 576:
                for tile in range(count // 8):
                    columns[head] = columns[head] + d_score[8 * tile : 8 * tile + 8, :LANES]
                line = jnp.sum(d_score, axis=0, keepdims=True)
                line = jnp.concatenate([jnp.where(lane == 0, 0.0, line[:, :LANES]), line[:, LANES:]], axis=1)
                strip[head, 0:1, : 5 * LANES] = strip[head, 0:1, : 5 * LANES] + line
            else:
                for block in range(start // STRIP, (start + count) // STRIP):
                    at = block * STRIP - start
                    piece = d_score[at : at + STRIP, :]
                    left = piece[:, :LANES]
                    rest = piece[:, LANES:]
                    if block == 0:
                        tops[head] = piece[0:1, :]
                        left = jnp.where(block_row == 0, 0.0, left)
                        rest = jnp.concatenate(
                            [
                                jnp.where(block_row == 0, 0.0, rest[:, n * LANES : (n + 1) * LANES])
                                for n in range(4)
                            ],
                            axis=1,
                        )
                    columns[head] = columns[head] + left[0:8] + left[8:16] + left[16:24]
                    piece = jnp.concatenate(
                        [jnp.where(block_lane == 0, 0.0, left), rest, zeros], axis=1
                    )
                    off = (STRIP - block) * STRIP
                    base = off // LANES * LANES
                    if off - base:
                        piece = pltpu.roll(piece, off - base, axis=1)
                    strip[head, :, base : base + 6 * LANES] = (
                        strip[head, :, base : base + 6 * LANES] + piece
                    )
        dq_all[start : start + count, :] = total
    dqkv_out[0] = dq_all[...].astype(BF) * BF(0.125)
    turned_query = qkv[0].astype(F32).T.astype(BF)
    turned_grads = grad_all[...].T.astype(BF)
    half_lanes = LANES // 2
    for at, left, right in ((1, turned_query, d_scores), (2, turned_grads, expo)):
        sides = [
            mul(left[half_lanes * head : half_lanes * (head + 1), :], right[head])
            for head in range(2)
        ]
        dqkv_out[at] = jnp.concatenate(sides, axis=0).T.astype(BF)
    picks = even_mask[...] > 0.5
    row_id = lax.broadcasted_iota(jnp.int32, (STRIP, STRIP_WIDTH), 0)
    wide_lane = lax.broadcasted_iota(jnp.int32, (1, STRIP_WIDTH), 1)
    for head in range(2):
        held = strip[head]
        lines = []
        for par in range(2):
            part = jnp.where(picks, held, 0.0) if par == 0 else jnp.where(picks, 0.0, held)
            part = pltpu.roll(part, STRIP_WIDTH - 1, axis=1)
            for bit in (1, 2, 4, 8, 16):
                part = jnp.where(
                    (row_id & bit) > 0, pltpu.roll(part, STRIP_WIDTH - bit, axis=1), part
                )
            lines.append(jnp.sum(part, axis=0, keepdims=True))
        near = jnp.sum(jnp.where(lane == 0, columns[head], 0.0)).reshape(1, 1)
        corner = tops[head][:, 0:1]
        far = jnp.sum(tops[head], axis=1, keepdims=True) - corner
        line = lines[0]
        line = jnp.where(wide_lane >= 1152, 0.0, line)
        line = jnp.where(wide_lane == 1152, far, line)
        line = jnp.where(wide_lane == 1153, near, line)
        line = jnp.where(wide_lane == 1154, corner, line)
        strip_out[0, head, 0:1, :] = line
        strip_out[0, head, 1:2, :] = lines[1]


def d_act_kernel(place, cot, vecs, fc2, d_ffn_out, d_act_out):
    @pl.when(pl.program_id(0) == 0)
    def _():
        d_ffn_out[...] = (vecs[7:8, :] * cot[...].astype(F32)).astype(BF)

    d_act_out[...] = mul(d_ffn_out[...], fc2[...], NT).astype(BF)


def ffn_kernel(
    place, tokens, attn_own, attn_other, vecs, proj, fc1, fc1_bias, d_act,
    act_out, d_pre_out, fc1_bias_out, hidden_out, resid_out, attn_out, mixed_out,
):
    width = attn_own.shape[1]

    @pl.when(pl.program_id(0) == 0)
    def _():
        attn_out[:, pl.ds(pl.multiple_of(place[0] * width, LANES), width)] = attn_own[...]
        attn_out[:, pl.ds(pl.multiple_of((1 - place[0]) * width, LANES), width)] = attn_other[...]
        mixed = mul(attn_out[...], proj[...]) + vecs[2:3, :]
        mixed_out[...] = mixed
        resid = tokens[...].astype(F32) + vecs[3:4, :] * mixed
        resid_out[...] = resid
        normed, _ = layer_norm(resid)
        hidden_out[...] = (normed * vecs[4:5, :] + vecs[5:6, :]).astype(BF)

    pre = mul(hidden_out[...], fc1[...]) + fc1_bias[...]
    gate = 0.5 * (1.0 + lax.erf(pre * ROOT_HALF))
    act_out[...] = (pre * gate).astype(BF)
    slope = gate + pre * jnp.exp(-0.5 * pre * pre) * GAUSS_NORM
    d_pre = (d_act[...].astype(F32) * slope).astype(BF)
    d_pre_out[...] = d_pre
    fc1_bias_out[...] = jnp.sum(d_pre.astype(F32), axis=0, keepdims=True)


def ffn_back_kernel(
    place, d_pre, fc1, cot, d_ffn, resid, mixed_in, vecs, proj_own, proj_other,
    d_mixed_out, d_resid_out, grad_own_out, grad_send_out, small_out, d_hidden,
):
    step = pl.program_id(0)
    part = mul(d_pre[...], fc1[...], NT)

    @pl.when(step == 0)
    def _():
        d_hidden[...] = part

    @pl.when(step > 0)
    def _():
        d_hidden[...] += part

    @pl.when(step == pl.num_programs(0) - 1)
    def _():
        grad = d_hidden[...]
        mixed = mixed_in[...]
        normed, inverse = layer_norm(resid[...])
        d_resid = cot[...].astype(F32) + layer_norm_back(grad, normed, inverse, vecs[4:5, :])
        d_resid_out[...] = d_resid
        d_mixed = (vecs[3:4, :] * d_resid).astype(BF)
        d_mixed_out[...] = d_mixed
        grad_send_out[...] = mul(d_mixed, proj_other[...], NT).astype(BF)
        grad_own_out[...] = mul(d_mixed, proj_own[...], NT).astype(BF)
        small_out[0:1, :] = jnp.sum(grad * normed, axis=0, keepdims=True)
        small_out[1:2, :] = jnp.sum(grad, axis=0, keepdims=True)
        small_out[2:3, :] = jnp.sum(d_resid * mixed, axis=0, keepdims=True)
        small_out[3:4, :] = jnp.sum(d_mixed.astype(F32), axis=0, keepdims=True)
        small_out[4:5, :] = jnp.sum(d_ffn[...].astype(F32), axis=0, keepdims=True)
        small_out[5:8, :] = jnp.zeros((3, small_out.shape[1]), F32)


def fc2_grad_kernel(place, act, d_ffn, keep_out, send_out, held):
    core = place[1]
    held[...] = mul(act[...], d_ffn[...], TN)
    for pair in range(2):
        for seq in range(2):
            at = (0, pair ^ place[6], seq ^ place[0])
            columns = slice(384 * seq, 384 * seq + 384)
            low = pl.multiple_of(384 * pair + 192 * core, 64)
            high = pl.multiple_of(384 * pair + 192 * (1 - core), 64)
            keep_out[at] = held[pl.ds(low, 192), columns].astype(BF)
            send_out[at] = held[pl.ds(high, 192), columns].astype(BF)


def fc1_grad_kernel(place, hidden, d_pre, attn, d_mixed, keep_out, send_out, held, *, rest):
    step = pl.program_id(0)
    core = place[1]
    held[...] = mul(hidden[...], d_pre[...], TN)
    seq = step // 2
    lanes = pl.ds(pl.multiple_of((step % 2) * 768, LANES), 768)
    for pair in range(8):
        at = rest(pair % 2, pair // 2, seq) ^ place[3]
        low = pl.multiple_of(96 * pair + 48 * core, 16)
        high = pl.multiple_of(96 * pair + 48 * (1 - core), 16)
        keep_out[at, :, lanes] = held[pl.ds(low, 48), :].astype(BF)
        send_out[at, :, lanes] = held[pl.ds(high, 48), :].astype(BF)

    @pl.when(step == pl.num_programs(0) - 1)
    def _():
        held[...] = mul(attn[...], d_mixed[...], TN)
        for pair in range(8):
            low = pl.multiple_of(96 * pair + 48 * core, 16)
            high = pl.multiple_of(96 * pair + 48 * (1 - core), 16)
            for side in range(2):
                at = rest_label(ORDER_A)(pair % 2, pair // 2, side) ^ place[2]
                columns = slice(384 * side, 384 * side + 384)
                keep_out[at, :, 1536:1920] = held[pl.ds(low, 48), columns].astype(BF)
                send_out[at, :, 1536:1920] = held[pl.ds(high, 48), columns].astype(BF)


def result_kernel(place, act, fc2, resid, cot, vecs, result_out, small_out, total):
    step = pl.program_id(0)

    @pl.when(step == 0)
    def _():
        total[...] = jnp.zeros_like(total)

    total[...] += mul(act[...], fc2[...])

    @pl.when(step == pl.num_programs(0) - 1)
    def _():
        ffn = total[...] + vecs[6:7, :]
        result_out[...] = (resid[...] + vecs[7:8, :] * ffn).astype(BF)
        small_out[0:1, :] = jnp.sum(cot[...].astype(F32) * ffn, axis=0, keepdims=True)
        small_out[1:8, :] = jnp.zeros((7, small_out.shape[1]), F32)


def hidden1_grad_kernel(
    place, dqkv0, dqkv1, dqkv2, weight, own, other, keep_out, send_out, small_out, total, joined
):
    step = pl.program_id(0)
    rows = own.shape[0]
    here = pl.ds(pl.multiple_of(place[0] * rows, 64), rows)
    there = pl.ds(pl.multiple_of((1 - place[0]) * rows, 64), rows)

    @pl.when(step == 0)
    def _():
        total[...] = jnp.zeros_like(total)
        small_out[...] = jnp.zeros_like(small_out)

    for n, part in enumerate((dqkv0, dqkv1, dqkv2)):
        joined[:, LANES * n : LANES * (n + 1)] = part[0]
    grads = joined[...]
    total[...] += mul(grads, weight[...], NT)
    line = jnp.sum(grads.astype(F32), axis=0, keepdims=True)

    @pl.when(step == 0)
    def _():
        small_out[2:3, :384] = line

    @pl.when(step == 2)
    def _():
        small_out[2:3, 384:] = line
        mine = total[here, :]
        theirs = total[there, :]
        keep_out[...] = mine
        send_out[...] = theirs.astype(BF)
        normed_mine, _ = layer_norm(own[...].astype(F32))
        normed_theirs, _ = layer_norm(other[...].astype(F32))
        small_out[0:1, :] = jnp.sum(mine * normed_mine, axis=0, keepdims=True) + jnp.sum(
            theirs * normed_theirs, axis=0, keepdims=True
        )
        small_out[1:2, :] = jnp.sum(mine, axis=0, keepdims=True) + jnp.sum(
            theirs, axis=0, keepdims=True
        )


def qkv_grad_kernel(
    place, hidden, dqkv0, dqkv1, dqkv2, keep_out, send_out, held, joined, *, rest
):
    core = place[1]
    for n, part in enumerate((dqkv0, dqkv1, dqkv2)):
        joined[:, LANES * n : LANES * (n + 1)] = part[0]
    held[...] = mul(hidden[...], joined[...], TN)
    for pair in range(8):
        at = rest(pair % 2, pair // 2, 0) ^ place[4]
        low = pl.multiple_of(96 * pair + 48 * core, 16)
        high = pl.multiple_of(96 * pair + 48 * (1 - core), 16)
        keep_out[at] = held[pl.ds(low, 48), :].astype(BF)
        send_out[at] = held[pl.ds(high, 48), :].astype(BF)


def tokens_grad_kernel(place, keep, recv, own, d_resid, vecs, grad_out):
    grad = keep[...] + recv[...].astype(F32)
    normed, inverse = layer_norm(own[...].astype(F32))
    back = layer_norm_back(grad, normed, inverse, vecs[0:1, :])
    grad_out[...] = (d_resid[...] + back).astype(BF)


def rest_label(order):
    def rest(x_bit, line, seq):
        bits = {"x": x_bit, "z1": line & 1, "z2": line >> 1, "y": seq}
        total = 0
        for name in order[1:]:
            total = total * 2 + bits[name]
        return total

    return rest


ORDER_A = ("core", "x", "y", "z1", "z2")
ORDER_B = ("core", "z1", "x", "y", "z2")
ORDER_Q = ("core", "x", "z1", "z2")


SPAN = 2 * GRID - 1
CELLS = SPAN * SPAN


def flips():
    row = lax.broadcasted_iota(jnp.int32, (LANES, LANES), 0)
    lane = lax.broadcasted_iota(jnp.int32, (LANES, LANES), 1)
    return jnp.where(row + lane == LANES - 1, 1.0, 0.0)


def exact(left, right, dims):
    return lax.dot_general(
        left, right, dims, precision=lax.Precision.HIGHEST, preferred_element_type=F32
    )


def moved_window(source, start, target):
    base = start // LANES * LANES
    place = target % LANES
    held = source[:, base : base + 2 * LANES]
    turn = (place - (start - base)) % (2 * LANES)
    if turn:
        held = pltpu.roll(held, turn, axis=1)
    lane = lax.broadcasted_iota(jnp.int32, (1, 2 * LANES), 1)
    return jnp.where((lane >= place) & (lane < place + SPAN), held, 0.0)


def strips_kernel(place, table, strips_out, flat, sides):
    heads = table.shape[0]
    flat[...] = jnp.zeros_like(flat)
    flat[:heads, : CELLS + 3] = table[...]
    turned = pltpu.roll(flat[:, : 18 * LANES], 18 * LANES - CELLS, axis=1)
    tail = turned[:, :LANES]
    for n in range(18):
        block = 17 - n
        flat[:, LANES * n : LANES * (n + 1)] = exact(
            turned[:, LANES * block : LANES * (block + 1)], flips(), NN
        )
    sides[...] = jnp.zeros_like(sides)
    for b in range(SPAN):
        base = 24 * b // LANES * LANES
        part = moved_window(flat, SPAN * b, 24 * b)
        sides[b % 2, :, base : base + 2 * LANES] += part
    lane = lax.broadcasted_iota(jnp.int32, (16, LANES), 1)
    sides[0, :, 1152:1280] = jnp.where(lane < 3, tail, 0.0)
    for head in range(heads):
        for par in range(2):
            strips_out[head, par : par + 1, :] = sides[par, head : head + 1, :]


def pack_kernel(place, strip0, strip1, strip2, ffn, fc1_bias, last, result, packed_out, packed):
    packed[...] = jnp.zeros_like(packed)
    for n in range(5):
        lanes = slice(256 * n, 256 * n + 256)
        for pair, strip in enumerate((strip0, strip1, strip2)):
            for head in range(2):
                for par in range(2):
                    row = 16 * n + 6 * par + 2 * pair + head
                    packed[row : row + 1, :] = strip[0, head, par : par + 1, lanes]
    for n in range(3):
        lanes = slice(256 * n, 256 * n + 256)
        row = 80 + 16 * n
        packed[row : row + 5, :] = ffn[0:5, lanes]
        packed[row + 5 : row + 6, :] = result[0:1, lanes]
        packed[row + 6 : row + 9, :] = last[0:3, lanes]
        for part in range(4):
            packed[row + 9 + part : row + 10 + part, :] = fc1_bias[
                :, 768 * part + 256 * n : 768 * part + 256 * n + 256
            ]
    for n in range(8):
        packed_out[16 * (n // 4) : 16 * (n // 4) + 16, 256 * (n % 4) : 256 * (n % 4) + 256] = packed[
            16 * n : 16 * n + 16, :
        ].astype(BF)


def unpack_kernel(
    place, packed_in, mate_in, table_out, norm2_gain, norm2_bias, scale1, proj_bias, fc2_bias, scale2,
    norm1_gain, norm1_bias, query_bias, value_bias, fc1_bias, flat, sides, packed, mate,
):
    for held, source in ((packed, packed_in), (mate, mate_in)):
        for n in range(8):
            held[16 * n : 16 * n + 16, :] = source[
                16 * (n // 4) : 16 * (n // 4) + 16, 256 * (n % 4) : 256 * (n % 4) + 256
            ].astype(F32)
    heads = table_out.shape[0]
    half = heads // 2
    left = place[0] == 0
    flat[...] = jnp.zeros_like(flat)
    for n in range(5):
        lanes = slice(256 * n, 256 * n + 256)
        for par in range(2):
            rows = slice(16 * n + half * par, 16 * n + half * par + half)
            mine = packed[rows, :]
            theirs = mate[rows, :]
            sides[par, 0:half, lanes] = jnp.where(left, mine, theirs)
            sides[par, half:heads, lanes] = jnp.where(left, theirs, mine)
    for b in range(SPAN):
        target = SPAN * b
        base = target // LANES * LANES
        part = moved_window(sides.at[b % 2], 24 * b, target)
        flat[:, base : base + 2 * LANES] += part
    lane = lax.broadcasted_iota(jnp.int32, (16, LANES), 1)
    blocks = [
        exact(flat[:, LANES * (17 - n) : LANES * (18 - n)], flips(), NN) for n in range(18)
    ]
    blocks[0] = jnp.where(lane < 3, sides[0, :, 1152:1280], blocks[0])
    turned = pltpu.roll(jnp.concatenate(blocks, axis=1), CELLS, axis=1)
    table_out[...] = turned[:heads, : CELLS + 3]
    outs = (norm2_gain, norm2_bias, scale1, proj_bias, fc2_bias, scale2, norm1_gain, norm1_bias)
    for n in range(3):
        lanes = slice(256 * n, 256 * n + 256)
        for at, out in enumerate(outs):
            row = 80 + 16 * n + at
            out[lanes] = (packed[row : row + 1, :] + mate[row : row + 1, :]).reshape(256)
        for part in range(4):
            row = 89 + 16 * n + part
            fc1_bias[768 * part + 256 * n : 768 * part + 256 * n + 256] = (
                packed[row : row + 1, :] + mate[row : row + 1, :]
            ).reshape(256)
    for source, side in ((packed, place[0]), (mate, 1 - place[0])):
        line = jnp.concatenate([source[88 + 16 * n : 89 + 16 * n, :] for n in range(3)], axis=1)
        lanes = pl.ds(pl.multiple_of(side * 384, LANES), 384)
        query_bias[lanes] = line[:, :384].reshape(384)
        value_bias[lanes] = line[:, 384:].reshape(384)


def even_places():
    lane = np.arange(STRIP_WIDTH)[None, :]
    row = np.arange(STRIP)[:, None]
    turn = (lane - 1) // STRIP
    return np.where(row == 0, turn % 2 == 0, turn % 2 == 1).astype(np.float32)


def split_body(
    tokens,
    masked,
    out_grad,
    norm1_gain,
    norm1_bias,
    qkv_weight,
    query_bias,
    value_bias,
    rel_table,
    proj_weight,
    proj_bias,
    scale1,
    norm2_gain,
    norm2_bias,
    fc1_weight,
    fc1_bias,
    fc2_weight,
    fc2_bias,
    scale2,
):
    _, rows, width = tokens.shape
    slots = 2 * rows
    heads = rel_table.shape[1] // 2
    pairs = heads // 2
    share = width // 2
    hidden = fc1_weight.shape[1]
    seq = lax.axis_index("seq")
    img = lax.axis_index("img")
    core = img & 1
    line = img >> 2
    x_bit = (img >> 1) & 1
    place = jnp.stack(
        [
            seq,
            core,
            rest_label(ORDER_A)(x_bit, line, seq),
            rest_label(ORDER_B)(x_bit, line, seq),
            rest_label(ORDER_Q)(x_bit, line, seq),
            line,
            x_bit,
        ]
    ).astype(jnp.int32)
    own = tokens.reshape(rows, width)
    other = swapped(own, "y")
    cot = (out_grad.astype(F32) * masked.astype(F32)[..., None]).astype(BF).reshape(rows, width)
    vecs = jnp.stack(
        [norm1_gain, norm1_bias, proj_bias, scale1, norm2_gain, norm2_bias, fc2_bias, scale2]
    )
    strips = run(
        strips_kernel, place, (1,), [full(rel_table.shape[::-1])], [full((2 * heads, 2, STRIP_WIDTH))],
        [shape((2 * heads, 2, STRIP_WIDTH), F32)],
        [pltpu.VMEM((16, 2432), F32), pltpu.VMEM((2, 16, STRIP_WIDTH), F32)], (rel_table.T,), 0,
    )[0]
    even_mask = jnp.asarray(even_places())

    def qkv_rows(source, mine, held):
        def side(p):
            return p[0] if mine else 1 - p[0]

        return run(
            qkv_kernel, place, (3,),
            [
                full((rows, width)), full((8, width)),
                spec((width, share), lambda t, p: (0, 2 * t + p[0])),
                spec((1, share), lambda t, p: (0, p[0])), spec((1, share), lambda t, p: (0, p[0])),
            ],
            [
                spec((1, rows, share), lambda t, p: (t, side(p), 0)),
                spec((rows, width), lambda t, p: (side(p), 0)),
            ],
            [shape((3, slots, share), BF), shape((slots, width), BF)],
            [],
            (source, vecs, qkv_weight, query_bias.reshape(1, width), value_bias.reshape(1, width)),
            0, after=held, reuse=() if mine else ((0, 0), (1, 1)),
        )

    qkv, hidden1 = qkv_rows(other, False, qkv_rows(own, True, ()))
    pair_rows = spec((slots, LANES), lambda n, p: (0, n))
    pair_half = spec((rows, LANES), lambda n, p: (0, n))
    pair_qkv = spec((3, slots, LANES), lambda n, p: (0, 0, n))
    pair_expo = spec((2, slots, slots), lambda n, p: (n, 0, 0))
    attn_own, attn_send, expo, inv = run(
        attend_kernel, place, (pairs,),
        [pair_qkv, full((2 * heads, 2, STRIP_WIDTH)), full((STRIP, STRIP_WIDTH))],
        [pair_half, pair_half, pair_expo, pair_rows],
        [
            shape((rows, share), BF), shape((rows, share), BF),
            shape((heads, slots, slots), BF), shape((slots, share), F32),
        ],
        [pltpu.VMEM((2, STRIP, STRIP_WIDTH), F32), pltpu.VMEM((slots, LANES), F32)],
        (qkv, strips, even_mask),
        16 * slots * slots * 64 * heads,
    )
    attn_other = swapped(attn_send, "y")
    parts = 4
    part = hidden // parts
    whole = full((rows, width))
    sliced = spec((rows, part), lambda c, p: (0, c))
    d_ffn, d_act = run(
        d_act_kernel, place, (parts,),
        [whole, full((8, width)), spec((part, width), lambda c, p: (c, 0))],
        [whole, sliced], [shape((rows, width), BF), shape((rows, hidden), BF)], [],
        (cot, vecs, fc2_weight), 0, after=(attn_send,),
    )
    act, d_pre, fc1_bias_part, hidden2, resid, attn_low, mixed = run(
        ffn_kernel, place, (parts,),
        [
            whole, full((rows, share)), full((rows, share)), full((8, width)),
            full((width, width)), spec((width, part), lambda c, p: (0, c)),
            spec((1, part), lambda c, p: (0, c)), sliced,
        ],
        [sliced, sliced, spec((1, part), lambda c, p: (0, c)), whole, whole, whole, whole],
        [
            shape((rows, hidden), BF), shape((rows, hidden), BF), shape((1, hidden), F32),
            shape((rows, width), BF), shape((rows, width), F32), shape((rows, width), BF),
            shape((rows, width), F32),
        ],
        [],
        (own, attn_own, attn_other, vecs, proj_weight, fc1_weight, fc1_bias.reshape(1, hidden), d_act),
        0,
    )
    cube = (4, 2, 2, 192, share)

    def line_place(c, p):
        far = c ^ p[5]
        return (far & 1) * 2 + (far >> 1), 0, 0, 0, 0

    block = spec((1, *cube[1:]), line_place)
    keep_a, send_a = run(
        fc2_grad_kernel, place, (parts,), [sliced, whole], [block, block],
        [shape(cube, BF), shape(cube, BF)], [pltpu.VMEM((part, width), F32)], (act, d_ffn), 0,
    )
    terms_a = [keep_a, swapped(send_a, "core")]
    d_mixed, d_resid, grad_own, grad_send, small_ffn = run(
        ffn_back_kernel, place, (parts,),
        [
            sliced, spec((width, part), lambda c, p: (0, c)), whole, whole, whole, whole, full((8, width)),
            spec((share, width), lambda c, p: (p[0], 0)), spec((share, width), lambda c, p: (1 - p[0], 0)),
        ],
        [whole, whole, full((rows, share)), full((rows, share)), full((8, width))],
        [
            shape((rows, width), BF), shape((rows, width), F32), shape((rows, share), BF),
            shape((rows, share), BF), shape((8, width), F32),
        ],
        [pltpu.VMEM((rows, width), F32)],
        (d_pre, fc1_weight, cot, d_ffn, resid, mixed, vecs, proj_weight, proj_weight), 0, after=(send_a,),
    )
    grad_other = swapped(grad_send, "y")
    out_a1 = x_part(place, terms_a, 1, (grad_send,))
    terms_a = [*terms_a, swapped(out_a1, ORDER_A[1])]
    block = (16, 48, 5 * share)
    keep_b, send_b = run(
        functools.partial(fc1_grad_kernel, rest=rest_label(ORDER_B)), place, (parts,),
        [whole, sliced, whole, whole], [full(block), full(block)],
        [shape(block, BF), shape(block, BF)],
        [pltpu.VMEM((width, part), F32)], (hidden2, d_pre, attn_low, d_mixed), 0, after=(out_a1,),
    )
    terms_b = [keep_b, swapped(send_b, "core")]

    def attend_back(pair, after):
        pair_expo = spec((2, slots, slots), lambda n, p: (pair, 0, 0))
        pair_rows = spec((slots, LANES), lambda n, p: (0, pair))
        pair_half = spec((rows, LANES), lambda n, p: (0, pair))
        return run(
            attend_back_kernel, place, (1,),
            [
                spec((3, slots, LANES), lambda n, p: (0, 0, pair)), pair_expo, pair_half, pair_half,
                pair_half, pair_half, pair_rows, full((STRIP, STRIP_WIDTH)),
            ],
            [full((3, slots, LANES)), full((1, 2, 2, STRIP_WIDTH))],
            [shape((3, slots, LANES), BF), shape((1, 2, 2, STRIP_WIDTH), F32)],
            [
                pltpu.VMEM((slots, LANES), F32), pltpu.VMEM((slots, LANES), F32),
                pltpu.VMEM((2, slots, slots), BF), pltpu.VMEM((2, STRIP, STRIP_WIDTH), F32),
                pltpu.VMEM((slots, LANES), F32),
            ],
            (qkv, expo, attn_own, attn_send, grad_own, grad_other, inv, even_mask),
            32 * slots * slots * 64 * 2, after=after, us=40.0 if pair == 0 else None,
        )

    dqkv0, strip0 = attend_back(0, (send_b,))
    out_p1 = half_out(place, terms_b, (dqkv0,), column=4, columns=share)
    terms_p = [*terms_b, swapped(out_p1, ORDER_A[1])]
    out_b1 = half_out(place, terms_b, (out_p1,), columns=4 * share)
    terms_b = [*terms_b, swapped(out_b1, ORDER_B[1])]
    dqkv1, strip1 = attend_back(1, (dqkv0, out_b1))
    dqkv2, strip2 = attend_back(2, (dqkv1,))
    dqkv = (dqkv0, dqkv1, dqkv2)
    third = [spec((1, slots, LANES), lambda t, p: (t, 0, 0))] * 3
    dh_keep, dh_send, small_last = run(
        hidden1_grad_kernel, place, (3,),
        [*third, spec((width, share), lambda t, p: (0, 2 * t + p[0])), whole, whole],
        [whole, whole, full((8, width))],
        [shape((rows, width), F32), shape((rows, width), BF), shape((8, width), F32)],
        [pltpu.VMEM((slots, width), F32), pltpu.VMEM((slots, share), BF)], (*dqkv, qkv_weight, own, other),
        2 * slots * width * 3 * share,
    )
    block = (8, 48, 3 * share)
    keep_q, send_q = run(
        functools.partial(qkv_grad_kernel, rest=rest_label(ORDER_Q)), place, (3,),
        [full((slots, width)), *third], [spec((8, 48, share), lambda t, p: (0, 0, t))] * 2,
        [shape(block, BF), shape(block, BF)],
        [pltpu.VMEM((width, share), F32), pltpu.VMEM((slots, share), BF)], (hidden1, *dqkv), 2 * slots * width * 3 * share,
        after=(dh_send,),
    )
    recv_q = swapped(send_q, "core")
    out_a2, rest_a = joined_halves(place, terms_a, terms_p, (send_q,))
    terms_a = [rest_a, swapped(out_a2, "y")]
    result, small_result = run(
        result_kernel, place, (parts,),
        [sliced, spec((part, width), lambda c, p: (c, 0)), whole, whole, full((8, width))],
        [whole, full((8, width))],
        [shape((rows, width), BF), shape((8, width), F32)],
        [pltpu.VMEM((rows, width), F32)], (act, fc2_weight, resid, cot, vecs),
        2 * rows * width * hidden, after=(out_a2, rest_a),
    )
    packed = run(
        pack_kernel, place, (1,),
        [*[full((1, 2, 2, STRIP_WIDTH))] * 3, full((8, width)), full((1, hidden)), full((8, width)), full((8, width))],
        [full(NOTE)], [shape(NOTE, BF)], [pltpu.VMEM((128, 256), F32)],
        (strip0, strip1, strip2, small_ffn, fc1_bias_part, small_last, small_result), 0,
    )[0]
    mate = swapped(packed, "core")
    def wide(blocks, columns):
        return (48 * blocks + NOTE[0], columns)

    send, rest = run(
        qs_first_kernel, place, (1,),
        [full((8, 48, 3 * share))] * 2 + [full(NOTE)] * 2, [full(wide(4, 3 * share))] * 2,
        [shape(wide(4, 3 * share), BF)] * 2, [], (keep_q, recv_q, packed, mate), 0, after=(),
    )
    recv = swapped(send, "x")
    out_b2 = half_out(place, terms_b, (send,), columns=4 * share)
    terms_b = [*terms_b, swapped(out_b2, "x")]
    out_a3 = half_out(place, terms_a, (out_b2,))
    terms_a = [*terms_a, swapped(out_a3, "z1")]
    dh_late = run(
        add_kernel, place, (1,), [whole], [whole], [shape((rows, width), BF)], [], (dh_send,), 0,
        after=(out_a3,),
    )[0]
    dh_recv = swapped(dh_late, "y")
    send, rest = run(
        qs_next_kernel, place, (1,), [full(wide(4, 3 * share))] * 2, [full(wide(2, 3 * share))] * 2,
        [shape(wide(2, 3 * share), BF)] * 2, [], (rest, recv), 0, after=(dh_late,),
    )
    recv = swapped(send, "z1")
    out_a4 = half_out(place, terms_a, (send,))
    terms_a = [*terms_a, swapped(out_a4, "z2")]
    out_b3 = half_out(place, terms_b, (out_a4,), columns=4 * share)
    terms_b = [*terms_b, swapped(out_b3, "y")]
    q_keep, q_line, q_side, q_cross, note = run(
        qs_last_kernel, place, (1,), [full(wide(2, 3 * share))] * 2,
        [
            full((48, 2 * share)), full(wide(1, NOTE[1])), full((48, share)), full((48, share)), full(NOTE),
        ],
        [
            shape((48, 2 * share), F32), shape(wide(1, NOTE[1]), BF), shape((48, share), BF),
            shape((48, share), BF), shape(NOTE, BF),
        ],
        [pltpu.VMEM(wide(2, 3 * share), F32)], (rest, recv), 0, after=(out_b3,),
    )
    q_sends = (swapped(q_line, "z2"), swapped(q_side, "y"), swapped(q_cross, "z2", "y"))
    tokens_grad = run(
        tokens_grad_kernel, place, (1,),
        [whole, whole, whole, whole, full((8, width))], [whole],
        [shape((rows, width), BF)], [], (dh_keep, dh_recv, own, d_resid, vecs), 0,
        after=(q_line,),
    )[0]
    out_b4 = half_out(place, terms_b, (tokens_grad,), columns=4 * share)
    terms_b = [*terms_b, swapped(out_b4, "z2")]
    qkv_grad, packed = run(
        qs_join_kernel, place, (1,),
        [full((48, 2 * share)), full(wide(1, NOTE[1])), full((48, share)), full((48, share)), full(NOTE)],
        [full((48, 3 * share)), full(NOTE)], [shape((48, 3 * share), F32), shape(NOTE, BF)], [],
        (q_keep, *q_sends, note), 0, after=(out_b4,),
    )
    mate = swapped(packed, "y")
    fc2_proj = added(terms_a)
    fc1_grad = added([term[:, :, : 4 * share] for term in terms_b])
    fc2_grad = fc2_proj[:192]
    proj_grad = fc2_proj[192:]
    vector = shape((width,), F32)
    table_grad, *small = run(
        unpack_kernel, place, (1,), [full(NOTE)] * 2,
        [full(rel_table.shape[::-1]), *[full((width,))] * 10, full((hidden,))],
        [shape(rel_table.shape[::-1], F32), *[vector] * 10, shape((hidden,), F32)],
        [
            pltpu.VMEM((16, 2432), F32), pltpu.VMEM((2, 16, STRIP_WIDTH), F32),
            pltpu.VMEM((128, 256), F32), pltpu.VMEM((128, 256), F32),
        ], (packed, mate), 0,
    )
    return (
        result.reshape(tokens.shape),
        tokens_grad.reshape(tokens.shape),
        small[6],
        small[7],
        qkv_grad,
        small[8],
        small[9],
        table_grad.T,
        proj_grad,
        small[3],
        small[2],
        small[0],
        small[1],
        fc1_grad,
        small[10],
        fc2_grad,
        small[4],
        small[5],
    )


def solution(mesh):
    in_specs = (
        P("img", "seq", None),
        P("img", "seq"),
        P("img", "seq", None),
        P(),
        P(),
        P(),
        P(),
        P(),
        P(),
        P(),
        P(),
        P(),
        P(),
        P(),
        P(),
        P(),
        P(),
        P(),
        P(),
    )
    out_specs = (
        P("img", "seq", None),
        P("img", "seq", None),
        P(),
        P(),
        P("img", "seq"),
        P(),
        P(),
        P(),
        P("img", "seq"),
        P(),
        P(),
        P(),
        P(),
        P("img", "seq"),
        P(),
        P("img", "seq"),
        P(),
        P(),
    )
    sizes = dict(mesh.shape)
    body = split_body if (sizes["img"], sizes["seq"]) == (16, 2) else general_body
    return jax.shard_map(body, mesh=mesh, in_specs=in_specs, out_specs=out_specs, check_vma=False)
```

```python
import functools

import jax
import jax.numpy as jnp
import numpy as np
from jax import lax
from jax.experimental import pallas as pl
from jax.experimental.pallas import tpu as pltpu
from jax.sharding import PartitionSpec as P

GRID = 24


EPSILON = 1e-06
NEGATIVE = -1e30
ROOT_HALF = 0.7071067811865476
GAUSS_NORM = 0.3989422804014327


def passed_along(value, axis, steps):
    count = lax.axis_size(axis)
    pairs = [(source, (source + steps) % count) for source in range(count)]
    return lax.ppermute(value, axis, pairs)


def gap_onehot():
    span_width = 2 * GRID - 1
    grid_ids = jnp.arange(GRID, dtype=jnp.int32)
    gaps = grid_ids[:, None, None] - grid_ids[None, :, None] + GRID - 1
    return (gaps == jnp.arange(span_width, dtype=jnp.int32)[None, None, :]).astype(jnp.float32)


def bias_full(rel_table, all_slots):
    highest = lax.Precision.HIGHEST
    span_width = 2 * GRID - 1
    far_index = span_width * span_width
    cells = GRID * GRID
    head_count = rel_table.shape[1]
    spare = all_slots - 1 - cells
    selector = gap_onehot()
    patch_table = rel_table[0:far_index].reshape(span_width, span_width, head_count)
    row_pick = jnp.einsum("pqa,abh->pqbh", selector, patch_table, precision=highest)
    spread = jnp.einsum("pqbh,rsb->hprqs", row_pick, selector, precision=highest)
    patch_bias = spread.reshape(head_count, cells, cells)
    patch_bias = jnp.concatenate(
        [
            patch_bias,
            jnp.broadcast_to(patch_bias[:, cells - 1 : cells, :], (head_count, spare, cells)),
        ],
        axis=1,
    )
    patch_bias = jnp.concatenate(
        [
            patch_bias,
            jnp.broadcast_to(
                patch_bias[:, :, cells - 1 : cells], (head_count, cells + spare, spare)
            ),
        ],
        axis=2,
    )
    top_row = jnp.broadcast_to(rel_table[far_index][:, None, None], (head_count, 1, all_slots - 1))
    left_col = jnp.broadcast_to(
        rel_table[far_index + 1][:, None, None], (head_count, all_slots - 1, 1)
    )
    corner = rel_table[far_index + 2][:, None, None]
    upper = jnp.concatenate([corner, top_row], axis=2)
    lower = jnp.concatenate([left_col, patch_bias], axis=2)
    return jnp.concatenate([upper, lower], axis=1)


def table_back(grad_full):
    highest = lax.Precision.HIGHEST
    span_width = 2 * GRID - 1
    cells = GRID * GRID
    head_count = grad_full.shape[0]
    corner = grad_full[:, 0, 0]
    far_grad = jnp.sum(grad_full[:, 0, 1:], axis=1)
    near_grad = jnp.sum(grad_full[:, 1:, 0], axis=1)
    patch_grad = grad_full[:, 1:, 1:]
    patch_grad = jnp.concatenate(
        [
            patch_grad[:, 0 : cells - 1, :],
            jnp.sum(patch_grad[:, cells - 1 :, :], axis=1, keepdims=True),
        ],
        axis=1,
    )
    patch_grad = jnp.concatenate(
        [
            patch_grad[:, :, 0 : cells - 1],
            jnp.sum(patch_grad[:, :, cells - 1 :], axis=2, keepdims=True),
        ],
        axis=2,
    )
    selector = gap_onehot()
    spread = patch_grad.reshape(head_count, GRID, GRID, GRID, GRID)
    row_sums = jnp.einsum("hprqs,rsb->pqbh", spread, selector, precision=highest)
    patch_table = jnp.einsum("pqa,pqbh->abh", selector, row_sums, precision=highest)
    tail = jnp.stack([far_grad, near_grad, corner], axis=0)
    return jnp.concatenate([patch_table.reshape(span_width * span_width, head_count), tail], axis=0)


def gelu_value(argument):
    return 0.5 * argument * (1.0 + lax.erf(argument * ROOT_HALF))


def gelu_slope(argument):
    return (
        0.5 * (1.0 + lax.erf(argument * ROOT_HALF))
        + argument * jnp.exp(-0.5 * argument * argument) * GAUSS_NORM
    )


def normalize(values, gain, shift):
    center = values - jnp.mean(values, axis=-1, keepdims=True)
    inverse = lax.rsqrt(jnp.mean(center * center, axis=-1, keepdims=True) + EPSILON)
    normed = center * inverse
    return (normed * gain + shift, normed, inverse)


def normalize_back(grad_out, normed, inverse, gain):
    signal = grad_out * gain
    inner = (
        signal
        - jnp.mean(signal, axis=-1, keepdims=True)
        - normed * jnp.mean(signal * normed, axis=-1, keepdims=True)
    )
    return (inverse * inner, jnp.sum(grad_out * normed, axis=0), jnp.sum(grad_out, axis=0))


def general_body(
    tokens,
    masked,
    out_grad,
    norm1_gain,
    norm1_bias,
    qkv_weight,
    query_bias,
    value_bias,
    rel_table,
    proj_weight,
    proj_bias,
    scale1,
    norm2_gain,
    norm2_bias,
    fc1_weight,
    fc1_bias,
    fc2_weight,
    fc2_bias,
    scale2,
):
    images, local_rows, model_width = tokens.shape
    head_count = rel_table.shape[1]
    head_size = model_width // head_count
    head_scale = head_size ** (-0.5)
    cycle_size = lax.axis_size("seq")
    position = lax.axis_index("seq")
    all_slots = local_rows * cycle_size
    key_pos = jnp.arange(all_slots, dtype=jnp.int32)
    position_bias = lax.dynamic_slice_in_dim(
        bias_full(rel_table, all_slots), position * local_rows, local_rows, 1
    )
    key_valid = key_pos <= GRID * GRID
    flat_rows = images * local_rows
    head_shape = (images, local_rows, head_count, head_size)
    inputs = tokens.astype(jnp.float32).reshape(flat_rows, model_width)
    normed1, centred1, inverse1 = normalize(inputs, norm1_gain, norm1_bias)
    hidden1 = normed1.astype(jnp.bfloat16)
    projected = jnp.dot(hidden1, qkv_weight, preferred_element_type=jnp.float32)
    queries = ((projected[:, 0:model_width] + query_bias) * head_scale).astype(jnp.bfloat16)
    keys_local = (
        projected[:, model_width : 2 * model_width]
        .astype(jnp.bfloat16)
        .reshape(images, local_rows, model_width)
    )
    values_local = (
        (projected[:, 2 * model_width :] + value_bias)
        .astype(jnp.bfloat16)
        .reshape(images, local_rows, model_width)
    )
    query_heads = queries.reshape(head_shape)

    def block_scores(key_block, offset):
        key_count = key_block.shape[1]
        key_heads = key_block.reshape(images, key_count, head_count, head_size)
        logits = jnp.einsum(
            "gqhd,gkhd->ghqk", query_heads, key_heads, preferred_element_type=jnp.float32
        )
        logits = logits + lax.dynamic_slice_in_dim(position_bias, offset, key_count, 2)[None]
        usable = lax.dynamic_slice_in_dim(key_valid, offset, key_count, 0)
        return (jnp.where(usable, logits, NEGATIVE), usable)

    row_max = jnp.full((images, head_count, local_rows), NEGATIVE, jnp.float32)
    key_block = lax.all_gather(keys_local, "seq", axis=1, tiled=True)
    value_block = lax.all_gather(values_local, "seq", axis=1, tiled=True)
    key_count = key_block.shape[1]
    scores, usable = block_scores(key_block, jnp.int32(0))
    new_max = jnp.maximum(row_max, jnp.max(scores, axis=-1))
    weights = jnp.where(usable, jnp.exp(scores - new_max[..., None]), 0.0)
    totals = jnp.sum(weights, axis=-1)
    value_heads = value_block.reshape(images, key_count, head_count, head_size)
    update = jnp.einsum(
        "ghqk,gkhd->gqhd",
        weights.astype(jnp.bfloat16),
        value_heads,
        preferred_element_type=jnp.float32,
    )
    weighted = update
    row_max, totals, weighted = (new_max, totals, weighted)
    log_total = row_max + jnp.log(totals)
    attended = weighted / jnp.transpose(totals, (0, 2, 1))[..., None]
    attn_low = attended.reshape(flat_rows, model_width).astype(jnp.bfloat16)
    mixed_out = jnp.dot(attn_low, proj_weight, preferred_element_type=jnp.float32) + proj_bias
    residual1 = inputs + scale1 * mixed_out
    normed2, centred2, inverse2 = normalize(residual1, norm2_gain, norm2_bias)
    hidden2 = normed2.astype(jnp.bfloat16)
    pre_act = jnp.dot(hidden2, fc1_weight, preferred_element_type=jnp.float32) + fc1_bias
    activated = gelu_value(pre_act).astype(jnp.bfloat16)
    ffn_out = jnp.dot(activated, fc2_weight, preferred_element_type=jnp.float32) + fc2_bias
    result = (residual1 + scale2 * ffn_out).astype(jnp.bfloat16).reshape(tokens.shape)
    cotangent = (out_grad.astype(jnp.float32) * masked.astype(jnp.float32)[..., None]).reshape(
        flat_rows, model_width
    )
    d_ffn = (scale2 * cotangent).astype(jnp.bfloat16)
    scale2_grad = jnp.sum(cotangent * ffn_out, axis=0)
    fc2_bias_grad = jnp.sum(d_ffn.astype(jnp.float32), axis=0)
    fc2_weight_grad = jnp.einsum("nf,nd->fd", activated, d_ffn, preferred_element_type=jnp.float32)
    d_act = jnp.einsum("nd,fd->nf", d_ffn, fc2_weight, preferred_element_type=jnp.float32)
    d_pre = (d_act * gelu_slope(pre_act)).astype(jnp.bfloat16)
    fc1_bias_grad = jnp.sum(d_pre.astype(jnp.float32), axis=0)
    fc1_weight_grad = jnp.einsum("nd,nf->df", hidden2, d_pre, preferred_element_type=jnp.float32)
    d_hidden2 = jnp.einsum("nf,df->nd", d_pre, fc1_weight, preferred_element_type=jnp.float32)
    back_two, norm2_gain_grad, norm2_bias_grad = normalize_back(
        d_hidden2, centred2, inverse2, norm2_gain
    )
    d_resid1 = cotangent + back_two
    d_mixed = (scale1 * d_resid1).astype(jnp.bfloat16)
    scale1_grad = jnp.sum(d_resid1 * mixed_out, axis=0)
    proj_bias_grad = jnp.sum(d_mixed.astype(jnp.float32), axis=0)
    proj_weight_grad = jnp.einsum(
        "nc,nd->cd", attn_low, d_mixed, preferred_element_type=jnp.float32
    )
    d_attn = jnp.einsum(
        "nd,cd->nc", d_mixed, proj_weight, preferred_element_type=jnp.float32
    ).astype(jnp.bfloat16)
    d_attn_heads = d_attn.reshape(head_shape)
    row_delta = jnp.transpose(
        jnp.sum(d_attn_heads.astype(jnp.float32) * attended, axis=-1), (0, 2, 1)
    )

    def back_block(key_block, value_block, offset):
        key_count = key_block.shape[1]
        scores, usable = block_scores(key_block, offset)
        prob_full = jnp.where(usable, jnp.exp(scores - log_total[..., None]), 0.0)
        prob_low = prob_full.astype(jnp.bfloat16)
        key_heads = key_block.reshape(images, key_count, head_count, head_size)
        value_heads = value_block.reshape(images, key_count, head_count, head_size)
        d_value = jnp.einsum(
            "ghqk,gqhd->gkhd", prob_low, d_attn_heads, preferred_element_type=jnp.float32
        )
        d_probs = jnp.einsum(
            "gqhd,gkhd->ghqk", d_attn_heads, value_heads, preferred_element_type=jnp.float32
        )
        d_scores = (prob_full * (d_probs - row_delta[..., None])).astype(jnp.bfloat16)
        d_query = jnp.einsum(
            "ghqk,gkhd->gqhd", d_scores, key_heads, preferred_element_type=jnp.float32
        )
        d_key = jnp.einsum(
            "ghqk,gqhd->gkhd", d_scores, query_heads, preferred_element_type=jnp.float32
        )
        table_part = jnp.sum(d_scores.astype(jnp.float32), axis=0)
        return (
            d_query,
            d_key.reshape(images, key_count, model_width),
            d_value.reshape(images, key_count, model_width),
            table_part,
        )

    def turn_grads(grad_pair):
        return (
            passed_along(grad_pair[0].astype(jnp.bfloat16), "seq", 1).astype(jnp.float32),
            passed_along(grad_pair[1].astype(jnp.bfloat16), "seq", 1).astype(jnp.float32),
        )

    def cycle_step(turn_index, cycle_state):
        key_block, value_block, d_key_acc, d_value_acc, d_query_acc, table_acc = cycle_state
        owner_rank = (position - turn_index) % cycle_size
        offset = owner_rank * local_rows
        d_query, d_key, d_value, table_part = back_block(key_block, value_block, offset)
        table_acc = lax.dynamic_update_slice_in_dim(table_acc, table_part, offset, 2)
        d_key_acc, d_value_acc = turn_grads((d_key_acc + d_key, d_value_acc + d_value))
        key_block, value_block = passed_along((key_block, value_block), "seq", 1)
        return (key_block, value_block, d_key_acc, d_value_acc, d_query_acc + d_query, table_acc)

    kv_zeros = jnp.zeros((images, local_rows, model_width), jnp.float32)
    initial = (
        keys_local,
        values_local,
        kv_zeros,
        kv_zeros,
        jnp.zeros(head_shape, jnp.float32),
        jnp.zeros((head_count, local_rows, all_slots), jnp.float32),
    )
    cycle_state = lax.fori_loop(0, cycle_size - 1, cycle_step, initial)
    key_block, value_block, d_key_acc, d_value_acc, d_query_acc, table_acc = cycle_state
    offset = (position + 1) % cycle_size * local_rows
    d_query, d_key, d_value, table_part = back_block(key_block, value_block, offset)
    table_acc = lax.dynamic_update_slice_in_dim(table_acc, table_part, offset, 2)
    d_key_all, d_value_all = turn_grads((d_key_acc + d_key, d_value_acc + d_value))
    d_query_all = d_query_acc + d_query
    d_query_low = d_query_all.reshape(flat_rows, model_width).astype(jnp.bfloat16) * head_scale
    d_key_low = d_key_all.reshape(flat_rows, model_width).astype(jnp.bfloat16)
    d_value_low = d_value_all.reshape(flat_rows, model_width).astype(jnp.bfloat16)
    d_qkv = jnp.concatenate([d_query_low, d_key_low, d_value_low], axis=1)
    qkv_weight_grad = jnp.einsum("nd,ne->de", hidden1, d_qkv, preferred_element_type=jnp.float32)
    query_bias_grad = jnp.sum(d_query_low.astype(jnp.float32), axis=0)
    value_bias_grad = jnp.sum(d_value_low.astype(jnp.float32), axis=0)
    d_hidden1 = jnp.einsum("ne,de->nd", d_qkv, qkv_weight, preferred_element_type=jnp.float32)
    back_one, norm1_gain_grad, norm1_bias_grad = normalize_back(
        d_hidden1, centred1, inverse1, norm1_gain
    )
    tokens_grad = (d_resid1 + back_one).astype(jnp.bfloat16).reshape(tokens.shape)
    grad_square = lax.dynamic_update_slice_in_dim(
        jnp.zeros((head_count, all_slots, all_slots), jnp.float32),
        table_acc,
        position * local_rows,
        1,
    )
    table_grad = table_back(grad_square)
    half_summed = (
        lax.psum_scatter(
            qkv_weight_grad.astype(jnp.bfloat16), "img", scatter_dimension=0, tiled=True
        ).astype(jnp.float32),
        lax.psum_scatter(
            proj_weight_grad.astype(jnp.bfloat16), "img", scatter_dimension=0, tiled=True
        ).astype(jnp.float32),
        lax.psum_scatter(
            fc1_weight_grad.astype(jnp.bfloat16), "img", scatter_dimension=0, tiled=True
        ).astype(jnp.float32),
        lax.psum_scatter(
            fc2_weight_grad.astype(jnp.bfloat16), "img", scatter_dimension=0, tiled=True
        ).astype(jnp.float32),
    )
    summed = (
        lax.psum_scatter(
            half_summed[0].astype(jnp.bfloat16), "seq", scatter_dimension=1, tiled=True
        ).astype(jnp.float32),
        lax.psum_scatter(
            half_summed[1].astype(jnp.bfloat16), "seq", scatter_dimension=1, tiled=True
        ).astype(jnp.float32),
        lax.psum_scatter(
            half_summed[2].astype(jnp.bfloat16), "seq", scatter_dimension=1, tiled=True
        ).astype(jnp.float32),
        lax.psum_scatter(
            half_summed[3].astype(jnp.bfloat16), "seq", scatter_dimension=1, tiled=True
        ).astype(jnp.float32),
    )
    smalls = lax.psum(
        (
            table_grad,
            norm1_gain_grad,
            norm1_bias_grad,
            query_bias_grad,
            value_bias_grad,
            proj_bias_grad,
            scale1_grad,
            norm2_gain_grad,
            norm2_bias_grad,
            fc1_bias_grad,
            fc2_bias_grad,
            scale2_grad,
        ),
        ("img", "seq"),
    )
    return (
        result,
        tokens_grad,
        smalls[1],
        smalls[2],
        summed[0],
        smalls[3],
        smalls[4],
        smalls[0],
        summed[1],
        smalls[5],
        smalls[6],
        smalls[7],
        smalls[8],
        summed[2],
        smalls[9],
        summed[3],
        smalls[10],
        smalls[11],
    )


LANES = 128
RATE = 1.15e9
STRIP = 24
STRIP_WIDTH = 1280
MEGA = 1 << 20
NT = (((1,), (1,)), ((), ()))
TN = (((0,), (0,)), ((), ()))
NN = (((1,), (0,)), ((), ()))
BF = jnp.bfloat16
F32 = jnp.float32


def mul(left, right, dims=NN):
    return lax.dot_general(left, right, dims, preferred_element_type=F32)


def bits_of(img, seq):
    line = img >> 2
    return {"core": img & 1, "x": (img >> 1) & 1, "z1": line & 1, "z2": line >> 1, "y": seq}


def label_of(img, seq, order):
    bits = bits_of(img, seq)
    total = 0
    for name in order:
        total = total * 2 + bits[name]
    return total


def swap_pairs(*names):
    order = ("core", "x", "z1", "z2", "y")
    where = {label_of(img, seq, order): img * 2 + seq for img in range(16) for seq in range(2)}
    flip = sum(1 << (len(order) - 1 - order.index(name)) for name in names)
    return [(device, where[label ^ flip]) for label, device in where.items()]


def swapped(value, *names):
    return lax.ppermute(value, ("img", "seq"), swap_pairs(*names))


def added(terms):
    return sum(term[0].astype(F32) for term in terms)


def layer_norm(values):
    center = values - jnp.mean(values, axis=-1, keepdims=True)
    inverse = lax.rsqrt(jnp.mean(center * center, axis=-1, keepdims=True) + EPSILON)
    return center * inverse, inverse


def layer_norm_back(grad_out, normed, inverse, gain):
    signal = grad_out * gain
    return inverse * (
        signal
        - jnp.mean(signal, axis=-1, keepdims=True)
        - normed * jnp.mean(signal * normed, axis=-1, keepdims=True)
    )


def spec(block, index):
    return pl.BlockSpec(block, index)


def full(shape):
    zeros = (0,) * len(shape)
    return pl.BlockSpec(shape, lambda *_: zeros, pipeline_mode=pl.Buffered(1))


SIZES = {
    "strips_kernel": (1.7, 5),
    "qkv_kernel": (1.9, 10),
    "attend_kernel": (9.0, 42),
    "ffn_kernel": (5.5, 16),
    "ffn_back_kernel": (4.5, 14),
    "d_act_kernel": (2.5, 12),
    "fc2_grad_kernel": (4.6, 14),
    "fc1_grad_kernel": (5.5, 14),
    "attend_back_kernel": (4.4, 14),
    "hidden1_grad_kernel": (4.2, 12),
    "join_kernel": (1.0, 12),
    "qkv_grad_kernel": (3.2, 12),
    "result_kernel": (40.0, 10),
    "tokens_grad_kernel": (2.0, 10),
}


def run(kernel, place, grid, in_specs, out_specs, out_shapes, scratch, operands, flops, after=(), us=None, reuse=()):
    held = len(operands)
    inner = kernel
    cost, vmem = SIZES.get(getattr(kernel, "func", kernel).__name__, (0.01, 10))
    us = us or cost

    def kernel(place_ref, *refs):
        inner(place_ref, *refs[:held], *refs[held + len(after) :])

    in_specs = [*in_specs, *[pl.BlockSpec(memory_space=pl.ANY)] * len(after)]
    return pl.pallas_call(
        kernel,
        grid_spec=pltpu.PrefetchScalarGridSpec(
            num_scalar_prefetch=1,
            grid=grid,
            in_specs=in_specs,
            out_specs=out_specs,
            scratch_shapes=scratch,
        ),
        out_shape=out_shapes,
        input_output_aliases={1 + held + i: o for i, o in reuse},
        compiler_params=pltpu.CompilerParams(vmem_limit_bytes=vmem * MEGA),
        cost_estimate=pl.CostEstimate(flops=int(us * RATE), bytes_accessed=1, transcendentals=0),
    )(place, *operands, *after)


def add_kernel(place, *refs):
    refs[-1][...] = sum(ref[...].astype(F32) for ref in refs[:-1]).astype(BF)


def half_sum(place, terms, side, after=(), column=0, columns=None):
    size = terms[-1].shape[0] // 2
    _, height, columns = (*terms[0].shape[:2], columns or terms[0].shape[2])
    block = (min(size, 4), height, columns)
    count = size // block[0]
    return run(
        add_kernel, place, (count,),
        [spec(block, lambda n, p: (n + side * count, 0, column))] * len(terms),
        [spec(block, lambda n, p: (n, 0, 0))], [shape((size, *block[1:]), BF)], [], tuple(terms), 0,
        after=after,
    )[0]


def half_out(place, terms, after=(), **how):
    return half_sum(place, terms, 1, after, **how)


def join_kernel(place, *refs):
    cut = refs[0].shape[1]
    for n, out in enumerate(refs[-2:]):
        six = [ref[...].astype(F32) for ref in refs[6 * n : 6 * n + 6]]
        out[:, :cut, :] = (six[0] + six[1] + six[2]).astype(BF)
        out[:, cut:, :] = (six[3] + six[4] + six[5]).astype(BF)


def joined_halves(place, terms, others, after=()):
    line, _, _, high, wide = terms[0].shape
    low = others[-1].shape[1]
    total = (line, high + low, wide)
    specs = []
    for side in (1, 0):
        cube = spec((line, None, None, high, wide), lambda n, p, side=side: (0, 0, side, 0, 0))
        specs += [cube, cube, spec((line, high, wide), lambda n, p, side=side: (side, 0, 0))]
        under = spec((line, low, wide), lambda n, p, side=side: (side, 0, 4))
        specs += [under, under, spec((line, low, wide), lambda n, p, side=side: (side, 0, 0))]
    return run(
        join_kernel, place, (1,), specs, [full(total)] * 2, [shape(total, BF)] * 2, [],
        (*terms, *others) * 2, 0, after=after,
    )


def x_part(place, terms, side, after=()):
    line, _, seqs, *block = terms[0].shape
    return run(
        add_kernel, place, (line,),
        [spec((None, None, seqs, *block), lambda n, p: (n, side, 0, 0, 0))] * len(terms),
        [spec((seqs, None, *block), lambda n, p: (0, n, 0, 0))], [shape((seqs, line, *block), BF)], [],
        tuple(terms), 0, after=after,
    )[0].reshape(line * seqs, *block)


NOTE = (32, 1024)


def note_sum(left, right):
    return (left.astype(F32) + right.astype(F32)).astype(BF)


def qs_first_kernel(place, keep, recv, note, mate, send_out, rest_out):
    count, height, _ = keep.shape
    half = count // 2
    total = note_sum(note[...], mate[...])
    for out, base in ((send_out, half), (rest_out, 0)):
        for n in range(half):
            out[height * n : height * (n + 1), :] = note_sum(keep[base + n], recv[base + n])
        out[height * half :, :] = jnp.zeros((NOTE[0], out.shape[1]), BF)
        out[height * half :, : NOTE[1]] = total


def qs_next_kernel(place, keep, recv, send_out, rest_out):
    part = send_out.shape[0] - NOTE[0]
    total = note_sum(keep[...], recv[...])
    for out, base in ((send_out, part), (rest_out, 0)):
        out[:part, :] = total[base : base + part, :]
        out[part:, :] = total[2 * part :, :]


def qs_last_kernel(place, keep, recv, keep_out, line_out, side_out, cross_out, note_out, total):
    share = side_out.shape[1]
    height = side_out.shape[0]
    stay = pl.ds(pl.multiple_of(place[0] * share, LANES), 2 * share)
    leave = pl.ds(pl.multiple_of((1 - place[0]) * 2 * share, LANES), share)
    total[...] = keep[...].astype(F32) + recv[...].astype(F32)
    keep_out[...] = total[:height, stay]
    side_out[...] = total[:height, leave].astype(BF)
    cross_out[...] = total[height : 2 * height, leave].astype(BF)
    note = total[2 * height :, : NOTE[1]].astype(BF)
    note_out[...] = note
    line_out[...] = jnp.zeros_like(line_out)
    line_out[:height, : 2 * share] = total[height : 2 * height, stay].astype(BF)
    line_out[height:, :] = note


def note_kernel(place, note, line, note_out):
    note_out[...] = note_sum(note[...], line[line.shape[0] - NOTE[0] :, :])


def qs_join_kernel(place, keep, line, side, cross, out):
    height, share = side.shape
    both = keep[...] + line[:height, : 2 * share].astype(F32)
    out[:, :share] = both[:, :share]
    out[:, share : 2 * share] = side[...].astype(F32) + cross[...].astype(F32)
    out[:, 2 * share :] = both[:, share:]


def shape(dims, dtype):
    return jax.ShapeDtypeStruct(dims, dtype)


def qkv_kernel(place, source, vecs, weight, qb, vb, qkv_out, hidden_out):
    step = pl.program_id(0)

    @pl.when(step == 0)
    def _():
        normed, _ = layer_norm(source[...].astype(F32))
        hidden_out[...] = (normed * vecs[0:1, :] + vecs[1:2, :]).astype(BF)

    wide = mul(hidden_out[...], weight[...])
    shift = jnp.where(step == 0, qb[...], jnp.where(step == 2, vb[...], 0.0))
    factor = jnp.where(step == 0, 0.125, 1.0)
    qkv_out[0] = ((wide + shift) * factor).astype(BF)


def window(strip, block):
    off = (STRIP - block) * STRIP
    base = off // LANES * LANES
    held = strip[:, base : base + 6 * LANES]
    if off - base:
        held = pltpu.roll(held, 6 * LANES - (off - base), axis=1)
    return held[:, : 5 * LANES]


FORWARD_CHUNKS = ((0, 288), (288, 288), (576, 64))
CHUNKS = tuple((start * 144, 144) for start in range(4)) + ((576, 64),)


def attend_kernel(place, qkv, strips, even_mask, own_out, send_out, expo_out, inv_out, strip, attended):
    slots = qkv.shape[1]
    half = slots // 2
    side = place[0]
    lane = lax.broadcasted_iota(jnp.int32, (1, LANES), 1)
    first = lane < LANES // 2
    masks = (jnp.where(first, 1.0, 0.0).astype(BF), jnp.where(first, 0.0, 1.0).astype(BF))
    keys = [qkv[1] * m for m in masks]
    values = [qkv[2] * m for m in masks]
    picks = even_mask[...] > 0.5
    at = side * 6 + 2 * pl.program_id(0)
    for head in range(2):
        rolled = [
            pltpu.roll(
                jnp.broadcast_to(strips[at + head, par : par + 1, :], (STRIP, STRIP_WIDTH)),
                1,
                axis=1,
                stride=1,
                stride_axis=0,
            )
            for par in range(2)
        ]
        strip[head] = jnp.where(picks, rolled[0], rolled[1])
    block_lane = lax.broadcasted_iota(jnp.int32, (STRIP, LANES), 1)
    block_row = lax.broadcasted_iota(jnp.int32, (STRIP, LANES), 0)
    for start, count in FORWARD_CHUNKS:
        query = qkv[0, start : start + count, :]
        total = None
        scale = None
        for head in range(2):
            lone = strips[at + head, 0:1, 1152:1280]
            far = lone[:, 0:1]
            near = lone[:, 1:2]
            corner = lone[:, 2:3]
            biases = []
            for block in range(start // STRIP, min(start + count, 576) // STRIP):
                piece = window(strip.at[head], block)
                left = jnp.where(block_lane == 0, near, piece[:, :LANES])
                middle = piece[:, LANES : 4 * LANES]
                right = piece[:, 4 * LANES :]
                if block == 0:
                    top_row = block_row == 0
                    left = jnp.where(top_row, jnp.where(block_lane == 0, corner, far), left)
                    middle = jnp.concatenate(
                        [
                            jnp.where(top_row, far, middle[:, n * LANES : (n + 1) * LANES])
                            for n in range(3)
                        ],
                        axis=1,
                    )
                    right = jnp.where(top_row, far, right)
                right = jnp.where(block_lane > 64, NEGATIVE, right)
                biases.append(jnp.concatenate([left, middle, right], axis=1))
            if start + count > 576:
                row = window(strip.at[head, 0:8, :], STRIP)[0:1, :]
                row = jnp.concatenate(
                    [
                        jnp.where(lane == 0, near, row[:, :LANES]),
                        row[:, LANES : 4 * LANES],
                        jnp.where(lane > 64, NEGATIVE, row[:, 4 * LANES :]),
                    ],
                    axis=1,
                )
                biases.append(jnp.broadcast_to(row, (start + count - 576, 5 * LANES)))
            scores = mul(query, keys[head], NT) + jnp.concatenate(biases, axis=0)
            top = jnp.max(scores, axis=1, keepdims=True)
            expo = jnp.exp(scores - top)
            inverse = 1.0 / jnp.sum(expo, axis=1, keepdims=True)
            low = expo.astype(BF)
            expo_out[head, start : start + count, :] = low
            part = mul(low, values[head]) * inverse
            total = part if head == 0 else total + part
            spread = jnp.broadcast_to(inverse, (count, LANES))
            scale = spread if head == 0 else jnp.where(first, scale, spread)
        attended[start : start + count, :] = total
        inv_out[start : start + count, :] = scale
    own_out[...] = attended[pl.ds(pl.multiple_of(side * half, 64), half), :].astype(BF)
    send_out[...] = attended[pl.ds(pl.multiple_of((1 - side) * half, 64), half), :].astype(BF)


def attend_back_kernel(
    place, qkv, expo, attn_own, attn_send, grad_own, grad_other, inv, even_mask,
    dqkv_out, strip_out, grad_all, attn_all, d_scores, strip, dq_all,
):
    slots = qkv.shape[1]
    half = slots // 2
    here = pl.ds(pl.multiple_of(place[0] * half, 64), half)
    there = pl.ds(pl.multiple_of((1 - place[0]) * half, 64), half)
    lane = lax.broadcasted_iota(jnp.int32, (1, LANES), 1)
    first = lane < LANES // 2
    masks = (jnp.where(first, 1.0, 0.0).astype(BF), jnp.where(first, 0.0, 1.0).astype(BF))
    scaled = grad_own[...].astype(F32) * inv[here, :]
    grad_all[here, :] = scaled
    attn_all[here, :] = scaled * attn_own[...].astype(F32)
    scaled = grad_other[...].astype(F32) * inv[there, :]
    grad_all[there, :] = scaled
    attn_all[there, :] = scaled * attn_send[...].astype(F32)
    keys = [qkv[1] * m for m in masks]
    values = [qkv[2] * m for m in masks]
    block_lane = lax.broadcasted_iota(jnp.int32, (STRIP, LANES), 1)
    block_row = lax.broadcasted_iota(jnp.int32, (STRIP, LANES), 0)
    strip[...] = jnp.zeros_like(strip)
    columns = [jnp.zeros((8, LANES), F32) for _ in range(2)]
    tops = [None, None]
    zeros = jnp.zeros((STRIP, LANES), F32)
    for start, count in CHUNKS:
        grads = grad_all[start : start + count, :].astype(BF)
        products = attn_all[start : start + count, :]
        total = None
        for head in range(2):
            chosen = first if head == 0 else jnp.logical_not(first)
            delta = jnp.sum(jnp.where(chosen, products, 0.0), axis=1, keepdims=True)
            d_probs = mul(grads, values[head], NT)
            d_score = expo[head, start : start + count, :].astype(F32) * (d_probs - delta)
            low = d_score.astype(BF)
            d_scores[head, start : start + count, :] = low
            part = mul(low, keys[head])
            total = part if head == 0 else total + part
            if start == 576:
                for tile in range(count // 8):
                    columns[head] = columns[head] + d_score[8 * tile : 8 * tile + 8, :LANES]
                line = jnp.sum(d_score, axis=0, keepdims=True)
                line = jnp.concatenate([jnp.where(lane == 0, 0.0, line[:, :LANES]), line[:, LANES:]], axis=1)
                strip[head, 0:1, : 5 * LANES] = strip[head, 0:1, : 5 * LANES] + line
            else:
                for block in range(start // STRIP, (start + count) // STRIP):
                    at = block * STRIP - start
                    piece = d_score[at : at + STRIP, :]
                    left = piece[:, :LANES]
                    rest = piece[:, LANES:]
                    if block == 0:
                        tops[head] = piece[0:1, :]
                        left = jnp.where(block_row == 0, 0.0, left)
                        rest = jnp.concatenate(
                            [
                                jnp.where(block_row == 0, 0.0, rest[:, n * LANES : (n + 1) * LANES])
                                for n in range(4)
                            ],
                            axis=1,
                        )
                    columns[head] = columns[head] + left[0:8] + left[8:16] + left[16:24]
                    piece = jnp.concatenate(
                        [jnp.where(block_lane == 0, 0.0, left), rest, zeros], axis=1
                    )
                    off = (STRIP - block) * STRIP
                    base = off // LANES * LANES
                    if off - base:
                        piece = pltpu.roll(piece, off - base, axis=1)
                    strip[head, :, base : base + 6 * LANES] = (
                        strip[head, :, base : base + 6 * LANES] + piece
                    )
        dq_all[start : start + count, :] = total
    dqkv_out[0] = dq_all[...].astype(BF) * BF(0.125)
    turned_query = qkv[0].astype(F32).T.astype(BF)
    turned_grads = grad_all[...].T.astype(BF)
    half_lanes = LANES // 2
    for at, left, right in ((1, turned_query, d_scores), (2, turned_grads, expo)):
        sides = [
            mul(left[half_lanes * head : half_lanes * (head + 1), :], right[head])
            for head in range(2)
        ]
        dqkv_out[at] = jnp.concatenate(sides, axis=0).T.astype(BF)
    picks = even_mask[...] > 0.5
    row_id = lax.broadcasted_iota(jnp.int32, (STRIP, STRIP_WIDTH), 0)
    wide_lane = lax.broadcasted_iota(jnp.int32, (1, STRIP_WIDTH), 1)
    for head in range(2):
        held = strip[head]
        lines = []
        for par in range(2):
            part = jnp.where(picks, held, 0.0) if par == 0 else jnp.where(picks, 0.0, held)
            part = pltpu.roll(part, STRIP_WIDTH - 1, axis=1)
            for bit in (1, 2, 4, 8, 16):
                part = jnp.where(
                    (row_id & bit) > 0, pltpu.roll(part, STRIP_WIDTH - bit, axis=1), part
                )
            lines.append(jnp.sum(part, axis=0, keepdims=True))
        near = jnp.sum(jnp.where(lane == 0, columns[head], 0.0)).reshape(1, 1)
        corner = tops[head][:, 0:1]
        far = jnp.sum(tops[head], axis=1, keepdims=True) - corner
        line = lines[0]
        line = jnp.where(wide_lane >= 1152, 0.0, line)
        line = jnp.where(wide_lane == 1152, far, line)
        line = jnp.where(wide_lane == 1153, near, line)
        line = jnp.where(wide_lane == 1154, corner, line)
        strip_out[0, head, 0:1, :] = line
        strip_out[0, head, 1:2, :] = lines[1]


def d_act_kernel(place, cot, vecs, fc2, d_ffn_out, d_act_out):
    @pl.when(pl.program_id(0) == 0)
    def _():
        d_ffn_out[...] = (vecs[7:8, :] * cot[...].astype(F32)).astype(BF)

    d_act_out[...] = mul(d_ffn_out[...], fc2[...], NT).astype(BF)


def ffn_kernel(
    place, tokens, attn_own, attn_other, vecs, proj, fc1, fc1_bias, d_act,
    act_out, d_pre_out, fc1_bias_out, hidden_out, resid_out, attn_out, mixed_out,
):
    width = attn_own.shape[1]

    @pl.when(pl.program_id(0) == 0)
    def _():
        attn_out[:, pl.ds(pl.multiple_of(place[0] * width, LANES), width)] = attn_own[...]
        attn_out[:, pl.ds(pl.multiple_of((1 - place[0]) * width, LANES), width)] = attn_other[...]
        mixed = mul(attn_out[...], proj[...]) + vecs[2:3, :]
        mixed_out[...] = mixed
        resid = tokens[...].astype(F32) + vecs[3:4, :] * mixed
        resid_out[...] = resid
        normed, _ = layer_norm(resid)
        hidden_out[...] = (normed * vecs[4:5, :] + vecs[5:6, :]).astype(BF)

    pre = mul(hidden_out[...], fc1[...]) + fc1_bias[...]
    gate = 0.5 * (1.0 + lax.erf(pre * ROOT_HALF))
    act_out[...] = (pre * gate).astype(BF)
    slope = gate + pre * jnp.exp(-0.5 * pre * pre) * GAUSS_NORM
    d_pre = (d_act[...].astype(F32) * slope).astype(BF)
    d_pre_out[...] = d_pre
    fc1_bias_out[...] = jnp.sum(d_pre.astype(F32), axis=0, keepdims=True)


def ffn_back_kernel(
    place, d_pre, fc1, cot, d_ffn, resid, mixed_in, vecs, proj_own, proj_other,
    d_mixed_out, d_resid_out, grad_own_out, grad_send_out, small_out, d_hidden,
):
    step = pl.program_id(0)
    part = mul(d_pre[...], fc1[...], NT)

    @pl.when(step == 0)
    def _():
        d_hidden[...] = part

    @pl.when(step > 0)
    def _():
        d_hidden[...] += part

    @pl.when(step == pl.num_programs(0) - 1)
    def _():
        grad = d_hidden[...]
        mixed = mixed_in[...]
        normed, inverse = layer_norm(resid[...])
        d_resid = cot[...].astype(F32) + layer_norm_back(grad, normed, inverse, vecs[4:5, :])
        d_resid_out[...] = d_resid
        d_mixed = (vecs[3:4, :] * d_resid).astype(BF)
        d_mixed_out[...] = d_mixed
        grad_send_out[...] = mul(d_mixed, proj_other[...], NT).astype(BF)
        grad_own_out[...] = mul(d_mixed, proj_own[...], NT).astype(BF)
        small_out[0:1, :] = jnp.sum(grad * normed, axis=0, keepdims=True)
        small_out[1:2, :] = jnp.sum(grad, axis=0, keepdims=True)
        small_out[2:3, :] = jnp.sum(d_resid * mixed, axis=0, keepdims=True)
        small_out[3:4, :] = jnp.sum(d_mixed.astype(F32), axis=0, keepdims=True)
        small_out[4:5, :] = jnp.sum(d_ffn[...].astype(F32), axis=0, keepdims=True)
        small_out[5:8, :] = jnp.zeros((3, small_out.shape[1]), F32)


def fc2_grad_kernel(place, act, d_ffn, keep_out, send_out, held):
    core = place[1]
    held[...] = mul(act[...], d_ffn[...], TN)
    for pair in range(2):
        for seq in range(2):
            at = (0, pair ^ place[6], seq ^ place[0])
            columns = slice(384 * seq, 384 * seq + 384)
            low = pl.multiple_of(384 * pair + 192 * core, 64)
            high = pl.multiple_of(384 * pair + 192 * (1 - core), 64)
            keep_out[at] = held[pl.ds(low, 192), columns].astype(BF)
            send_out[at] = held[pl.ds(high, 192), columns].astype(BF)


def fc1_grad_kernel(place, hidden, d_pre, attn, d_mixed, keep_out, send_out, held, *, rest):
    step = pl.program_id(0)
    core = place[1]
    held[...] = mul(hidden[...], d_pre[...], TN)
    seq = step // 2
    lanes = pl.ds(pl.multiple_of((step % 2) * 768, LANES), 768)
    for pair in range(8):
        at = rest(pair % 2, pair // 2, seq) ^ place[3]
        low = pl.multiple_of(96 * pair + 48 * core, 16)
        high = pl.multiple_of(96 * pair + 48 * (1 - core), 16)
        keep_out[at, :, lanes] = held[pl.ds(low, 48), :].astype(BF)
        send_out[at, :, lanes] = held[pl.ds(high, 48), :].astype(BF)

    @pl.when(step == pl.num_programs(0) - 1)
    def _():
        held[...] = mul(attn[...], d_mixed[...], TN)
        for pair in range(8):
            low = pl.multiple_of(96 * pair + 48 * core, 16)
            high = pl.multiple_of(96 * pair + 48 * (1 - core), 16)
            for side in range(2):
                at = rest_label(ORDER_A)(pair % 2, pair // 2, side) ^ place[2]
                columns = slice(384 * side, 384 * side + 384)
                keep_out[at, :, 1536:1920] = held[pl.ds(low, 48), columns].astype(BF)
                send_out[at, :, 1536:1920] = held[pl.ds(high, 48), columns].astype(BF)


def result_kernel(place, act, fc2, resid, cot, vecs, result_out, small_out, total):
    step = pl.program_id(0)

    @pl.when(step == 0)
    def _():
        total[...] = jnp.zeros_like(total)

    total[...] += mul(act[...], fc2[...])

    @pl.when(step == pl.num_programs(0) - 1)
    def _():
        ffn = total[...] + vecs[6:7, :]
        result_out[...] = (resid[...] + vecs[7:8, :] * ffn).astype(BF)
        small_out[0:1, :] = jnp.sum(cot[...].astype(F32) * ffn, axis=0, keepdims=True)
        small_out[1:8, :] = jnp.zeros((7, small_out.shape[1]), F32)


def hidden1_grad_kernel(
    place, first, others, weight, hidden, vecs, keep_out, send_out, small_out, total, joined
):
    step = pl.program_id(0)
    rows = keep_out.shape[0]
    here = pl.ds(pl.multiple_of(place[0] * rows, 64), rows)
    there = pl.ds(pl.multiple_of((1 - place[0]) * rows, 64), rows)
    joined[:, :LANES] = first[0]
    joined[:, LANES:] = others[0]
    grads = joined[...]
    part = mul(grads, weight[...], NT)
    line = jnp.sum(grads.astype(F32), axis=0, keepdims=True)

    @pl.when(step == 0)
    def _():
        total[...] = part
        small_out[...] = jnp.zeros_like(small_out)
        small_out[2:3, :384] = line

    @pl.when(step > 0)
    def _():
        total[...] += part

    @pl.when(step == 2)
    def _():
        small_out[2:3, 384:] = line
        keep_out[...] = total[here, :]
        send_out[...] = total[there, :].astype(BF)
        both = total[...]
        plain = jnp.sum(both, axis=0, keepdims=True)
        scaled = jnp.sum(both * hidden[...].astype(F32), axis=0, keepdims=True)
        small_out[0:1, :] = (scaled - vecs[1:2, :] * plain) / vecs[0:1, :]
        small_out[1:2, :] = plain


def qkv_grad_kernel(
    place, hidden, first, others, keep_out, send_out, held, joined, *, rest
):
    core = place[1]
    joined[:, :LANES] = first[0]
    joined[:, LANES:] = others[0]
    held[...] = mul(hidden[...], joined[...], TN)
    for pair in range(8):
        at = rest(pair % 2, pair // 2, 0) ^ place[4]
        low = pl.multiple_of(96 * pair + 48 * core, 16)
        high = pl.multiple_of(96 * pair + 48 * (1 - core), 16)
        keep_out[at] = held[pl.ds(low, 48), :].astype(BF)
        send_out[at] = held[pl.ds(high, 48), :].astype(BF)


def tokens_grad_kernel(place, keep, recv, own, d_resid, vecs, grad_out):
    grad = keep[...] + recv[...].astype(F32)
    normed, inverse = layer_norm(own[...].astype(F32))
    back = layer_norm_back(grad, normed, inverse, vecs[0:1, :])
    grad_out[...] = (d_resid[...] + back).astype(BF)


def rest_label(order):
    def rest(x_bit, line, seq):
        bits = {"x": x_bit, "z1": line & 1, "z2": line >> 1, "y": seq}
        total = 0
        for name in order[1:]:
            total = total * 2 + bits[name]
        return total

    return rest


ORDER_A = ("core", "x", "y", "z1", "z2")
ORDER_B = ("core", "z1", "x", "y", "z2")
ORDER_Q = ("core", "x", "z1", "z2")


SPAN = 2 * GRID - 1
CELLS = SPAN * SPAN


def flips():
    row = lax.broadcasted_iota(jnp.int32, (LANES, LANES), 0)
    lane = lax.broadcasted_iota(jnp.int32, (LANES, LANES), 1)
    return jnp.where(row + lane == LANES - 1, 1.0, 0.0)


def exact(left, right, dims):
    return lax.dot_general(
        left, right, dims, precision=lax.Precision.HIGHEST, preferred_element_type=F32
    )


def moved_window(source, start, target):
    base = start // LANES * LANES
    place = target % LANES
    held = source[:, base : base + 2 * LANES]
    turn = (place - (start - base)) % (2 * LANES)
    if turn:
        held = pltpu.roll(held, turn, axis=1)
    lane = lax.broadcasted_iota(jnp.int32, (1, 2 * LANES), 1)
    return jnp.where((lane >= place) & (lane < place + SPAN), held, 0.0)


def strips_kernel(place, table, strips_out, flat, sides):
    heads = table.shape[0]
    flat[...] = jnp.zeros_like(flat)
    flat[:heads, : CELLS + 3] = table[...]
    turned = pltpu.roll(flat[:, : 18 * LANES], 18 * LANES - CELLS, axis=1)
    tail = turned[:, :LANES]
    for n in range(18):
        block = 17 - n
        flat[:, LANES * n : LANES * (n + 1)] = exact(
            turned[:, LANES * block : LANES * (block + 1)], flips(), NN
        )
    sides[...] = jnp.zeros_like(sides)
    for b in range(SPAN):
        base = 24 * b // LANES * LANES
        part = moved_window(flat, SPAN * b, 24 * b)
        sides[b % 2, :, base : base + 2 * LANES] += part
    lane = lax.broadcasted_iota(jnp.int32, (16, LANES), 1)
    sides[0, :, 1152:1280] = jnp.where(lane < 3, tail, 0.0)
    for head in range(heads):
        for par in range(2):
            strips_out[head, par : par + 1, :] = sides[par, head : head + 1, :]


def pack_kernel(place, first, others, ffn, fc1_bias, last, result, packed_out, packed):
    packed[...] = jnp.zeros_like(packed)
    for n in range(5):
        lanes = slice(256 * n, 256 * n + 256)
        for pair in range(3):
            strip, at = (first, 0) if pair == 0 else (others, pair - 1)
            for head in range(2):
                for par in range(2):
                    row = 16 * n + 6 * par + 2 * pair + head
                    packed[row : row + 1, :] = strip[at, head, par : par + 1, lanes]
    for n in range(3):
        lanes = slice(256 * n, 256 * n + 256)
        row = 80 + 16 * n
        packed[row : row + 5, :] = ffn[0:5, lanes]
        packed[row + 5 : row + 6, :] = result[0:1, lanes]
        packed[row + 6 : row + 9, :] = last[0:3, lanes]
        for part in range(4):
            packed[row + 9 + part : row + 10 + part, :] = fc1_bias[
                :, 768 * part + 256 * n : 768 * part + 256 * n + 256
            ]
    for n in range(8):
        packed_out[16 * (n // 4) : 16 * (n // 4) + 16, 256 * (n % 4) : 256 * (n % 4) + 256] = packed[
            16 * n : 16 * n + 16, :
        ].astype(BF)


def unpack_kernel(
    place, packed_in, mate_in, table_out, norm2_gain, norm2_bias, scale1, proj_bias, fc2_bias, scale2,
    norm1_gain, norm1_bias, query_bias, value_bias, fc1_bias, flat, sides, packed, mate,
):
    for held, source in ((packed, packed_in), (mate, mate_in)):
        for n in range(8):
            held[16 * n : 16 * n + 16, :] = source[
                16 * (n // 4) : 16 * (n // 4) + 16, 256 * (n % 4) : 256 * (n % 4) + 256
            ].astype(F32)
    heads = table_out.shape[0]
    half = heads // 2
    left = place[0] == 0
    flat[...] = jnp.zeros_like(flat)
    for n in range(5):
        lanes = slice(256 * n, 256 * n + 256)
        for par in range(2):
            rows = slice(16 * n + half * par, 16 * n + half * par + half)
            mine = packed[rows, :]
            theirs = mate[rows, :]
            sides[par, 0:half, lanes] = jnp.where(left, mine, theirs)
            sides[par, half:heads, lanes] = jnp.where(left, theirs, mine)
    for b in range(SPAN):
        target = SPAN * b
        base = target // LANES * LANES
        part = moved_window(sides.at[b % 2], 24 * b, target)
        flat[:, base : base + 2 * LANES] += part
    lane = lax.broadcasted_iota(jnp.int32, (16, LANES), 1)
    turn = flips().astype(BF)
    blocks = [
        mul(flat[:, LANES * (17 - n) : LANES * (18 - n)].astype(BF), turn) for n in range(18)
    ]
    blocks[0] = jnp.where(lane < 3, sides[0, :, 1152:1280], blocks[0])
    turned = pltpu.roll(jnp.concatenate(blocks, axis=1), CELLS, axis=1)
    table_out[...] = turned[:heads, : CELLS + 3]
    outs = (norm2_gain, norm2_bias, scale1, proj_bias, fc2_bias, scale2, norm1_gain, norm1_bias)
    for n in range(3):
        lanes = slice(256 * n, 256 * n + 256)
        for at, out in enumerate(outs):
            row = 80 + 16 * n + at
            out[lanes] = (packed[row : row + 1, :] + mate[row : row + 1, :]).reshape(256)
        for part in range(4):
            row = 89 + 16 * n + part
            fc1_bias[768 * part + 256 * n : 768 * part + 256 * n + 256] = (
                packed[row : row + 1, :] + mate[row : row + 1, :]
            ).reshape(256)
    for source, side in ((packed, place[0]), (mate, 1 - place[0])):
        line = jnp.concatenate([source[88 + 16 * n : 89 + 16 * n, :] for n in range(3)], axis=1)
        lanes = pl.ds(pl.multiple_of(side * 384, LANES), 384)
        query_bias[lanes] = line[:, :384].reshape(384)
        value_bias[lanes] = line[:, 384:].reshape(384)


def even_places():
    lane = np.arange(STRIP_WIDTH)[None, :]
    row = np.arange(STRIP)[:, None]
    turn = (lane - 1) // STRIP
    return np.where(row == 0, turn % 2 == 0, turn % 2 == 1).astype(np.float32)


def split_body(
    tokens,
    masked,
    out_grad,
    norm1_gain,
    norm1_bias,
    qkv_weight,
    query_bias,
    value_bias,
    rel_table,
    proj_weight,
    proj_bias,
    scale1,
    norm2_gain,
    norm2_bias,
    fc1_weight,
    fc1_bias,
    fc2_weight,
    fc2_bias,
    scale2,
):
    _, rows, width = tokens.shape
    slots = 2 * rows
    heads = rel_table.shape[1] // 2
    pairs = heads // 2
    share = width // 2
    hidden = fc1_weight.shape[1]
    seq = lax.axis_index("seq")
    img = lax.axis_index("img")
    core = img & 1
    line = img >> 2
    x_bit = (img >> 1) & 1
    place = jnp.stack(
        [
            seq,
            core,
            rest_label(ORDER_A)(x_bit, line, seq),
            rest_label(ORDER_B)(x_bit, line, seq),
            rest_label(ORDER_Q)(x_bit, line, seq),
            line,
            x_bit,
        ]
    ).astype(jnp.int32)
    own = tokens.reshape(rows, width)
    other = swapped(own, "y")
    cot = (out_grad.astype(F32) * masked.astype(F32)[..., None]).astype(BF).reshape(rows, width)
    vecs = jnp.stack(
        [norm1_gain, norm1_bias, proj_bias, scale1, norm2_gain, norm2_bias, fc2_bias, scale2]
    )
    strips = run(
        strips_kernel, place, (1,), [full(rel_table.shape[::-1])], [full((2 * heads, 2, STRIP_WIDTH))],
        [shape((2 * heads, 2, STRIP_WIDTH), F32)],
        [pltpu.VMEM((16, 2432), F32), pltpu.VMEM((2, 16, STRIP_WIDTH), F32)], (rel_table.T,), 0,
    )[0]
    even_mask = jnp.asarray(even_places())

    def qkv_rows(source, mine, held):
        def side(p):
            return p[0] if mine else 1 - p[0]

        return run(
            qkv_kernel, place, (3,),
            [
                full((rows, width)), full((8, width)),
                spec((width, share), lambda t, p: (0, 2 * t + p[0])),
                spec((1, share), lambda t, p: (0, p[0])), spec((1, share), lambda t, p: (0, p[0])),
            ],
            [
                spec((1, rows, share), lambda t, p: (t, side(p), 0)),
                spec((rows, width), lambda t, p: (side(p), 0)),
            ],
            [shape((3, slots, share), BF), shape((slots, width), BF)],
            [],
            (source, vecs, qkv_weight, query_bias.reshape(1, width), value_bias.reshape(1, width)),
            0, after=held, reuse=() if mine else ((0, 0), (1, 1)),
        )

    qkv, hidden1 = qkv_rows(other, False, qkv_rows(own, True, ()))
    pair_rows = spec((slots, LANES), lambda n, p: (0, n))
    pair_half = spec((rows, LANES), lambda n, p: (0, n))
    pair_qkv = spec((3, slots, LANES), lambda n, p: (0, 0, n))
    pair_expo = spec((2, slots, slots), lambda n, p: (n, 0, 0))
    attn_own, attn_send, expo, inv = run(
        attend_kernel, place, (pairs,),
        [pair_qkv, full((2 * heads, 2, STRIP_WIDTH)), full((STRIP, STRIP_WIDTH))],
        [pair_half, pair_half, pair_expo, pair_rows],
        [
            shape((rows, share), BF), shape((rows, share), BF),
            shape((heads, slots, slots), BF), shape((slots, share), F32),
        ],
        [pltpu.VMEM((2, STRIP, STRIP_WIDTH), F32), pltpu.VMEM((slots, LANES), F32)],
        (qkv, strips, even_mask),
        16 * slots * slots * 64 * heads,
    )
    attn_other = swapped(attn_send, "y")
    parts = 4
    part = hidden // parts
    whole = full((rows, width))
    sliced = spec((rows, part), lambda c, p: (0, c))
    d_ffn, d_act = run(
        d_act_kernel, place, (parts,),
        [whole, full((8, width)), spec((part, width), lambda c, p: (c, 0))],
        [whole, sliced], [shape((rows, width), BF), shape((rows, hidden), BF)], [],
        (cot, vecs, fc2_weight), 0, after=(attn_send,),
    )
    act, d_pre, fc1_bias_part, hidden2, resid, attn_low, mixed = run(
        ffn_kernel, place, (parts,),
        [
            whole, full((rows, share)), full((rows, share)), full((8, width)),
            full((width, width)), spec((width, part), lambda c, p: (0, c)),
            spec((1, part), lambda c, p: (0, c)), sliced,
        ],
        [sliced, sliced, spec((1, part), lambda c, p: (0, c)), whole, whole, whole, whole],
        [
            shape((rows, hidden), BF), shape((rows, hidden), BF), shape((1, hidden), F32),
            shape((rows, width), BF), shape((rows, width), F32), shape((rows, width), BF),
            shape((rows, width), F32),
        ],
        [],
        (own, attn_own, attn_other, vecs, proj_weight, fc1_weight, fc1_bias.reshape(1, hidden), d_act),
        0,
    )
    cube = (4, 2, 2, 192, share)

    def line_place(c, p):
        far = c ^ p[5]
        return (far & 1) * 2 + (far >> 1), 0, 0, 0, 0

    block = spec((1, *cube[1:]), line_place)
    keep_a, send_a = run(
        fc2_grad_kernel, place, (parts,), [sliced, whole], [block, block],
        [shape(cube, BF), shape(cube, BF)], [pltpu.VMEM((part, width), F32)], (act, d_ffn), 0,
    )
    terms_a = [keep_a, swapped(send_a, "core")]
    d_mixed, d_resid, grad_own, grad_send, small_ffn = run(
        ffn_back_kernel, place, (parts,),
        [
            sliced, spec((width, part), lambda c, p: (0, c)), whole, whole, whole, whole, full((8, width)),
            spec((share, width), lambda c, p: (p[0], 0)), spec((share, width), lambda c, p: (1 - p[0], 0)),
        ],
        [whole, whole, full((rows, share)), full((rows, share)), full((8, width))],
        [
            shape((rows, width), BF), shape((rows, width), F32), shape((rows, share), BF),
            shape((rows, share), BF), shape((8, width), F32),
        ],
        [pltpu.VMEM((rows, width), F32)],
        (d_pre, fc1_weight, cot, d_ffn, resid, mixed, vecs, proj_weight, proj_weight), 0, after=(send_a,),
    )
    grad_other = swapped(grad_send, "y")
    out_a1 = x_part(place, terms_a, 1, (grad_send,))
    terms_a = [*terms_a, swapped(out_a1, ORDER_A[1])]
    block = (16, 48, 5 * share)
    keep_b, send_b = run(
        functools.partial(fc1_grad_kernel, rest=rest_label(ORDER_B)), place, (parts,),
        [whole, sliced, whole, whole], [full(block), full(block)],
        [shape(block, BF), shape(block, BF)],
        [pltpu.VMEM((width, part), F32)], (hidden2, d_pre, attn_low, d_mixed), 0, after=(out_a1,),
    )
    terms_b = [keep_b, swapped(send_b, "core")]

    def attend_back(pair, count, after):
        half_rows = spec((rows, LANES), lambda n, p: (0, pair + n))
        return run(
            attend_back_kernel, place, (count,),
            [
                spec((3, slots, LANES), lambda n, p: (0, 0, pair + n)),
                spec((2, slots, slots), lambda n, p: (pair + n, 0, 0)),
                half_rows, half_rows, half_rows, half_rows,
                spec((slots, LANES), lambda n, p: (0, pair + n)), full((STRIP, STRIP_WIDTH)),
            ],
            [
                spec((3, slots, LANES), lambda n, p: (0, 0, n)),
                spec((1, 2, 2, STRIP_WIDTH), lambda n, p: (n, 0, 0, 0)),
            ],
            [shape((3, slots, count * LANES), BF), shape((count, 2, 2, STRIP_WIDTH), F32)],
            [
                pltpu.VMEM((slots, LANES), F32), pltpu.VMEM((slots, LANES), F32),
                pltpu.VMEM((2, slots, slots), BF), pltpu.VMEM((2, STRIP, STRIP_WIDTH), F32),
                pltpu.VMEM((slots, LANES), F32),
            ],
            (qkv, expo, attn_own, attn_send, grad_own, grad_other, inv, even_mask), 0, after=after,
            us=40.0 if pair == 0 else 8.0,
        )

    dqkv0, strip0 = attend_back(0, 1, (send_b,))
    out_p1 = half_out(place, terms_b, (dqkv0,), column=4, columns=share)
    terms_p = [*terms_b, swapped(out_p1, ORDER_A[1])]
    out_b1 = half_out(place, terms_b, (out_p1,), columns=4 * share)
    terms_b = [*terms_b, swapped(out_b1, ORDER_B[1])]
    dqkv1, strip1 = attend_back(1, pairs - 1, (dqkv0, out_b1))
    dqkv = (dqkv0, dqkv1)
    third = [
        spec((1, slots, LANES), lambda t, p: (t, 0, 0)),
        spec((1, slots, share - LANES), lambda t, p: (t, 0, 0)),
    ]
    dh_keep, dh_send, small_last = run(
        hidden1_grad_kernel, place, (3,),
        [*third, spec((width, share), lambda t, p: (0, 2 * t + p[0])), full((slots, width)), full((8, width))],
        [whole, whole, full((8, width))],
        [shape((rows, width), F32), shape((rows, width), BF), shape((8, width), F32)],
        [pltpu.VMEM((slots, width), F32), pltpu.VMEM((slots, share), BF)], (*dqkv, qkv_weight, hidden1, vecs),
        2 * slots * width * 3 * share,
    )
    block = (8, 48, 3 * share)
    keep_q, send_q = run(
        functools.partial(qkv_grad_kernel, rest=rest_label(ORDER_Q)), place, (3,),
        [full((slots, width)), *third], [spec((8, 48, share), lambda t, p: (0, 0, t))] * 2,
        [shape(block, BF), shape(block, BF)],
        [pltpu.VMEM((width, share), F32), pltpu.VMEM((slots, share), BF)], (hidden1, *dqkv), 2 * slots * width * 3 * share,
        after=(dh_send,),
    )
    recv_q = swapped(send_q, "core")
    out_a2, rest_a = joined_halves(place, terms_a, terms_p, (send_q,))
    terms_a = [rest_a, swapped(out_a2, "y")]
    result, small_result = run(
        result_kernel, place, (parts,),
        [sliced, spec((part, width), lambda c, p: (c, 0)), whole, whole, full((8, width))],
        [whole, full((8, width))],
        [shape((rows, width), BF), shape((8, width), F32)],
        [pltpu.VMEM((rows, width), F32)], (act, fc2_weight, resid, cot, vecs),
        2 * rows * width * hidden, after=(out_a2, rest_a),
    )
    packed = run(
        pack_kernel, place, (1,),
        [full((1, 2, 2, STRIP_WIDTH)), full((2, 2, 2, STRIP_WIDTH)), full((8, width)), full((1, hidden)), full((8, width)), full((8, width))],
        [full(NOTE)], [shape(NOTE, BF)], [pltpu.VMEM((128, 256), F32)],
        (strip0, strip1, small_ffn, fc1_bias_part, small_last, small_result), 0,
    )[0]
    mate = swapped(packed, "core")
    def wide(blocks, columns):
        return (48 * blocks + NOTE[0], columns)

    send, rest = run(
        qs_first_kernel, place, (1,),
        [full((8, 48, 3 * share))] * 2 + [full(NOTE)] * 2, [full(wide(4, 3 * share))] * 2,
        [shape(wide(4, 3 * share), BF)] * 2, [], (keep_q, recv_q, packed, mate), 0, after=(),
    )
    recv = swapped(send, "x")
    out_b2 = half_out(place, terms_b, (send,), columns=4 * share)
    terms_b = [*terms_b, swapped(out_b2, "x")]
    out_a3 = half_out(place, terms_a, (out_b2,))
    terms_a = [*terms_a, swapped(out_a3, "z1")]
    dh_late = run(
        add_kernel, place, (1,), [whole], [whole], [shape((rows, width), BF)], [], (dh_send,), 0,
        after=(out_a3,),
    )[0]
    dh_recv = swapped(dh_late, "y")
    send, rest = run(
        qs_next_kernel, place, (1,), [full(wide(4, 3 * share))] * 2, [full(wide(2, 3 * share))] * 2,
        [shape(wide(2, 3 * share), BF)] * 2, [], (rest, recv), 0, after=(dh_late,),
    )
    recv = swapped(send, "z1")
    out_a4 = half_out(place, terms_a, (send,))
    terms_a = [*terms_a, swapped(out_a4, "z2")]
    out_b3 = half_out(place, terms_b, (out_a4,), columns=4 * share)
    terms_b = [*terms_b, swapped(out_b3, "y")]
    q_keep, q_line, q_side, q_cross, note = run(
        qs_last_kernel, place, (1,), [full(wide(2, 3 * share))] * 2,
        [
            full((48, 2 * share)), full(wide(1, NOTE[1])), full((48, share)), full((48, share)), full(NOTE),
        ],
        [
            shape((48, 2 * share), F32), shape(wide(1, NOTE[1]), BF), shape((48, share), BF),
            shape((48, share), BF), shape(NOTE, BF),
        ],
        [pltpu.VMEM(wide(2, 3 * share), F32)], (rest, recv), 0, after=(out_b3,),
    )
    q_sends = (swapped(q_line, "z2"), swapped(q_side, "y"), swapped(q_cross, "z2", "y"))
    tokens_grad = run(
        tokens_grad_kernel, place, (1,),
        [whole, whole, whole, whole, full((8, width))], [whole],
        [shape((rows, width), BF)], [], (dh_keep, dh_recv, own, d_resid, vecs), 0,
        after=(q_line,),
    )[0]
    out_b4 = half_out(place, terms_b, (tokens_grad,), columns=4 * share)
    terms_b = [*terms_b, swapped(out_b4, "z2")]
    packed = run(
        note_kernel, place, (1,), [full(NOTE), full(wide(1, NOTE[1]))], [full(NOTE)],
        [shape(NOTE, BF)], [], (note, q_sends[0]), 0, after=(out_b4,),
    )[0]
    mate = swapped(packed, "y")
    qkv_grad = run(
        qs_join_kernel, place, (1,),
        [full((48, 2 * share)), full(wide(1, NOTE[1])), full((48, share)), full((48, share))],
        [full((48, 3 * share))], [shape((48, 3 * share), F32)], [], (q_keep, *q_sends), 0,
        after=(packed,),
    )[0]
    fc2_proj = added(terms_a)
    fc1_grad = added([term[:, :, : 4 * share] for term in terms_b])
    fc2_grad = fc2_proj[:192]
    proj_grad = fc2_proj[192:]
    vector = shape((width,), F32)
    table_grad, *small = run(
        unpack_kernel, place, (1,), [full(NOTE)] * 2,
        [full(rel_table.shape[::-1]), *[full((width,))] * 10, full((hidden,))],
        [shape(rel_table.shape[::-1], F32), *[vector] * 10, shape((hidden,), F32)],
        [
            pltpu.VMEM((16, 2432), F32), pltpu.VMEM((2, 16, STRIP_WIDTH), F32),
            pltpu.VMEM((128, 256), F32), pltpu.VMEM((128, 256), F32),
        ], (packed, mate), 0,
    )
    return (
        result.reshape(tokens.shape),
        tokens_grad.reshape(tokens.shape),
        small[6],
        small[7],
        qkv_grad,
        small[8],
        small[9],
        table_grad.T,
        proj_grad,
        small[3],
        small[2],
        small[0],
        small[1],
        fc1_grad,
        small[10],
        fc2_grad,
        small[4],
        small[5],
    )


def solution(mesh):
    in_specs = (
        P("img", "seq", None),
        P("img", "seq"),
        P("img", "seq", None),
        P(),
        P(),
        P(),
        P(),
        P(),
        P(),
        P(),
        P(),
        P(),
        P(),
        P(),
        P(),
        P(),
        P(),
        P(),
        P(),
    )
    out_specs = (
        P("img", "seq", None),
        P("img", "seq", None),
        P(),
        P(),
        P("img", "seq"),
        P(),
        P(),
        P(),
        P("img", "seq"),
        P(),
        P(),
        P(),
        P(),
        P("img", "seq"),
        P(),
        P("img", "seq"),
        P(),
        P(),
    )
    sizes = dict(mesh.shape)
    body = split_body if (sizes["img"], sizes["seq"]) == (16, 2) else general_body
    return jax.shard_map(body, mesh=mesh, in_specs=in_specs, out_specs=out_specs, check_vma=False)
```
